128 devices in a mesh: dp: 8 (over z, x_lo), ctx: 16 (over y, x_hi, core).
Axes of the slice: x: 4 (x_hi: 2, x_lo: 2; x = x_hi * 2 + x_lo), y: 4, z: 4, core: 2. Of those that a mesh axis runs over, the one named last changes fastest.
Arguments:
- hidden_in: bfloat16 [8, 2048, 512], P('dp', 'ctx'), may hold values from -6 to 6
- positions: int32 [8, 2048], P('dp', 'ctx'), may hold values from 0 to 127, as said below
- block_order: int32 [32], replicated, may hold values from 0 to 31, as said below
- norm1_gain: bfloat16 [512], P(('dp', 'ctx')), may hold values from 0.5 to 1.5
- norm1_bias: bfloat16 [512], P(('dp', 'ctx')), may hold values from -1 to 1
- norm2_gain: bfloat16 [512], P(('dp', 'ctx')), may hold values from 0.5 to 1.5
- norm2_bias: bfloat16 [512], P(('dp', 'ctx')), may hold values from -1 to 1
- qkv_weight: bfloat16 [512, 1536], P(('dp', 'ctx')), may hold values from -0.25 to 0.25
- qkv_bias: bfloat16 [1536], P(('dp', 'ctx')), may hold values from -1.5 to 1.5
- attn_out_weight: bfloat16 [512, 512], P(('dp', 'ctx')), may hold values from -1 to 1
- out_bias: bfloat16 [512], P(('dp', 'ctx')), may hold values from -1.5 to 1.5
- up_weight: bfloat16 [512, 2048], P(('dp', 'ctx')), may hold values from -0.25 to 0.25
- up_bias: bfloat16 [2048], P(('dp', 'ctx')), may hold values from -1.5 to 1.5
- down_weight: bfloat16 [2048, 512], P(('dp', 'ctx')), may hold values from -0.125 to 0.125
- out_grad: bfloat16 [8, 2048, 512], P('dp', 'ctx'), may hold values from -6 to 6
Outputs:
- block_out: bfloat16 [8, 2048, 512], P('dp', 'ctx')
- input_grad: float32 [8, 2048, 512], P('dp', 'ctx')
- norm1_gain_grad: float32 [512], P(('dp', 'ctx'))
- norm1_bias_grad: float32 [512], P(('dp', 'ctx'))
- norm2_gain_grad: float32 [512], P(('dp', 'ctx'))
- norm2_bias_grad: float32 [512], P(('dp', 'ctx'))
- qkv_weight_grad: float32 [512, 1536], P(('dp', 'ctx'))
- qk_bias_grad: float32 [1024], P(('dp', 'ctx'))
- value_bias_grad: float32 [512], P(('dp', 'ctx'))
- attn_out_weight_grad: float32 [512, 512], P(('dp', 'ctx'))
- out_bias_grad: float32 [512], P(('dp', 'ctx'))
- up_weight_grad: float32 [512, 2048], P(('dp', 'ctx'))
- up_bias_grad: float32 [2048], P(('dp', 'ctx'))
- down_weight_grad: float32 [2048, 512], P(('dp', 'ctx'))
The draws below stay inside these ranges and needn't reach their ends.
Inputs may be any that keep to these rules, and one draw needn't show every extreme that they name: `block_order`: slots 2c and 2c+1 hold blocks j and 31 - j for some j; every block appears once. `positions`: positions count up by one along a sequence's true order and restart at 0 at the start of each packed document; a document starts at every multiple of 128 true rows and possibly in between; the first document of each sequence has exactly 128 rows.
All inputs are finite; a program needn't handle non-finite values.
Results may differ from the reference program's by a relative error of at most 0.025.
Values may be sent and summed in bfloat16 or wider, within the bound.
A program may use at most 128 MiB of HBM per device.

```python
import jax
import jax.numpy as jnp
from jax import lax

D = 512
FF = 2048
HEADS = 8
HEAD_DIM = 64
ROT_DIM = 16
BLK = 64
SEQS = 8
SEQ = 2048
N_CTX = 16


def make_table(key):
    order = jax.random.permutation(jax.random.fold_in(key, 11), N_CTX).astype(jnp.int32)
    flips = jax.random.randint(jax.random.fold_in(key, 12), (N_CTX,), 0, 2)
    first = jnp.where(flips == 1, order, 2 * N_CTX - 1 - order)
    second = 2 * N_CTX - 1 - first
    return jnp.stack([first, second], axis=1).reshape(2 * N_CTX).astype(jnp.int32)


def draw_block_order(key, part):
    table = make_table(key)
    return table


def draw_positions(key, part):
    table = make_table(key)
    key = jax.random.fold_in(key, 5)
    length = 2 * BLK * N_CTX
    places = jnp.arange(length, dtype=jnp.int32)[None, :]
    random_starts = (jax.random.randint(key, (SEQS, length), 0, 2 * BLK) == 0) & (places >= 2 * BLK)
    starts = random_starts | (places % (2 * BLK) == 0)
    marks = jnp.where(starts, places, 0)
    begins = lax.cummax(marks, axis=1)
    true_pos = (places - begins).astype(jnp.int32)
    blocks = true_pos.reshape(SEQS, 2 * N_CTX, BLK)[:, table]
    return blocks.reshape(SEQS, length).astype(jnp.int32)


def block_scale(stream_key, extent, pieces, smallest, top_value):
    level, own = 1.0, jax.random.fold_in(stream_key, 6)
    for dim, parts in pieces:
        heights = jnp.exp(jax.random.uniform(jax.random.fold_in(own, dim), (parts,), jnp.float32, smallest / len(pieces), top_value / len(pieces)))
        level = level * jnp.repeat(heights, extent[dim] // parts).reshape([-1 if axis == dim else 1 for axis in range(len(extent))])
    return level


def bell_draw(own_key, dims, scale, reach, split=(), held_as=jnp.bfloat16):
    array = scale * jax.random.normal(own_key, dims, jnp.float32)
    if split:
        array = array * block_scale(own_key, dims, split, -0.22, 0.18)
    return jnp.clip(array, -reach, reach).astype(held_as)


def setup_inputs(seed: int = 0) -> dict:
    seeds = jax.random.split(jax.random.key(seed), 16)
    hidden_in = bell_draw(seeds[0], (SEQS, SEQ, D), 1.0, 6.0, ((0, 8), (1, 16)))
    positions = draw_positions(jax.random.fold_in(seeds[15], 71), 0)
    block_order = draw_block_order(jax.random.fold_in(seeds[15], 71), 0)
    norm1_gain = jnp.clip(1.0 + 0.1 * jax.random.normal(seeds[3], (D,), jnp.float32), 0.5, 1.5).astype(jnp.bfloat16)
    norm1_bias = bell_draw(seeds[4], (D,), 0.2, 1.0, ((0, 128),))
    norm2_gain = jnp.clip(1.0 + 0.1 * jax.random.normal(seeds[5], (D,), jnp.float32), 0.5, 1.5).astype(jnp.bfloat16)
    norm2_bias = bell_draw(seeds[6], (D,), 0.2, 1.0, ((0, 128),))
    qkv_weight = bell_draw(seeds[7], (D, 3 * D), D ** -0.5, 0.25, ((0, 128),))
    qkv_bias = bell_draw(seeds[8], (3 * D,), 0.3, 1.5, ((0, 128),))
    attn_out_weight = bell_draw(seeds[9], (D, D), (D // 16) ** -0.5, 1.0, ((0, 128),))
    out_bias = bell_draw(seeds[10], (D,), 0.3, 1.5, ((0, 128),))
    up_weight = bell_draw(seeds[11], (D, FF), D ** -0.5, 0.25, ((0, 128),))
    up_bias = bell_draw(seeds[12], (FF,), 0.3, 1.5, ((0, 128),))
    down_weight = bell_draw(seeds[13], (FF, D), FF ** -0.5, 0.125, ((0, 128),))
    out_grad = bell_draw(seeds[14], (SEQS, SEQ, D), 1.0, 6.0, ((0, 8), (1, 16)))
    return {"hidden_in": hidden_in, "positions": positions, "block_order": block_order, "norm1_gain": norm1_gain, "norm1_bias": norm1_bias, "norm2_gain": norm2_gain, "norm2_bias": norm2_bias, "qkv_weight": qkv_weight, "qkv_bias": qkv_bias, "attn_out_weight": attn_out_weight, "out_bias": out_bias, "up_weight": up_weight, "up_bias": up_bias, "down_weight": down_weight, "out_grad": out_grad}


EPS = 1e-05
NEG_BIG = -1e+30
HIGH = lax.Precision.HIGHEST

@jax.custom_vjp
def low(v):
    return lax.optimization_barrier(v.astype(jnp.bfloat16)).astype(jnp.float32)

@jax.custom_vjp
def low_back(v):
    return v

def low_keep(v):
    return (low(v), None)

def low_pass(kept, grad):
    return (grad,)

def back_keep(v):
    return (v, None)

def back_low(kept, grad):
    return (low(grad),)
low.defvjp(low_keep, low_pass)
low_back.defvjp(back_keep, back_low)

def layer_norm(values, gain, shift):
    center = values - lax.optimization_barrier(jnp.mean(values, axis=-1, keepdims=True))
    spread = lax.optimization_barrier(jnp.mean(center * center, axis=-1, keepdims=True))
    return center * lax.rsqrt(spread + EPS) * gain + shift

def rotary(tensor, places):
    half_rot = ROT_DIM // 2
    freqs = 10000.0 ** (-jnp.arange(half_rot, dtype=jnp.float32) * 2.0 / ROT_DIM)
    angle = places.astype(jnp.float32)[:, None] * freqs[None, :]
    angle = jnp.concatenate([angle, angle], axis=-1)[:, None, :]
    turned_part = tensor[..., :ROT_DIM]
    swapped = jnp.concatenate([-turned_part[..., half_rot:], turned_part[..., :half_rot]], axis=-1)
    return jnp.concatenate([turned_part * jnp.cos(angle) + swapped * jnp.sin(angle), tensor[..., ROT_DIM:]], axis=-1)

def one_sequence(values, places, table, params):
    gain_one, shift_one, gain_two, shift_two, w_qkv, b_qkv, w_out, b_out, w_up, b_up, w_down = params
    nrows = values.shape[0]
    slots = table.shape[0]
    width = values.shape[1]
    blk_rows = nrows // slots
    x_true = jnp.zeros((slots, blk_rows, width), values.dtype).at[table].set(values.reshape(slots, blk_rows, width)).reshape(nrows, width)
    pos_true = jnp.zeros((slots, blk_rows), places.dtype).at[table].set(places.reshape(slots, blk_rows)).reshape(nrows)
    normed_one = low(layer_norm(x_true, gain_one, shift_one))
    normed_two = low(layer_norm(x_true, gain_two, shift_two))
    qkv = low_back(jnp.dot(normed_one, w_qkv, precision=HIGH) + b_qkv).reshape(nrows, 3, HEADS, HEAD_DIM)
    queries = low(rotary(qkv[:, 0], pos_true))
    keys_all = low(rotary(qkv[:, 1], pos_true))
    vals_all = low(qkv[:, 2])
    qrows = min(512, nrows)
    qblocks = queries.reshape(nrows // qrows, qrows, HEADS, HEAD_DIM)
    starts = jnp.arange(nrows // qrows, dtype=jnp.int32) * qrows
    key_at = jnp.arange(nrows, dtype=jnp.int32)
    factor = HEAD_DIM ** (-0.5)

    def attend(pair):
        qpart, start = pair
        query_at = start + jnp.arange(qrows, dtype=jnp.int32)
        scores = jnp.einsum('qhd,khd->hqk', qpart, keys_all, precision=HIGH) * factor
        allowed = query_at[:, None] >= key_at[None, :]
        scores = low_back(jnp.where(allowed[None], scores, NEG_BIG))
        probs = low(jax.nn.softmax(scores, axis=-1))
        return jnp.einsum('hqk,khd->qhd', probs, vals_all, precision=HIGH)
    attended = lax.map(jax.checkpoint(attend), (qblocks, starts)).reshape(nrows, width)
    mixed_att = low(low_back(attended))
    upper = low_back(jnp.dot(normed_two, w_up, precision=HIGH) + b_up)
    gelu_out = low(jax.nn.gelu(upper, approximate=False))
    result = x_true + jnp.dot(mixed_att, w_out, precision=HIGH) + jnp.dot(gelu_out, w_down, precision=HIGH) + b_out
    return result.reshape(slots, blk_rows, width)[table].reshape(nrows, width)

def reference(hidden_in, positions, block_order, norm1_gain, norm1_bias, norm2_gain, norm2_bias, qkv_weight, qkv_bias, attn_out_weight, out_bias, up_weight, up_bias, down_weight, out_grad):
    params = tuple((item.astype(jnp.float32) for item in (norm1_gain, norm1_bias, norm2_gain, norm2_bias, qkv_weight, qkv_bias, attn_out_weight, out_bias, up_weight, up_bias, down_weight)))
    inputs = hidden_in.astype(jnp.float32)
    cotangent = out_grad.astype(jnp.float32)

    def forward(values, weights):
        return lax.map(lambda pair: one_sequence(pair[0], pair[1], block_order, weights), (values, positions))
    outputs, pull = jax.vjp(forward, inputs, params)
    input_grad, grads = pull(cotangent)
    bias_all = grads[5]
    return (outputs.astype(jnp.bfloat16), input_grad, grads[0], grads[1], grads[2], grads[3], grads[4], bias_all[:2 * D], bias_all[2 * D:], grads[6], grads[7], grads[8], grads[9], grads[10])
```

```python
import jax
import jax.numpy as jnp
from jax import lax
from jax.experimental import pallas as pl
from jax.experimental.pallas import tpu as pltpu
from jax.sharding import PartitionSpec as P

HEAD_DIM = 64
ROT_DIM = 16
EPS = 1e-05
MESH = pl.DeviceIdType.MESH
F32 = jnp.float32
BF16 = jnp.bfloat16
VMEM = pltpu.VMEM
LIMIT = 56 * 1024 * 1024

STREAMS = 7
TILES = [((16, 256), BF16)] * 6 + [((8, 128), F32)]


def coords(dp, ctx):
    z = lax.div(dp, 2)
    x = lax.rem(lax.div(ctx, 2), 2) * 2 + lax.rem(dp, 2)
    y = lax.div(ctx, 4)
    return z, x, y, lax.rem(ctx, 2)


def device_of(z, x, y, core):
    return (z * 2 + lax.rem(x, 2), y * 4 + lax.div(x, 2) * 2 + core)


def gray_bits(z, x, y):
    out = []
    for i in (x, y, z):
        hi = lax.div(i, 2)
        out += [lax.rem(hi + i, 2), hi]
    return out


def slot_of(p, bits):
    return sum(bits[(p + k) % 6] * 2**k for k in range(6))


def partner(j, z, x, y):
    def turn(i):
        return 3 - i if j % 2 else i + 1 - 2 * lax.rem(i, 2)

    if j < 2:
        return z, turn(x), y
    if j < 4:
        return z, x, turn(y)
    return turn(z), x, y


def quad_peer(delta, x, core):
    core_t = 1 - core if delta % 2 else core
    x_t = lax.rem(x + 2, 4) if delta // 2 else x
    return x_t, core_t, lax.div(x_t, 2) * 2 + core_t


def enter(peers):
    barrier = pltpu.get_barrier_semaphore()
    for peer in peers:
        pl.semaphore_signal(barrier, inc=1, device_id=peer, device_id_type=MESH)
    pl.semaphore_wait(barrier, len(peers))


def send(src, dst, ssem, rsem, peer):
    copy = pltpu.make_async_remote_copy(
        src_ref=src, dst_ref=dst, send_sem=ssem, recv_sem=rsem, device_id=peer, device_id_type=MESH
    )
    copy.start()
    return copy


def weight_peers(z, x, y, core):
    peers = [device_of(*partner(j, z, x, y), core) for j in range(6)]
    for delta in (1, 2, 3):
        x_t, core_t, _ = quad_peer(delta, x, core)
        peers.append(device_of(z, x_t, y, core_t))
    return peers


def gather_kernel(wa_ref, wd_ref, sm_ref, wa_out, wd_out, sm_out, *rest):
    bufs = rest[:STREAMS]
    squad, rquad, asm, qs, qr, ss, rs, fs, fr = rest[STREAMS:]
    z, x, y, core = coords(lax.axis_index("dp"), lax.axis_index("ctx"))
    bits = gray_bits(z, x, y)
    q = lax.div(x, 2) * 2 + core
    squad[...] = jnp.zeros_like(squad)
    own = wa_ref[...].astype(F32)
    for t in range(4):
        squad[t, 0:4, :] = own[:, 1024 * t : 1024 * (t + 1)]
    enter(weight_peers(z, x, y, core))
    quad = []
    for delta in (1, 2, 3):
        x_t, core_t, q_t = quad_peer(delta, x, core)
        quad.append(
            send(
                squad.at[q_t], rquad.at[q], qs.at[delta - 1], qr.at[delta - 1],
                device_of(z, x_t, y, core_t),
            )
        )
    rquad[q] = squad[q]
    slots = [slot_of(p, bits) for p in range(STREAMS)]
    bufs[4][core, slots[4]] = wd_ref[:, 0:256]
    bufs[5][core, slots[5]] = wd_ref[:, 256:512]
    bufs[6][core, slots[6]] = sm_ref[...]
    for copy in quad:
        copy.wait_recv()
    for t in range(4):
        asm[4 * t : 4 * t + 4, :] = rquad[t, 0:4, :]
    for p in range(4):
        bufs[p][core, slots[p]] = asm[:, 256 * p : 256 * (p + 1)].astype(BF16)
    sibling = device_of(z, x, y, 1 - core)
    steps, forwards = {}, {}
    for k in range(7):
        for p in (4, 5, 6, 0, 1, 2, 3):
            if k > 0:
                steps[p, k - 1].wait_recv()
            if k < 6:
                size = 2**k
                base = lax.div(slots[p], size) * size
                part = bufs[p].at[core, pl.ds(base, size)]
                peer = device_of(*partner((p + k) % 6, z, x, y), core)
                steps[p, k] = send(part, part, ss.at[p, k], rs.at[p, k], peer)
            if k == 0:
                fresh = bufs[p].at[core, pl.ds(slots[p], 1)]
            else:
                size = 2 ** (k - 1)
                base = lax.div(slots[p], size) * size
                base = base + size * (1 - 2 * bits[(p + k - 1) % 6])
                fresh = bufs[p].at[core, pl.ds(base, size)]
            forwards[p, k] = send(fresh, fresh, fs.at[p, k], fr.at[p, k], sibling)
    for copy in forwards.values():
        copy.wait_recv()
    for copy in quad + list(steps.values()) + list(forwards.values()):
        copy.wait_send()

    def unpack(row, carry):
        for t in range(4):
            z_i = lax.div(row, 8)
            x_i = (t // 2) * 2 + lax.rem(lax.div(row, 4), 2)
            b_i = gray_bits(z_i, x_i, lax.rem(row, 4))
            at = [slot_of(p, b_i) for p in range(STREAMS)]
            rows = pl.ds(pl.multiple_of(row * 16, 16), 16)
            for p in range(4):
                left = 1024 * t + 256 * p
                wa_out[rows, left : left + 256] = bufs[p][t % 2, at[p]]
            rows = pl.ds(pl.multiple_of(row * 64 + t * 16, 16), 16)
            wd_out[rows, 0:256] = bufs[4][t % 2, at[4]]
            wd_out[rows, 256:512] = bufs[5][t % 2, at[5]]
            sm_out[row * 4 + t] = bufs[6][t % 2, at[6]]
        return carry

    lax.fori_loop(0, 32, unpack, 0)


def gather_weights(wa, wd, sm):
    scratch = [VMEM((2, 64) + tile, dtype) for tile, dtype in TILES]
    scratch += [VMEM((4, 8, 1024), F32), VMEM((4, 8, 1024), F32), VMEM((16, 1024), F32)]
    dma = pltpu.SemaphoreType.DMA
    scratch += [dma((3,)), dma((3,)), dma((7, 6)), dma((7, 6)), dma((7, 7)), dma((7, 7))]
    return pl.pallas_call(
        gather_kernel,
        out_shape=(
            jax.ShapeDtypeStruct((512, 4096), BF16),
            jax.ShapeDtypeStruct((2048, 512), BF16),
            jax.ShapeDtypeStruct((128, 8, 128), F32),
        ),
        in_specs=[pl.BlockSpec(memory_space=VMEM)] * 3,
        out_specs=[pl.BlockSpec(memory_space=VMEM)] * 3,
        scratch_shapes=scratch,
        compiler_params=pltpu.CompilerParams(
            collective_id=0, has_side_effects=True, vmem_limit_bytes=LIMIT
        ),
    )(wa, wd, sm)


def reduce_kernel(wa_ref, wd_ref, sm_ref, qkv_out, proj_out, up_out, wd_out, sm_out, *rest):
    bufs = rest[:STREAMS]
    recv = rest[STREAMS : 2 * STREAMS]
    squad, rquad, asm, qs, qr, ss, rs, fs, fr = rest[2 * STREAMS :]
    z, x, y, core = coords(lax.axis_index("dp"), lax.axis_index("ctx"))
    bits = gray_bits(z, x, y)
    q = lax.div(x, 2) * 2 + core
    slots = [slot_of(p, bits) for p in range(STREAMS)]

    def pack(row, carry):
        for t in range(4):
            z_i = lax.div(row, 8)
            x_i = (t // 2) * 2 + lax.rem(lax.div(row, 4), 2)
            b_i = gray_bits(z_i, x_i, lax.rem(row, 4))
            at = [slot_of(p, b_i) for p in range(STREAMS)]
            rows = pl.ds(pl.multiple_of(row * 16, 16), 16)
            for p in range(4):
                left = 1024 * t + 256 * p
                bufs[p][t % 2, at[p]] = wa_ref[rows, left : left + 256]
            rows = pl.ds(pl.multiple_of(row * 64 + t * 16, 16), 16)
            bufs[4][t % 2, at[4]] = wd_ref[rows, 0:256]
            bufs[5][t % 2, at[5]] = wd_ref[rows, 256:512]
            bufs[6][t % 2, at[6]] = sm_ref[row * 4 + t]
        return carry

    lax.fori_loop(0, 32, pack, 0)
    enter(weight_peers(z, x, y, core))
    sibling = device_of(z, x, y, 1 - core)
    forwards = [
        send(bufs[p].at[1 - core], recv[p].at[pl.ds(0, 64)], fs.at[p], fr.at[p], sibling)
        for p in range(STREAMS)
    ]
    steps = {}

    def add(p, base, off, count):
        unit = min(count, 4)

        def body(i, carry):
            here = pl.ds(base + i * unit, unit)
            there = pl.ds(off + i * unit, unit)
            bufs[p][core, here] = bufs[p][core, here] + recv[p][there]
            return carry

        lax.fori_loop(0, count // unit, body, 0)

    for k in range(6, -1, -1):
        size = 2**k
        for p in range(STREAMS):
            if k == 6:
                forwards[p].wait_recv()
                add(p, 0, 0, 64)
            else:
                steps[p, k].wait_recv()
                if k > 0:
                    base = lax.div(slots[p], size) * size
                    add(p, base, 128 - 2 * size, size)
            if k > 0:
                half = size // 2
                base = lax.div(slots[p], half) * half
                base = base + half * (1 - 2 * bits[(p + k - 1) % 6])
                peer = device_of(*partner((p + k - 1) % 6, z, x, y), core)
                steps[p, k - 1] = send(
                    bufs[p].at[core, pl.ds(base, half)],
                    recv[p].at[pl.ds(128 - 2 * half, half)],
                    ss.at[p, k - 1], rs.at[p, k - 1], peer,
                )
    last = [
        bufs[p][core, slots[p]].astype(F32) + recv[p][126].astype(F32) for p in range(STREAMS)
    ]
    for p in range(4):
        asm[:, 256 * p : 256 * (p + 1)] = last[p]
    wd_out[:, 0:256] = last[4]
    wd_out[:, 256:512] = last[5]
    sm_out[...] = last[6]
    squad[...] = jnp.zeros_like(squad)
    for t in range(4):
        squad[t, 0:4, :] = asm[4 * t : 4 * t + 4, :]
    quad = []
    for delta in (1, 2, 3):
        x_t, core_t, q_t = quad_peer(delta, x, core)
        quad.append(
            send(
                squad.at[q_t], rquad.at[q], qs.at[delta - 1], qr.at[delta - 1],
                device_of(z, x_t, y, core_t),
            )
        )
    rquad[q] = squad[q]
    for copy in quad:
        copy.wait_recv()
    qkv_out[:, 0:1024] = rquad[0, 0:4, :]
    qkv_out[:, 1024:1536] = rquad[1, 0:4, 0:512]
    proj_out[...] = rquad[1, 0:4, 512:1024]
    up_out[:, 0:1024] = rquad[2, 0:4, :]
    up_out[:, 1024:2048] = rquad[3, 0:4, :]
    for copy in quad + list(steps.values()) + forwards:
        copy.wait_send()


def reduce_grads(wa, wd, sm):
    scratch = [VMEM((2, 64) + tile, dtype) for tile, dtype in TILES]
    scratch += [VMEM((128,) + tile, dtype) for tile, dtype in TILES]
    scratch += [VMEM((4, 8, 1024), F32), VMEM((4, 8, 1024), F32), VMEM((16, 1024), F32)]
    dma = pltpu.SemaphoreType.DMA
    scratch += [dma((3,)), dma((3,)), dma((7, 6)), dma((7, 6)), dma((7,)), dma((7,))]
    return pl.pallas_call(
        reduce_kernel,
        out_shape=(
            jax.ShapeDtypeStruct((4, 1536), F32),
            jax.ShapeDtypeStruct((4, 512), F32),
            jax.ShapeDtypeStruct((4, 2048), F32),
            jax.ShapeDtypeStruct((16, 512), F32),
            jax.ShapeDtypeStruct((8, 128), F32),
        ),
        in_specs=[pl.BlockSpec(memory_space=VMEM)] * 3,
        out_specs=[pl.BlockSpec(memory_space=VMEM)] * 5,
        scratch_shapes=scratch,
        compiler_params=pltpu.CompilerParams(
            collective_id=1, has_side_effects=True, vmem_limit_bytes=LIMIT
        ),
    )(wa, wd, sm)


def head_peer(delta, ctx):
    y, x_hi, core = lax.div(ctx, 4), lax.rem(lax.div(ctx, 2), 2), lax.rem(ctx, 2)
    if delta % 2:
        x_hi = 1 - x_hi
    if delta // 2 == 1:
        y = y + 1 - 2 * lax.rem(y, 2)
    elif delta // 2 == 2:
        y = lax.rem(y + 2, 4)
    elif delta // 2 == 3:
        y = 3 - y
    return y * 2 + x_hi, core


def head_peers(dp, ctx):
    peers = []
    for delta in range(1, 8):
        m, core = head_peer(delta, ctx)
        peers.append((dp, m * 2 + core))
    m, core = head_peer(0, ctx)
    return peers + [(dp, m * 2 + 1 - core)]


def spread_kernel(x_ref, y_ref, ss, rs, fs, fr):
    dp, ctx = lax.axis_index("dp"), lax.axis_index("ctx")
    core, me = lax.rem(ctx, 2), lax.div(ctx, 2)
    peers = head_peers(dp, ctx)
    enter(peers)
    sends = []
    for delta in range(1, 8):
        m, _ = head_peer(delta, ctx)
        sends.append(
            send(
                x_ref.at[m], y_ref.at[core, me], ss.at[delta - 1], rs.at[delta - 1],
                peers[delta - 1],
            )
        )
    y_ref[core, me] = x_ref[me]
    mine = y_ref.at[core, me]
    forwards = [send(mine, mine, fs.at[0], fr.at[0], peers[7])]
    for delta in range(1, 8):
        m, _ = head_peer(delta, ctx)
        sends[delta - 1].wait_recv()
        part = y_ref.at[core, m]
        forwards.append(send(part, part, fs.at[delta], fr.at[delta], peers[7]))
    for copy in forwards:
        copy.wait_recv()
    for copy in sends + forwards:
        copy.wait_send()


def spread_heads(x):
    dma = pltpu.SemaphoreType.DMA
    return pl.pallas_call(
        spread_kernel,
        out_shape=jax.ShapeDtypeStruct((2, 8, 128, 256), BF16),
        in_specs=[pl.BlockSpec(memory_space=VMEM)],
        out_specs=pl.BlockSpec(memory_space=VMEM),
        scratch_shapes=[dma((7,)), dma((7,)), dma((8,)), dma((8,))],
        compiler_params=pltpu.CompilerParams(
            collective_id=2, has_side_effects=True, vmem_limit_bytes=LIMIT
        ),
    )(x)


def collect_kernel(z_ref, o_ref, recv, total, ss, rs, fs, fr):
    dp, ctx = lax.axis_index("dp"), lax.axis_index("ctx")
    core, me = lax.rem(ctx, 2), lax.div(ctx, 2)
    peers = head_peers(dp, ctx)
    enter(peers)
    forwards = []
    for delta in (1, 2, 3, 4, 5, 6, 7, 0):
        m, _ = head_peer(delta, ctx)
        forwards.append(
            send(z_ref.at[1 - core, m], recv.at[m], fs.at[delta], fr.at[delta], peers[7])
        )
    sends = []
    for delta in (1, 2, 3, 4, 5, 6, 7, 0):
        m, _ = head_peer(delta, ctx)
        forwards[delta - 1].wait_recv()
        total[m] = z_ref[core, m] + recv[m]
        if delta:
            sends.append(
                send(
                    total.at[m], o_ref.at[me], ss.at[delta - 1], rs.at[delta - 1],
                    peers[delta - 1],
                )
            )
        else:
            o_ref[me] = total[m]
    for copy in sends:
        copy.wait_recv()
    for copy in sends + forwards:
        copy.wait_send()


def collect_heads(z):
    dma = pltpu.SemaphoreType.DMA
    return pl.pallas_call(
        collect_kernel,
        out_shape=jax.ShapeDtypeStruct((8, 128, 256), BF16),
        in_specs=[pl.BlockSpec(memory_space=VMEM)],
        out_specs=pl.BlockSpec(memory_space=VMEM),
        scratch_shapes=[
            VMEM((8, 128, 256), BF16), VMEM((8, 128, 256), BF16),
            dma((7,)), dma((7,)), dma((8,)), dma((8,)),
        ],
        compiler_params=pltpu.CompilerParams(
            collective_id=3, has_side_effects=True, vmem_limit_bytes=LIMIT
        ),
    )(z)


def nt(a, b):
    return lax.dot_general(a, b, (((1,), (1,)), ((), ())), preferred_element_type=F32)


def nn(a, b):
    return lax.dot_general(a, b, (((1,), (0,)), ((), ())), preferred_element_type=F32)


def tn(a, b):
    return lax.dot_general(a, b, (((0,), (0,)), ((), ())), preferred_element_type=F32)


def attend_kernel(order_ref, y_ref, z_ref, qb, kb, vb, db, att_b, dq_b, dk_b, dv_b):
    core = lax.rem(lax.axis_index("ctx"), 2)
    for s in range(32):
        there = pl.ds(pl.multiple_of(order_ref[s] * 64, 64), 64)
        part = y_ref[(s // 2) % 2, s // 4, 64 * (s % 2) : 64 * (s % 2) + 64, :]
        qb[there, :] = part[:, 0:64]
        kb[there, :] = part[:, 64:128]
        vb[there, :] = part[:, 128:192]
        db[there, :] = part[:, 192:256]
    att_b[...] = jnp.zeros_like(att_b)
    dq_b[...] = jnp.zeros_like(dq_b)
    dk_b[...] = jnp.zeros_like(dk_b)
    dv_b[...] = jnp.zeros_like(dv_b)
    for j in range(4):
        width = 512 * (j + 1)
        row = 512 * j + 256 * (1 - core if j % 2 else core)
        rows = pl.ds(pl.multiple_of(row, 256), 256)
        queries = qb[rows, :] * jnp.asarray(0.125, BF16)
        d_o = db[rows, :]
        keys, vals = kb[0:width, :], vb[0:width, :]
        scores = nt(queries, keys)
        at_q = row + lax.broadcasted_iota(jnp.int32, (256, width), 0)
        at_k = lax.broadcasted_iota(jnp.int32, (256, width), 1)
        scores = jnp.where(at_q >= at_k, scores, -1e30)
        probs = jnp.exp(scores - jnp.max(scores, axis=1, keepdims=True))
        probs = probs * (1.0 / jnp.sum(probs, axis=1, keepdims=True))
        low = probs.astype(BF16)
        att = nn(low, vals)
        delta = jnp.sum(d_o.astype(F32) * att, axis=1, keepdims=True)
        d_s = (probs * (nt(d_o, vals) - delta)).astype(BF16)
        att_b[rows, :] = att
        dq_b[rows, :] = nn(d_s, keys) * 0.125
        dk_b[0:width, :] += tn(d_s, queries)
        dv_b[0:width, :] += tn(low, d_o)
    for s in range(32):
        here = pl.ds(pl.multiple_of(order_ref[s] * 64, 64), 64)
        z_ref[(s // 2) % 2, s // 4, 64 * (s % 2) : 64 * (s % 2) + 64, :] = jnp.concatenate(
            [att_b[here, :], dq_b[here, :], dk_b[here, :], dv_b[here, :]], axis=1
        ).astype(BF16)


def attend(order, y):
    return pl.pallas_call(
        attend_kernel,
        out_shape=jax.ShapeDtypeStruct((2, 8, 128, 256), BF16),
        in_specs=[pl.BlockSpec(memory_space=pltpu.SMEM), pl.BlockSpec(memory_space=VMEM)],
        out_specs=pl.BlockSpec(memory_space=VMEM),
        scratch_shapes=[VMEM((2048, 64), BF16)] * 4 + [VMEM((2048, 64), F32)] * 4,
        compiler_params=pltpu.CompilerParams(vmem_limit_bytes=LIMIT),
    )(order, y)


def layer_norm(values, gain, shift):
    center = values - jnp.mean(values, axis=-1, keepdims=True)
    spread = jnp.mean(center * center, axis=-1, keepdims=True)
    return center * lax.rsqrt(spread + EPS) * gain + shift


def rotary(tensor, places):
    half_rot = ROT_DIM // 2
    freqs = 10000.0 ** (-jnp.arange(half_rot, dtype=jnp.float32) * 2.0 / ROT_DIM)
    angle = places.astype(jnp.float32)[:, None] * freqs[None, :]
    angle = jnp.concatenate([angle, angle], axis=-1)[:, None, :]
    turned_part = tensor[..., :ROT_DIM]
    swapped = jnp.concatenate([-turned_part[..., half_rot:], turned_part[..., :half_rot]], axis=-1)
    return jnp.concatenate(
        [turned_part * jnp.cos(angle) + swapped * jnp.sin(angle), tensor[..., ROT_DIM:]], axis=-1
    )


def per_device(
    hidden_in, positions, block_order, norm1_gain, norm1_bias, norm2_gain, norm2_bias,
    qkv_weight, qkv_bias, attn_out_weight, out_bias, up_weight, up_bias, down_weight, out_grad,
):
    small = jnp.concatenate(
        [norm1_gain, norm1_bias, norm2_gain, norm2_bias, qkv_bias, out_bias, up_bias]
    ).astype(F32)
    small = jnp.pad(small[None], ((0, 7), (0, 80)))
    wide = jnp.concatenate([qkv_weight, attn_out_weight, up_weight], axis=1)
    w_all, w_down, smalls = gather_weights(wide, down_weight, small)
    w_qkv, w_out, w_up = w_all[:, :1536], w_all[:, 1536:2048], w_all[:, 2048:]
    smalls = smalls[:, 0, :48]
    gain_one, shift_one, gain_two, shift_two = (
        smalls[:, 4 * i : 4 * i + 4].reshape(512) for i in range(4)
    )
    b_qkv = smalls[:, 16:28].reshape(1536)
    b_out = smalls[:, 28:32].reshape(512)
    b_up = smalls[:, 32:48].reshape(2048)

    inputs = hidden_in[0].astype(F32)
    grad_out = out_grad[0]
    nrows, width = inputs.shape
    places = positions[0]

    def norms(values, g_one, s_one, g_two, s_two):
        return (layer_norm(values, g_one, s_one), layer_norm(values, g_two, s_two))

    (normed_one, normed_two), norm_pull = jax.vjp(
        norms, inputs, gain_one, shift_one, gain_two, shift_two
    )
    normed_one = normed_one.astype(BF16)
    normed_two = normed_two.astype(BF16)
    qkv = (nn(normed_one, w_qkv) + b_qkv).reshape(nrows, 3, 8, 64)

    def turn_both(q_part, k_part):
        return (rotary(q_part, places), rotary(k_part, places))

    (q_turned, k_turned), turn_pull = jax.vjp(turn_both, qkv[:, 0], qkv[:, 1])
    d_mixed = nt(grad_out, w_out).astype(BF16).reshape(nrows, 8, 64)
    heads = jnp.stack(
        [q_turned.astype(BF16), k_turned.astype(BF16), qkv[:, 2].astype(BF16), d_mixed], axis=2
    )
    heads = heads.transpose(1, 0, 2, 3).reshape(8, nrows, 256)
    back = collect_heads(attend(block_order, spread_heads(heads)))
    back = back.reshape(8, nrows, 4, 64).transpose(2, 1, 0, 3)
    mixed_att = back[0].reshape(nrows, width)

    upper = nn(normed_two, w_up) + b_up
    gelu_val, gelu_pull = jax.vjp(lambda arg_in: jax.nn.gelu(arg_in, approximate=False), upper)
    gelu_out = gelu_val.astype(BF16)
    result = inputs + nn(mixed_att, w_out) + nn(gelu_out, w_down) + b_out
    block_out = result.astype(BF16)[None]
    grad_w_out = tn(mixed_att, grad_out)
    grad_w_down = tn(gelu_out, grad_out)
    grad_b_out = jnp.sum(grad_out.astype(F32), axis=0)
    d_upper = gelu_pull(nt(grad_out, w_down))[0].astype(BF16)
    grad_w_up = tn(normed_two, d_upper)
    grad_b_up = jnp.sum(d_upper.astype(F32), axis=0)
    d_normed_two = nt(d_upper, w_up)
    d_q_pre, d_k_pre = turn_pull((back[1].astype(F32), back[2].astype(F32)))
    d_qkv = (
        jnp.stack([d_q_pre, d_k_pre, back[3].astype(F32)], axis=1)
        .reshape(nrows, 3 * width)
        .astype(BF16)
    )
    grad_w_qkv = tn(normed_one, d_qkv)
    grad_b_qkv = jnp.sum(d_qkv.astype(F32), axis=0)
    d_normed_one = nt(d_qkv, w_qkv)
    d_inputs, grad_g_one, grad_s_one, grad_g_two, grad_s_two = norm_pull(
        (d_normed_one, d_normed_two)
    )
    input_grad = (grad_out.astype(F32) + d_inputs)[None]
    wide_grad = jnp.concatenate([grad_w_qkv, grad_w_out, grad_w_up], axis=1).astype(BF16)
    small_grad = jnp.concatenate(
        [
            item.reshape(128, -1)
            for item in (
                grad_g_one, grad_s_one, grad_g_two, grad_s_two,
                grad_b_qkv[:1024], grad_b_qkv[1024:], grad_b_out, grad_b_up,
            )
        ],
        axis=1,
    )
    small_grad = jnp.pad(small_grad[:, None, :], ((0, 0), (0, 7), (0, 80)))
    g_qkv, g_proj, g_up, g_down, g_small = reduce_grads(
        wide_grad, grad_w_down.astype(BF16), small_grad
    )
    g_small = g_small[0]
    return (
        block_out, input_grad, g_small[0:4], g_small[4:8], g_small[8:12], g_small[12:16],
        g_qkv, g_small[16:24], g_small[24:28], g_proj, g_small[28:32], g_up, g_small[32:48],
        g_down,
    )


def solution(mesh):
    both = ("dp", "ctx")
    rows, vec, mat = P("dp", "ctx", None), P(both), P(both, None)
    return jax.shard_map(
        per_device,
        mesh=mesh,
        in_specs=(
            rows, P("dp", "ctx"), P(), vec, vec, vec, vec, mat, vec, mat, vec, mat, vec, mat, rows,
        ),
        out_specs=(
            rows, rows, vec, vec, vec, vec, mat, vec, vec, mat, vec, mat, vec, mat,
        ),
        check_vma=False,
    )
```

```python
import jax
import jax.numpy as jnp
import numpy as np
from jax import lax
from jax.experimental import pallas as pl
from jax.experimental.pallas import tpu as pltpu
from jax.sharding import PartitionSpec as P

EPS = 1e-05
MESH = pl.DeviceIdType.MESH
F32 = jnp.float32
BF16 = jnp.bfloat16
VMEM = pltpu.VMEM
LIMIT = 60 * 1024 * 1024

ORDERS = ((0, 1, 2), (1, 2, 0), (2, 0, 1))
ORDER_OF = (0, 1, 2, 1, 0, 1, 1, 2)
COLS = (256, 128, 128, 128, 256, 256, 128, 384)
LEFT = (0, 256, 384, 0, 512, 768, 0, 128)
N = 8
FIRST, SMALL, LATER = (0, 1, 2), 3, (4, 5, 6, 7)
TILES = [((8, 128), F32) if p == SMALL else ((16, COLS[p]), BF16) for p in range(N)]
SECTIONS_IN = ((4, 0), (4, 4), (4, 8), (4, 12), (12, 16), (4, 28), (16, 32))
SECTIONS_OUT = ((4, 0), (4, 4), (4, 8), (4, 12), (8, 16), (4, 24), (4, 28), (16, 32))


def device_of(x, y, z, core):
    return (z * 2 + lax.rem(x, 2), y * 4 + lax.div(x, 2) * 2 + core)


def slot_of(p, at):
    return sum(at[axis] * 4**k for k, axis in enumerate(ORDERS[ORDER_OF[p]]))


def moved(at, axis, delta):
    at = list(at)
    at[axis] = lax.rem(at[axis] + delta, 4)
    return at


def send(src, dst, ssem, rsem, peer):
    copy = pltpu.make_async_remote_copy(
        src_ref=src, dst_ref=dst, send_sem=ssem, recv_sem=rsem, device_id=peer, device_id_type=MESH
    )
    copy.start()
    return copy


def nt(a, b):
    return lax.dot_general(a, b, (((1,), (1,)), ((), ())), preferred_element_type=F32)


def nn(a, b):
    return lax.dot_general(a, b, (((1,), (0,)), ((), ())), preferred_element_type=F32)


def tn(a, b):
    return lax.dot_general(a, b, (((0,), (0,)), ((), ())), preferred_element_type=F32)


def selectors(n, off):
    cols = lax.broadcasted_iota(jnp.int32, (1, 128 * n), 1)
    owner = ((cols.astype(F32) + 0.5) * (1.0 / n)).astype(jnp.int32)
    lane = cols - owner * n + off
    rows = lax.broadcasted_iota(jnp.int32, (128, 128 * n), 0)
    pick = jnp.where(rows == lane, 1.0, 0.0).astype(BF16)
    return pick, rows == owner


def swap_halves(u):
    lane = lax.broadcasted_iota(jnp.int32, u.shape, 1)
    lane = lane - 64 * (lane >= 64).astype(jnp.int32)
    return jnp.where(lane < 8, pltpu.roll(u, 120, 1), pltpu.roll(u, 8, 1))


def block_kernel(
    table, hid, dy_ref, pos, freq, small, w_qkv, w_proj, w_upper, w_lower,
    out_ref, ingrad_ref, gqkv_ref, gproj_ref, gup_ref, gdown_ref, gsmall_ref,
    *rest,
):
    rest = list(rest)

    def take(count):
        got = rest[:count]
        del rest[:count]
        return got

    bufs, grads, recv = take(N), take(N), take(N)
    squad, rquad, squad2, rquad2, asm, asm2 = take(6)
    wa, wu, wd, ga, gu, gd, smat, gmat = take(8)
    xs, ys, zs, crecv, ctotal, back = take(6)
    qb, kb, vb, db, att_b, dq_b, dk_b, dv_b = take(8)
    xhat, inv_s, cos_s, sin_s, vecs, gvec, h1_s, h2_s, g_s, dup_s, mlp_s, dh2_s, dqkv_s = take(13)
    qs, qr, q2s, q2r, ags, agr, fws, fwr, rss, rsr, sps, spr, sfs, sfr = take(14)
    cos_, cor_, cfs, cfr = take(4)

    dp, ctx = lax.axis_index("dp"), lax.axis_index("ctx")
    core = lax.rem(ctx, 2)
    at = [
        lax.rem(lax.div(ctx, 2), 2) * 2 + lax.rem(dp, 2), lax.div(ctx, 4), lax.div(dp, 2)
    ]
    sibling = device_of(*at, 1 - core)
    q = lax.rem(ctx, 4)
    axis_peers = [
        [device_of(*moved(at, axis, delta), core) for delta in (1, 2, 3)] for axis in range(3)
    ]
    far = moved(at, 0, 2)
    far_cross = device_of(*far, 1 - core)
    head_at = []
    for delta in range(8):
        place = moved(far if delta % 2 else at, 1, delta // 2)
        head_at.append((place[1] * 2 + lax.div(place[0], 2), device_of(*place, core)))
    me = head_at[0][0]
    quad_peers = [(sibling, 1), (head_at[1][1], 2), (far_cross, 3)]

    def quad_index(delta):
        core_t = 1 - core if delta % 2 else core
        hi = lax.div(at[0], 2)
        return (1 - hi if delta // 2 else hi) * 2 + core_t

    everyone = [sibling, far_cross] + sum(axis_peers, [])
    everyone += [head_at[delta][1] for delta in (3, 5, 7)]
    barrier = pltpu.get_barrier_semaphore()
    for peer in everyone:
        pl.semaphore_signal(barrier, inc=1, device_id=peer, device_id_type=MESH)

    slots = [slot_of(p, at) for p in range(N)]
    started = []

    squad[...] = jnp.zeros_like(squad)
    qkv_rows = w_qkv[...].astype(F32)
    up_rows = w_upper[...].astype(F32)
    for t in range(3):
        squad[t, 0:4, 0:512] = qkv_rows[:, 512 * t : 512 * (t + 1)]
    squad[3, 0:4, 0:512] = w_proj[...].astype(F32)
    for t in range(4):
        squad[t, 0:4, 512:1024] = up_rows[:, 512 * t : 512 * (t + 1)]
    for p in (6, 7):
        bufs[p][core, slots[p]] = w_lower[:, LEFT[p] : LEFT[p] + COLS[p]]
    bufs[SMALL][core, slots[SMALL]] = small[...]
    pl.semaphore_wait(barrier, len(everyone))

    quad = []
    for peer, delta in quad_peers:
        quad.append(
            send(squad.at[quad_index(delta)], rquad.at[q], qs.at[delta - 1], qr.at[delta - 1], peer)
        )
    started += quad
    rquad[q] = squad[q]
    hops, fwd = {}, {}

    def block(p, k):
        size = 4**k
        return lax.div(slots[p], size) * size, size

    def gather_send(p, k):
        base, size = block(p, k)
        axis = ORDERS[ORDER_OF[p]][k]
        part = bufs[p].at[core, pl.ds(base, size)]
        for d in range(3):
            hops[p, k, d] = send(
                part, part, ags.at[p, 3 * k + d], agr.at[p, 3 * k + d], axis_peers[axis][d]
            )
            started.append(hops[p, k, d])
        if k == 2:
            fwd[p, 3] = send(part, part, fws.at[p, 3], fwr.at[p, 3], sibling)
            started.append(fwd[p, 3])

    def gather_wait(p, k):
        for d in range(3):
            hops[p, k, d].wait_recv()

    def gather_forward(p):
        axis = ORDERS[ORDER_OF[p]][2]
        for d in range(3):
            hops[p, 2, d].wait_recv()
            base = lax.rem(at[axis] + 3 - d, 4) * 16
            part = bufs[p].at[core, pl.ds(base, 16)]
            fwd[p, d] = send(part, part, fws.at[p, d], fwr.at[p, d], sibling)
            started.append(fwd[p, d])

    def gather_done(p):
        for d in range(4):
            fwd[p, d].wait_recv()

    for p in (SMALL, 6, 7):
        gather_send(p, 0)
    for copy in quad:
        copy.wait_recv()
    for t in range(4):
        asm[4 * t : 4 * t + 4, :] = rquad[t, 0:4, :]
    for p in (0, 1, 2, 4, 5):
        bufs[p][core, slots[p]] = asm[:, LEFT[p] : LEFT[p] + COLS[p]].astype(BF16)
        gather_send(p, 0)

    x = hid[0].astype(F32)
    center = x - jnp.mean(x, axis=1, keepdims=True)
    inv = lax.rsqrt(jnp.mean(center * center, axis=1, keepdims=True) + EPS)
    xhat[...] = center * inv
    inv_s[...] = jnp.broadcast_to(inv, (128, 128))
    places = jnp.transpose(jnp.broadcast_to(pos[...].astype(F32), (128, 128)))
    angle = places * freq[...]
    lane = lax.broadcasted_iota(jnp.int32, (128, 128), 1)
    lane = lane - 64 * (lane >= 64).astype(jnp.int32)
    sine = jnp.sin(angle)
    cos_s[...] = jnp.cos(angle)
    sin_s[...] = jnp.where(lane < 8, -sine, sine)

    for k in (1, 2):
        for p in (SMALL,) + FIRST + LATER:
            gather_wait(p, k - 1)
            gather_send(p, k)
    for p in (SMALL,) + FIRST:
        gather_forward(p)

    def place_of(row, t):
        x_lo = lax.rem(lax.div(row, 4), 2)
        return [(t // 2) * 2 + x_lo, lax.rem(row, 4), lax.div(row, 8)], t % 2

    def wide_loop(streams, left0, store):
        def body(row, carry):
            rows = pl.ds(pl.multiple_of(row * 16, 16), 16)
            for t in range(4):
                where, c = place_of(row, t)
                for p in streams:
                    left = 512 * t + LEFT[p] - left0
                    store(p, c, slot_of(p, where), rows, left)
            return carry

        lax.fori_loop(0, 32, body, 0)

    def tall_loop(store):
        def body(row, carry):
            for t in range(4):
                where, c = place_of(row, t)
                rows = pl.ds(pl.multiple_of(row * 64 + t * 16, 16), 16)
                for p in (6, 7):
                    store(p, c, slot_of(p, where), rows, LEFT[p])
            return carry

        lax.fori_loop(0, 32, body, 0)

    def unpack_to(dst):
        def store(p, c, slot, rows, left):
            dst[rows, left : left + COLS[p]] = bufs[p][c, slot]

        return store

    def pack_from(src):
        def store(p, c, slot, rows, left):
            grads[p][c, slot] = src[rows, left : left + COLS[p]]

        return store

    gather_done(SMALL)

    def small_rows(row, carry):
        for t in range(4):
            where, c = place_of(row, t)
            smat[pl.ds(row * 4 + t, 1), :] = bufs[SMALL][c, slot_of(SMALL, where), 0:1, :]
        return carry

    lax.fori_loop(0, 32, small_rows, 0)
    tiles = smat[...].astype(BF16)
    for i, (n, off) in enumerate(SECTIONS_IN):
        pick, own = selectors(n, off)
        vecs[i : i + 1, 0 : 128 * n] = jnp.sum(
            jnp.where(own, nn(tiles, pick), 0.0), axis=0, keepdims=True
        )
    normed = xhat[...]
    h1_s[...] = (normed * vecs[0:1, 0:512] + vecs[1:2, 0:512]).astype(BF16)
    h2_s[...] = (normed * vecs[2:3, 0:512] + vecs[3:4, 0:512]).astype(BF16)
    for p in FIRST:
        gather_done(p)
    wide_loop(FIRST, 0, unpack_to(wa))

    dy = dy_ref[0]
    parts = [nn(h1_s[...], wa[:, 512 * i : 512 * (i + 1)]) for i in range(3)]
    parts = [parts[i] + vecs[4:5, 512 * i : 512 * (i + 1)] for i in range(3)]
    cos_t, sin_t = cos_s[...], sin_s[...]

    def turn(u, sign):
        return jnp.concatenate(
            [
                u[:, c : c + 128] * cos_t + swap_halves(u[:, c : c + 128]) * (sin_t * sign)
                for c in range(0, 512, 128)
            ],
            axis=1,
        )

    sent = [turn(parts[0], 1.0), turn(parts[1], 1.0), parts[2], nt(dy, wa[:, 1536:2048])]
    sent = [item.astype(BF16) for item in sent]
    for h in range(8):
        piece = jnp.concatenate([item[:, 64 * h : 64 * h + 64] for item in sent], axis=1)
        xs[h, 0] = piece[0:64]
        xs[h, 1] = piece[64:128]
    spread, spread_fwd = [], []

    def spot(c, m):
        return pl.ds(c * 16 + m * 2, 2)

    for delta in range(1, 8):
        m, peer = head_at[delta]
        spread.append(
            send(xs.at[m], ys.at[spot(core, me)], sps.at[delta - 1], spr.at[delta - 1], peer)
        )
    ys[spot(core, me)] = xs[me]
    mine = ys.at[spot(core, me)]
    spread_fwd.append(send(mine, mine, sfs.at[0], sfr.at[0], sibling))

    for p in LATER:
        gather_forward(p)
    for p in LATER:
        gather_done(p)
    wide_loop((4, 5), 512, unpack_to(wu))
    tall_loop(unpack_to(wd))

    def mlp(t):
        cols = slice(512 * t, 512 * (t + 1))
        up = nn(h2_s[...], wu[:, cols]) + vecs[6:7, cols]
        cdf = 0.5 * (1.0 + lax.erf(up * np.float32(0.5**0.5)))
        pdf = jnp.exp(-0.5 * up * up) * np.float32((2 * np.pi) ** -0.5)
        g = (up * cdf).astype(BF16)
        d_up = (nt(dy, wd[cols, :]) * (cdf + up * pdf)).astype(BF16)
        g_s[:, cols] = g
        dup_s[:, cols] = d_up
        gvec[7:8, cols] = jnp.sum(d_up.astype(F32), axis=0, keepdims=True)
        gu[:, cols] = tn(h2_s[...], d_up).astype(BF16)
        gd[cols, :] = tn(g, dy).astype(BF16)

    for t in range(4):
        mlp(t)
        if t == 1:
            for delta in range(1, 8):
                back_y = (4 - delta // 2) % 4
                m = head_at[back_y * 2 + delta % 2][0]
                spread[delta - 1].wait_recv()
                part = ys.at[spot(core, m)]
                spread_fwd.append(send(part, part, sfs.at[delta], sfr.at[delta], sibling))
    started += spread + spread_fwd

    adds = {}

    def reduce_start(p):
        adds[p, 3] = send(
            grads[p].at[1 - core], recv[p].at[pl.ds(0, 64)], rss.at[p, 9], rsr.at[p, 9], sibling
        )
        started.append(adds[p, 3])

    def offset(k):
        return 64 + {2: 0, 1: 48, 0: 60}[k]

    def reduce_step(p, k):
        if k == 2:
            adds[p, 3].wait_recv()
            total, others, base = 64, (0,), 0
        else:
            for d in range(3):
                adds[p, k + 1, d].wait_recv()
            base, total = block(p, k + 1)
            others = [offset(k + 1) + d * total for d in range(3)]
        unit = min(total, 4)

        def body(i, carry):
            here = pl.ds(base + i * unit, unit)
            value = grads[p][core, here].astype(F32)
            for other in others:
                value = value + recv[p][pl.ds(other + i * unit, unit)].astype(F32)
            grads[p][core, here] = value.astype(grads[p].dtype)
            return carry

        lax.fori_loop(0, total // unit, body, 0)
        axis = ORDERS[ORDER_OF[p]][k]
        size = 4**k
        own, _ = block(p, k)
        for d in range(3):
            there = lax.rem(at[axis] + d + 1, 4)
            part = grads[p].at[core, pl.ds(own + (there - at[axis]) * size, size)]
            adds[p, k, d] = send(
                part, recv[p].at[pl.ds(offset(k) + d * size, size)],
                rss.at[p, 3 * k + d], rsr.at[p, 3 * k + d], axis_peers[axis][d],
            )
            started.append(adds[p, k, d])

    def reduce_end(p):
        for d in range(3):
            adds[p, 0, d].wait_recv()
        value = grads[p][core, slots[p]].astype(F32)
        for d in range(3):
            value = value + recv[p][offset(0) + d].astype(F32)
        return value

    wide_loop((4, 5), 512, pack_from(gu))
    tall_loop(pack_from(gd))
    for p in LATER:
        reduce_start(p)

    for copy in spread_fwd:
        copy.wait_recv()
    for t in range(32):
        part = ys[table[32 + t]]
        rows = slice(64 * t, 64 * t + 64)
        qb[rows, :] = part[:, 0:64]
        kb[rows, :] = part[:, 64:128]
        vb[rows, :] = part[:, 128:192]
        db[rows, :] = part[:, 192:256]
    att_b[...] = jnp.zeros_like(att_b)
    dq_b[...] = jnp.zeros_like(dq_b)
    dk_b[...] = jnp.zeros_like(dk_b)
    dv_b[...] = jnp.zeros_like(dv_b)

    def tile(j):
        width = 512 * (j + 1)
        row = 512 * j + 256 * (1 - core if j % 2 else core)
        rows = pl.ds(pl.multiple_of(row, 256), 256)
        queries = qb[rows, :] * jnp.asarray(0.125, BF16)
        d_o = db[rows, :]
        keys, vals = kb[0:width, :], vb[0:width, :]
        scores = nt(queries, keys)
        at_q = row + lax.broadcasted_iota(jnp.int32, (256, width), 0)
        at_k = lax.broadcasted_iota(jnp.int32, (256, width), 1)
        scores = jnp.where(at_q >= at_k, scores, -1e30)
        probs = jnp.exp(scores - jnp.max(scores, axis=1, keepdims=True))
        probs = probs * (1.0 / jnp.sum(probs, axis=1, keepdims=True))
        low = probs.astype(BF16)
        att = nn(low, vals)
        delta = jnp.sum(d_o.astype(F32) * att, axis=1, keepdims=True)
        d_s = (probs * (nt(d_o, vals) - delta)).astype(BF16)
        blocks = pl.ds(8 * j + 4 * (1 - core if j % 2 else core), 4)
        att_b[blocks] = att.reshape(4, 64, 64)
        dq_b[blocks] = (nn(d_s, keys) * 0.125).reshape(4, 64, 64)
        reach = slice(0, 8 * (j + 1))
        dk_b[reach] += tn(d_s, queries).reshape(8 * (j + 1), 64, 64)
        dv_b[reach] += tn(low, d_o).reshape(8 * (j + 1), 64, 64)

    for j in range(4):
        tile(j)
        if j > 0:
            for p in LATER:
                reduce_step(p, 3 - j)
    for i in range(32):
        t = table[i]
        zs[i] = jnp.concatenate([att_b[t], dq_b[t], dk_b[t], dv_b[t]], axis=1).astype(BF16)

    order = (1, 2, 3, 4, 5, 6, 7, 0)
    halves, collect = {}, []
    for delta in order:
        m, _ = head_at[delta]
        halves[delta] = send(
            zs.at[spot(1 - core, m)], crecv.at[m], cfs.at[delta], cfr.at[delta], sibling
        )
    started += list(halves.values())
    mlp_s[...] = nn(g_s[...], wd[...])
    for delta in order:
        m, peer = head_at[delta]
        halves[delta].wait_recv()
        ctotal[m] = zs[spot(core, m)] + crecv[m]
        if delta:
            collect.append(
                send(ctotal.at[m], back.at[me], cos_.at[delta - 1], cor_.at[delta - 1], peer)
            )
        else:
            back[me] = ctotal[m]
    started += collect
    dh2_s[...] = nt(dup_s[...], wu[...])
    dh2 = dh2_s[...]
    gvec[2:3, 0:512] = jnp.sum(dh2 * xhat[...], axis=0, keepdims=True)
    gvec[3:4, 0:512] = jnp.sum(dh2, axis=0, keepdims=True)
    gvec[6:7, 0:512] = jnp.sum(dy.astype(F32), axis=0, keepdims=True)
    for p in LATER:
        value = reduce_end(p)
        if p < 6:
            asm2[:, LEFT[p] : LEFT[p] + COLS[p]] = value
        else:
            gdown_ref[:, LEFT[p] : LEFT[p] + COLS[p]] = value
    for copy in collect:
        copy.wait_recv()

    def whole(i):
        return jnp.concatenate(
            [
                jnp.concatenate(
                    [back[h, 0, :, 64 * i : 64 * i + 64], back[h, 1, :, 64 * i : 64 * i + 64]],
                    axis=0,
                )
                for h in range(8)
            ],
            axis=1,
        )

    dqkv_s[:, 0:512] = turn(whole(1).astype(F32), -1.0).astype(BF16)
    dqkv_s[:, 512:1024] = turn(whole(2).astype(F32), -1.0).astype(BF16)
    dqkv_s[:, 1024:1536] = whole(3)
    mixed = whole(0)
    ga[:, 1536:2048] = tn(mixed, dy).astype(BF16)
    for t in range(3):
        ga[:, 512 * t : 512 * (t + 1)] = tn(
            h1_s[...], dqkv_s[:, 512 * t : 512 * (t + 1)]
        ).astype(BF16)
    wide_loop(FIRST, 0, pack_from(ga))
    for p in FIRST:
        reduce_start(p)
    dh1 = nt(dqkv_s[...], wa[:, 0:1536])
    gvec[0:1, 0:512] = jnp.sum(dh1 * xhat[...], axis=0, keepdims=True)
    gvec[1:2, 0:512] = jnp.sum(dh1, axis=0, keepdims=True)
    gvec[4:5, 0:1024] = jnp.sum(dqkv_s[:, 0:1024].astype(F32), axis=0, keepdims=True)
    gvec[5:6, 0:512] = jnp.sum(dqkv_s[:, 1024:1536].astype(F32), axis=0, keepdims=True)
    spread_out = jnp.zeros((128, 128), F32)
    for i, (n, off) in enumerate(SECTIONS_OUT):
        pick, own = selectors(n, off)
        value = jnp.where(own, gvec[i : i + 1, 0 : 128 * n], 0.0)
        high = value.astype(BF16)
        low = (value - high.astype(F32)).astype(BF16)
        spread_out = spread_out + nt(high, pick) + nt(low, pick)
    gmat[...] = spread_out
    grads[SMALL][...] = jnp.zeros_like(grads[SMALL])

    def small_grads(row, carry):
        for t in range(4):
            where, c = place_of(row, t)
            grads[SMALL][c, slot_of(SMALL, where), 0:1, :] = gmat[pl.ds(row * 4 + t, 1), :]
        return carry

    lax.fori_loop(0, 32, small_grads, 0)
    reduce_start(SMALL)
    for p in FIRST:
        reduce_step(p, 2)
    reduce_step(SMALL, 2)
    d_norm = dh1 * vecs[0:1, 0:512] + dh2_s[...] * vecs[2:3, 0:512]
    normed = xhat[...]
    d_x = d_norm - jnp.mean(d_norm, axis=1, keepdims=True)
    d_x = d_x - normed * jnp.mean(d_norm * normed, axis=1, keepdims=True)
    ingrad_ref[0] = dy.astype(F32) + d_x * inv_s[:, 0:1]
    result = hid[0].astype(F32) + nn(mixed, wa[:, 1536:2048]) + mlp_s[...] + vecs[5:6, 0:512]
    out_ref[0] = result.astype(BF16)
    for k in (1, 0):
        for p in FIRST + (SMALL,):
            reduce_step(p, k)
    for p in FIRST:
        asm2[:, LEFT[p] : LEFT[p] + COLS[p]] = reduce_end(p)
    gsmall_ref[...] = reduce_end(SMALL)
    squad2[...] = jnp.zeros_like(squad2)
    for t in range(4):
        squad2[t, 0:4, :] = asm2[4 * t : 4 * t + 4, :]
    quad = []
    for peer, delta in quad_peers:
        quad.append(
            send(
                squad2.at[quad_index(delta)], rquad2.at[q], q2s.at[delta - 1], q2r.at[delta - 1],
                peer,
            )
        )
    started += quad
    rquad2[q] = squad2[q]
    for copy in quad:
        copy.wait_recv()
    for t in range(3):
        gqkv_ref[:, 512 * t : 512 * (t + 1)] = rquad2[t, 0:4, 0:512]
    gproj_ref[...] = rquad2[3, 0:4, 0:512]
    for t in range(4):
        gup_ref[:, 512 * t : 512 * (t + 1)] = rquad2[t, 0:4, 512:1024]
    for copy in started:
        copy.wait_send()


def run_block(*args):
    dma = pltpu.SemaphoreType.DMA
    scratch = [VMEM((2, 64) + tile, dtype) for tile, dtype in TILES] * 2
    scratch += [VMEM((128,) + tile, dtype) for tile, dtype in TILES]
    scratch += [VMEM((4, 8, 1024), F32)] * 4 + [VMEM((16, 1024), F32)] * 2
    scratch += [VMEM((512, 2048), BF16), VMEM((512, 2048), BF16), VMEM((2048, 512), BF16)] * 2
    scratch += [VMEM((128, 128), F32)] * 2
    scratch += [VMEM((8, 2, 64, 256), BF16), VMEM((32, 64, 256), BF16), VMEM((32, 64, 256), BF16)]
    scratch += [VMEM((8, 2, 64, 256), BF16)] * 3
    scratch += [VMEM((2048, 64), BF16)] * 4 + [VMEM((32, 64, 64), F32)] * 4
    scratch += [VMEM((128, 512), F32)] + [VMEM((128, 128), F32)] * 3 + [VMEM((8, 2048), F32)] * 2
    scratch += [VMEM((128, 512), BF16)] * 2 + [VMEM((128, 2048), BF16)] * 2
    scratch += [VMEM((128, 512), F32)] * 2 + [VMEM((128, 1536), BF16)]
    scratch += [dma((3,))] * 4 + [dma((N, 9))] * 2 + [dma((N, 4))] * 2 + [dma((N, 10))] * 2
    scratch += [dma((7,)), dma((7,)), dma((8,)), dma((8,))] * 2
    shape = jax.ShapeDtypeStruct
    return pl.pallas_call(
        block_kernel,
        out_shape=(
            shape((1, 128, 512), BF16), shape((1, 128, 512), F32), shape((4, 1536), F32),
            shape((4, 512), F32), shape((4, 2048), F32), shape((16, 512), F32), shape((8, 128), F32),
        ),
        in_specs=[pl.BlockSpec(memory_space=pltpu.SMEM)] + [pl.BlockSpec(memory_space=VMEM)] * 9,
        out_specs=[pl.BlockSpec(memory_space=VMEM)] * 7,
        scratch_shapes=scratch,
        compiler_params=pltpu.CompilerParams(
            collective_id=0, has_side_effects=True, vmem_limit_bytes=LIMIT
        ),
    )(*args)


def finish_kernel(*refs):
    for src, dst in zip(refs[:6], refs[7:13]):
        dst[...] = src[...]
    row = refs[6][0:1, :]
    for (n, off), dst in zip(SECTIONS_OUT, refs[13:]):
        dst[...] = row[:, off : off + n]


def finish(*parts):
    shape = jax.ShapeDtypeStruct
    return pl.pallas_call(
        finish_kernel,
        out_shape=tuple(shape(part.shape, part.dtype) for part in parts[:6])
        + tuple(shape((1, n), F32) for n, _ in SECTIONS_OUT),
        in_specs=[pl.BlockSpec(memory_space=VMEM)] * 7,
        out_specs=[pl.BlockSpec(memory_space=VMEM)] * 14,
    )(*parts)


def per_device(
    hidden_in, positions, block_order, norm1_gain, norm1_bias, norm2_gain, norm2_bias,
    qkv_weight, qkv_bias, attn_out_weight, out_bias, up_weight, up_bias, down_weight, out_grad,
):
    small = jnp.concatenate(
        [norm1_gain, norm1_bias, norm2_gain, norm2_bias, qkv_bias, out_bias, up_bias]
    ).astype(F32)
    small = jnp.pad(small[None], ((0, 7), (0, 80)))
    held = block_order.reshape(8, 2, 2).transpose(1, 0, 2).reshape(32)
    ids = jnp.arange(32, dtype=jnp.int32)
    inverse = jnp.sum(jnp.where(held[:, None] == ids[None, :], ids[:, None], 0), axis=0)
    table = jnp.concatenate([held, inverse])
    freqs = 10000.0 ** (-np.arange(8, dtype=np.float32) * np.float32(2.0) / np.float32(16))
    lanes = np.concatenate([freqs, freqs, np.zeros(48)]).astype(np.float32)
    freq = jnp.asarray(np.concatenate([lanes, lanes])[None])
    parts = run_block(
        table, hidden_in, out_grad, positions, freq, small,
        qkv_weight, attn_out_weight, up_weight, down_weight,
    )
    done = finish(*parts)
    block_out, input_grad, g_qkv, g_proj, g_up, g_down = done[:6]
    n1g, n1b, n2g, n2b, qk, val, out, up = (item.reshape(-1) for item in done[6:])
    return (
        block_out, input_grad, n1g, n1b, n2g, n2b, g_qkv, qk, val, g_proj, out, g_up, up, g_down,
    )


def solution(mesh):
    both = ("dp", "ctx")
    rows, vec, mat = P("dp", "ctx", None), P(both), P(both, None)
    return jax.shard_map(
        per_device,
        mesh=mesh,
        in_specs=(
            rows, P("dp", "ctx"), P(), vec, vec, vec, vec, mat, vec, mat, vec, mat, vec, mat, rows,
        ),
        out_specs=(
            rows, rows, vec, vec, vec, vec, mat, vec, vec, mat, vec, mat, vec, mat,
        ),
        check_vma=False,
    )
```

```python
import jax
import jax.numpy as jnp
import numpy as np
from jax import lax
from jax.experimental import pallas as pl
from jax.experimental.pallas import tpu as pltpu
from jax.sharding import PartitionSpec as P

EPS = 1e-05
MESH = pl.DeviceIdType.MESH
F32 = jnp.float32
BF16 = jnp.bfloat16
VMEM = pltpu.VMEM
LIMIT = 60 * 1024 * 1024

ORDERS = ((0, 1, 2), (1, 2, 0), (2, 0, 1))
ORDER_OF = (0, 1, 2, 1, 0, 1, 1, 2)
COLS = (256, 128, 128, 128, 256, 256, 128, 384)
LEFT = (0, 256, 384, 0, 512, 768, 0, 128)
N = 8
FIRST, SMALL, LATER = (0, 1, 2), 3, (4, 5, 6, 7)
TILES = [((8, 128), F32) if p == SMALL else ((16, COLS[p]), BF16) for p in range(N)]
SECTIONS_IN = ((4, 0), (4, 4), (4, 8), (4, 12), (12, 16), (4, 28), (16, 32))
SECTIONS_OUT = ((4, 0), (4, 4), (4, 8), (4, 12), (8, 16), (4, 24), (4, 28), (16, 32))


def device_of(x, y, z, core):
    return (z * 2 + lax.rem(x, 2), y * 4 + lax.div(x, 2) * 2 + core)


def slot_of(p, at):
    return sum(at[axis] * 4**k for k, axis in enumerate(ORDERS[ORDER_OF[p]]))


def moved(at, axis, delta):
    at = list(at)
    at[axis] = lax.rem(at[axis] + delta, 4)
    return at


def send(src, dst, ssem, rsem, peer):
    copy = pltpu.make_async_remote_copy(
        src_ref=src, dst_ref=dst, send_sem=ssem, recv_sem=rsem, device_id=peer, device_id_type=MESH
    )
    copy.start()
    return copy


def nt(a, b):
    return lax.dot_general(a, b, (((1,), (1,)), ((), ())), preferred_element_type=F32)


def nn(a, b):
    return lax.dot_general(a, b, (((1,), (0,)), ((), ())), preferred_element_type=F32)


def tn(a, b):
    return lax.dot_general(a, b, (((0,), (0,)), ((), ())), preferred_element_type=F32)


def selectors(n, off):
    cols = lax.broadcasted_iota(jnp.int32, (1, 128 * n), 1)
    owner = ((cols.astype(F32) + 0.5) * (1.0 / n)).astype(jnp.int32)
    lane = cols - owner * n + off
    rows = lax.broadcasted_iota(jnp.int32, (128, 128 * n), 0)
    pick = jnp.where(rows == lane, 1.0, 0.0).astype(BF16)
    return pick, jnp.where(rows == owner, 1.0, 0.0).astype(BF16)


def swap_halves(u):
    lane = lax.broadcasted_iota(jnp.int32, u.shape, 1)
    lane = lane - 64 * (lane >= 64).astype(jnp.int32)
    return jnp.where(lane < 8, pltpu.roll(u, 120, 1), pltpu.roll(u, 8, 1))


def block_kernel(
    table, hid, dy_ref, pos, freq, small, w_qkv, w_proj, w_upper, w_lower,
    out_ref, ingrad_ref, gqkv_ref, gproj_ref, gup_ref, gdown_ref, gsmall_ref,
    *rest,
):
    rest = list(rest)

    def take(count):
        got = rest[:count]
        del rest[:count]
        return got

    bufs, grads, recv = take(N), take(N), take(N)
    squad, rquad, squad2, rquad2, asm, asm2 = take(6)
    wa, wu, wd, ga, gu, gd, smat, gmat = take(8)
    xs, ys, zs, crecv, ctotal, back = take(6)
    qb, kb, vb, db, att_b, dq_b, dk_b, dv_b = take(8)
    xhat, inv_s, cos_s, sin_s, vecs, gvec, h1_s, h2_s, g_s, dup_s, mlp_s, dh2_s, dqkv_s = take(13)
    qs, qr, q2s, q2r, ags, agr, fws, fwr, rss, rsr, sps, spr, sfs, sfr = take(14)
    cos_, cor_, cfs, cfr = take(4)
    pick_in, own_in, pick_out, own_out, kt_b, vt_b = take(6)

    dp, ctx = lax.axis_index("dp"), lax.axis_index("ctx")
    core = lax.rem(ctx, 2)
    at = [
        lax.rem(lax.div(ctx, 2), 2) * 2 + lax.rem(dp, 2), lax.div(ctx, 4), lax.div(dp, 2)
    ]
    sibling = device_of(*at, 1 - core)
    q = lax.rem(ctx, 4)
    axis_peers = [
        [device_of(*moved(at, axis, delta), core) for delta in (1, 2, 3)] for axis in range(3)
    ]
    far = moved(at, 0, 2)
    far_cross = device_of(*far, 1 - core)
    head_at = []
    for delta in range(8):
        place = moved(far if delta % 2 else at, 1, delta // 2)
        head_at.append((place[1] * 2 + lax.div(place[0], 2), device_of(*place, core)))
    me = head_at[0][0]
    quad_peers = [(sibling, 1), (head_at[1][1], 2), (far_cross, 3)]

    def quad_index(delta):
        core_t = 1 - core if delta % 2 else core
        hi = lax.div(at[0], 2)
        return (1 - hi if delta // 2 else hi) * 2 + core_t

    everyone = [sibling, far_cross] + sum(axis_peers, [])
    everyone += [head_at[delta][1] for delta in (3, 5, 7)]
    barrier = pltpu.get_barrier_semaphore()
    for peer in everyone:
        pl.semaphore_signal(barrier, inc=1, device_id=peer, device_id_type=MESH)

    slots = [slot_of(p, at) for p in range(N)]
    started = []

    squad[...] = jnp.zeros_like(squad)
    qkv_rows = w_qkv[...].astype(F32)
    up_rows = w_upper[...].astype(F32)
    for t in range(3):
        squad[t, 0:4, 0:512] = qkv_rows[:, 512 * t : 512 * (t + 1)]
    squad[3, 0:4, 0:512] = w_proj[...].astype(F32)
    for t in range(4):
        squad[t, 0:4, 512:1024] = up_rows[:, 512 * t : 512 * (t + 1)]
    for p in (6, 7):
        bufs[p][core, slots[p]] = w_lower[:, LEFT[p] : LEFT[p] + COLS[p]]
    bufs[SMALL][core, slots[SMALL]] = small[...]
    pl.semaphore_wait(barrier, len(everyone))

    quad = []
    for peer, delta in quad_peers:
        quad.append(
            send(squad.at[quad_index(delta)], rquad.at[q], qs.at[delta - 1], qr.at[delta - 1], peer)
        )
    started += quad
    rquad[q] = squad[q]
    hops, fwd = {}, {}

    def block(p, k):
        size = 4**k
        return lax.div(slots[p], size) * size, size

    def gather_send(p, k):
        base, size = block(p, k)
        axis = ORDERS[ORDER_OF[p]][k]
        part = bufs[p].at[core, pl.ds(base, size)]
        for d in range(3):
            hops[p, k, d] = send(
                part, part, ags.at[p, 3 * k + d], agr.at[p, 3 * k + d], axis_peers[axis][d]
            )
            started.append(hops[p, k, d])
        if k == 2:
            fwd[p, 3] = send(part, part, fws.at[p, 3], fwr.at[p, 3], sibling)
            started.append(fwd[p, 3])

    def gather_wait(p, k):
        for d in range(3):
            hops[p, k, d].wait_recv()

    def gather_forward(p):
        axis = ORDERS[ORDER_OF[p]][2]
        for d in range(3):
            hops[p, 2, d].wait_recv()
            base = lax.rem(at[axis] + 3 - d, 4) * 16
            part = bufs[p].at[core, pl.ds(base, 16)]
            fwd[p, d] = send(part, part, fws.at[p, d], fwr.at[p, d], sibling)
            started.append(fwd[p, d])

    def gather_done(p):
        for d in range(4):
            fwd[p, d].wait_recv()

    for p in (SMALL, 6, 7):
        gather_send(p, 0)
    for copy in quad:
        copy.wait_recv()
    for t in range(4):
        asm[4 * t : 4 * t + 4, :] = rquad[t, 0:4, :]
    for p in (0, 1, 2, 4, 5):
        bufs[p][core, slots[p]] = asm[:, LEFT[p] : LEFT[p] + COLS[p]].astype(BF16)
        gather_send(p, 0)

    x = hid[0].astype(F32)
    center = x - jnp.mean(x, axis=1, keepdims=True)
    inv = lax.rsqrt(jnp.mean(center * center, axis=1, keepdims=True) + EPS)
    xhat[...] = center * inv
    inv_s[...] = jnp.broadcast_to(inv, (128, 128))
    places = jnp.transpose(jnp.broadcast_to(pos[...].astype(F32), (128, 128)))
    angle = places * freq[...]
    lane = lax.broadcasted_iota(jnp.int32, (128, 128), 1)
    lane = lane - 64 * (lane >= 64).astype(jnp.int32)
    sine = jnp.sin(angle)
    cos_s[...] = jnp.cos(angle)
    sin_s[...] = jnp.where(lane < 8, -sine, sine)
    for sections, picks, owns in (
        (SECTIONS_IN, pick_in, own_in), (SECTIONS_OUT, pick_out, own_out)
    ):
        left = 0
        for n, off in sections:
            pick, own = selectors(n, off)
            picks[:, left : left + 128 * n] = pick
            owns[:, left : left + 128 * n] = own
            left += 128 * n

    for p in (SMALL,) + FIRST + LATER:
        gather_wait(p, 0)
        gather_send(p, 1)
    for p in (SMALL,) + FIRST:
        gather_wait(p, 1)
        gather_send(p, 2)
    for p in (SMALL,) + FIRST:
        gather_forward(p)
    for p in LATER:
        gather_wait(p, 1)
        gather_send(p, 2)

    def place_of(row, t):
        x_lo = lax.rem(lax.div(row, 4), 2)
        return [(t // 2) * 2 + x_lo, lax.rem(row, 4), lax.div(row, 8)], t % 2

    def wide_loop(streams, left0, store):
        def body(row, carry):
            rows = pl.ds(pl.multiple_of(row * 16, 16), 16)
            for t in range(4):
                where, c = place_of(row, t)
                for p in streams:
                    left = 512 * t + LEFT[p] - left0
                    store(p, c, slot_of(p, where), rows, left)
            return carry

        lax.fori_loop(0, 32, body, 0)

    def tall_loop(store):
        def body(row, carry):
            for t in range(4):
                where, c = place_of(row, t)
                rows = pl.ds(pl.multiple_of(row * 64 + t * 16, 16), 16)
                for p in (6, 7):
                    store(p, c, slot_of(p, where), rows, LEFT[p])
            return carry

        lax.fori_loop(0, 32, body, 0)

    def unpack_to(dst):
        def store(p, c, slot, rows, left):
            dst[rows, left : left + COLS[p]] = bufs[p][c, slot]

        return store

    def pack_from(src):
        def store(p, c, slot, rows, left):
            grads[p][c, slot] = src[rows, left : left + COLS[p]]

        return store

    gather_done(SMALL)

    def small_rows(row, carry):
        for t in range(4):
            where, c = place_of(row, t)
            smat[pl.ds(row * 4 + t, 1), :] = bufs[SMALL][c, slot_of(SMALL, where), 0:1, :]
        return carry

    lax.fori_loop(0, 32, small_rows, 0)
    tiles = smat[...].astype(BF16)
    left = 0
    for i, (n, off) in enumerate(SECTIONS_IN):
        cols = slice(left, left + 128 * n)
        left += 128 * n
        vecs[i : i + 1, 0 : 128 * n] = jnp.sum(
            own_in[:, cols].astype(F32) * nn(tiles, pick_in[:, cols]), axis=0, keepdims=True
        )
    normed = xhat[...]
    h1_s[...] = (normed * vecs[0:1, 0:512] + vecs[1:2, 0:512]).astype(BF16)
    h2_s[...] = (normed * vecs[2:3, 0:512] + vecs[3:4, 0:512]).astype(BF16)
    for p in FIRST:
        gather_done(p)
    wide_loop(FIRST, 0, unpack_to(wa))

    dy = dy_ref[0]
    parts = [nn(h1_s[...], wa[:, 512 * i : 512 * (i + 1)]) for i in range(3)]
    parts = [parts[i] + vecs[4:5, 512 * i : 512 * (i + 1)] for i in range(3)]
    cos_t, sin_t = cos_s[...], sin_s[...]

    def turn(u, sign):
        return jnp.concatenate(
            [
                u[:, c : c + 128] * cos_t + swap_halves(u[:, c : c + 128]) * (sin_t * sign)
                for c in range(0, 512, 128)
            ],
            axis=1,
        )

    sent = [turn(parts[0], 1.0), turn(parts[1], 1.0), parts[2], nt(dy, wa[:, 1536:2048])]
    sent = [item.astype(BF16) for item in sent]
    for h in range(8):
        piece = jnp.concatenate([item[:, 64 * h : 64 * h + 64] for item in sent], axis=1)
        xs[h, 0] = piece[0:64]
        xs[h, 1] = piece[64:128]
    spread, spread_fwd = [], []

    def spot(c, m):
        return pl.ds(c * 16 + m * 2, 2)

    for delta in range(1, 8):
        m, peer = head_at[delta]
        spread.append(
            send(xs.at[m], ys.at[spot(core, me)], sps.at[delta - 1], spr.at[delta - 1], peer)
        )
    ys[spot(core, me)] = xs[me]
    mine = ys.at[spot(core, me)]
    spread_fwd.append(send(mine, mine, sfs.at[0], sfr.at[0], sibling))

    for p in LATER:
        gather_forward(p)
    for p in LATER:
        gather_done(p)
    wide_loop((4, 5), 512, unpack_to(wu))
    tall_loop(unpack_to(wd))

    def mlp(t):
        cols = slice(512 * t, 512 * (t + 1))
        up = nn(h2_s[...], wu[:, cols]) + vecs[6:7, cols]
        cdf = 0.5 * (1.0 + lax.erf(up * np.float32(0.5**0.5)))
        pdf = jnp.exp(-0.5 * up * up) * np.float32((2 * np.pi) ** -0.5)
        g = (up * cdf).astype(BF16)
        d_up = (nt(dy, wd[cols, :]) * (cdf + up * pdf)).astype(BF16)
        g_s[:, cols] = g
        dup_s[:, cols] = d_up
        gvec[7:8, cols] = jnp.sum(d_up.astype(F32), axis=0, keepdims=True)
        gu[:, cols] = tn(h2_s[...], d_up).astype(BF16)
        gd[cols, :] = tn(g, dy).astype(BF16)

    for t in range(4):
        mlp(t)
        if t == 1:
            for delta in range(1, 8):
                back_y = (4 - delta // 2) % 4
                m = head_at[back_y * 2 + delta % 2][0]
                spread[delta - 1].wait_recv()
                part = ys.at[spot(core, m)]
                spread_fwd.append(send(part, part, sfs.at[delta], sfr.at[delta], sibling))
    started += spread + spread_fwd

    adds = {}

    def reduce_start(p):
        adds[p, 3] = send(
            grads[p].at[1 - core], recv[p].at[pl.ds(0, 64)], rss.at[p, 9], rsr.at[p, 9], sibling
        )
        started.append(adds[p, 3])

    def offset(k):
        return 64 + {2: 0, 1: 48, 0: 60}[k]

    def reduce_step(p, k):
        if k == 2:
            adds[p, 3].wait_recv()
            total, others, base = 64, (0,), 0
        else:
            for d in range(3):
                adds[p, k + 1, d].wait_recv()
            base, total = block(p, k + 1)
            others = [offset(k + 1) + d * total for d in range(3)]
        unit = min(total, 4)

        def body(i, carry):
            here = pl.ds(base + i * unit, unit)
            value = grads[p][core, here].astype(F32)
            for other in others:
                value = value + recv[p][pl.ds(other + i * unit, unit)].astype(F32)
            grads[p][core, here] = value.astype(grads[p].dtype)
            return carry

        lax.fori_loop(0, total // unit, body, 0)
        axis = ORDERS[ORDER_OF[p]][k]
        size = 4**k
        own, _ = block(p, k)
        for d in range(3):
            there = lax.rem(at[axis] + d + 1, 4)
            part = grads[p].at[core, pl.ds(own + (there - at[axis]) * size, size)]
            adds[p, k, d] = send(
                part, recv[p].at[pl.ds(offset(k) + d * size, size)],
                rss.at[p, 3 * k + d], rsr.at[p, 3 * k + d], axis_peers[axis][d],
            )
            started.append(adds[p, k, d])

    def reduce_end(p):
        for d in range(3):
            adds[p, 0, d].wait_recv()
        value = grads[p][core, slots[p]].astype(F32)
        for d in range(3):
            value = value + recv[p][offset(0) + d].astype(F32)
        return value

    wide_loop((4, 5), 512, pack_from(gu))
    tall_loop(pack_from(gd))
    for p in LATER:
        reduce_start(p)

    for copy in spread_fwd:
        copy.wait_recv()
    ones = jnp.where(lax.broadcasted_iota(jnp.int32, (64, 64), 1) < 2, 1.0, 0.0).astype(BF16)
    for t in range(32):
        part = ys[table[32 + t]]
        rows = slice(64 * t, 64 * t + 64)
        qb[rows, :] = part[:, 0:64]
        kb[rows, :] = part[:, 64:128]
        vb[rows, :] = jnp.concatenate([part[:, 128:192], ones], axis=1)
        db[rows, :] = part[:, 192:256]
    kt_b[...] = jnp.transpose(kb[...].astype(F32)).astype(BF16)
    vt_b[...] = jnp.transpose(vb[:, 0:64].astype(F32)).astype(BF16)

    def tile(j):
        low, width = 512 * j, 512 * (j + 1)
        turn_off = 1 - core if j % 2 else core
        row = low + 256 * turn_off
        rows = pl.ds(pl.multiple_of(row, 256), 256)
        queries = qb[rows, :].astype(F32) * 0.125
        q_t = jnp.transpose(queries).astype(BF16)
        do_t = jnp.transpose(db[rows, :].astype(F32))
        at_k = low + lax.broadcasted_iota(jnp.int32, (512, 256), 0)
        at_q = row + lax.broadcasted_iota(jnp.int32, (512, 256), 1)
        near = jnp.where(at_q >= at_k, nn(kb[low:width, :], q_t), -1e30)
        top = jnp.max(near, axis=0, keepdims=True)
        if j:
            away = nn(kb[0:low, :], q_t)
            top = jnp.maximum(top, jnp.max(away, axis=0, keepdims=True))
        near = jnp.exp(near - top)
        total = jnp.sum(near, axis=0, keepdims=True)
        probs = near.astype(BF16)
        if j:
            away = jnp.exp(away - top)
            total = total + jnp.sum(away, axis=0, keepdims=True)
            probs = jnp.concatenate([away.astype(BF16), probs], axis=0)
        scale = 1.0 / total
        att_t = nn(vt_b[:, 0:width], probs) * scale
        delta = jnp.sum(do_t * att_t, axis=0, keepdims=True) * scale
        do_t = do_t * scale
        high = delta.astype(BF16).astype(F32)
        tail = lax.broadcasted_iota(jnp.int32, (8, 256), 0)
        tail = jnp.where(tail == 0, -high, jnp.where(tail == 1, high - delta, 0.0))
        right = jnp.concatenate([do_t, tail, jnp.zeros((56, 256), F32)], axis=0).astype(BF16)
        d_s = (probs.astype(F32) * nn(vb[0:width, :], right)).astype(BF16)
        blocks = pl.ds(8 * j + 4 * turn_off, 4)
        blank = pl.ds(8 * j + 4 * (1 - turn_off), 4)
        att_b[blocks] = jnp.transpose(att_t).reshape(4, 64, 64)
        dq_b[blocks] = jnp.transpose(nn(kt_b[:, 0:width], d_s) * 0.125).reshape(4, 64, 64)
        att_b[blank] = jnp.zeros((4, 64, 64), F32)
        dq_b[blank] = jnp.zeros((4, 64, 64), F32)
        d_k = nn(d_s, queries.astype(BF16)).reshape(8 * (j + 1), 64, 64)
        d_v = nn(probs, jnp.transpose(do_t).astype(BF16)).reshape(8 * (j + 1), 64, 64)
        if j == 3:
            dk_b[...] = d_k
            dv_b[...] = d_v
        else:
            dk_b[0 : 8 * (j + 1)] += d_k
            dv_b[0 : 8 * (j + 1)] += d_v

    tile(3)
    for p in LATER:
        reduce_step(p, 2)
    for j in (2, 1, 0):
        tile(j)
    for i in range(32):
        t = table[i]
        zs[i] = jnp.concatenate([att_b[t], dq_b[t], dk_b[t], dv_b[t]], axis=1).astype(BF16)

    order = (1, 2, 3, 4, 5, 6, 7, 0)
    halves, collect = {}, []
    for delta in order:
        m, _ = head_at[delta]
        halves[delta] = send(
            zs.at[spot(1 - core, m)], crecv.at[m], cfs.at[delta], cfr.at[delta], sibling
        )
    started += list(halves.values())
    mlp_s[...] = nn(g_s[...], wd[...])
    for delta in order:
        m, peer = head_at[delta]
        halves[delta].wait_recv()
        ctotal[m] = zs[spot(core, m)] + crecv[m]
        if delta:
            collect.append(
                send(ctotal.at[m], back.at[me], cos_.at[delta - 1], cor_.at[delta - 1], peer)
            )
        else:
            back[me] = ctotal[m]
    started += collect
    for p in LATER:
        reduce_step(p, 1)
    dh2_s[...] = nt(dup_s[...], wu[...])
    dh2 = dh2_s[...]
    gvec[2:3, 0:512] = jnp.sum(dh2 * xhat[...], axis=0, keepdims=True)
    gvec[3:4, 0:512] = jnp.sum(dh2, axis=0, keepdims=True)
    gvec[6:7, 0:512] = jnp.sum(dy.astype(F32), axis=0, keepdims=True)
    for copy in collect:
        copy.wait_recv()

    def whole(i):
        return jnp.concatenate(
            [
                jnp.concatenate(
                    [back[h, 0, :, 64 * i : 64 * i + 64], back[h, 1, :, 64 * i : 64 * i + 64]],
                    axis=0,
                )
                for h in range(8)
            ],
            axis=1,
        )

    dqkv_s[:, 0:512] = turn(whole(1).astype(F32), -1.0).astype(BF16)
    dqkv_s[:, 512:1024] = turn(whole(2).astype(F32), -1.0).astype(BF16)
    dqkv_s[:, 1024:1536] = whole(3)
    mixed = whole(0)
    ga[:, 1536:2048] = tn(mixed, dy).astype(BF16)
    for t in range(3):
        ga[:, 512 * t : 512 * (t + 1)] = tn(
            h1_s[...], dqkv_s[:, 512 * t : 512 * (t + 1)]
        ).astype(BF16)
    wide_loop(FIRST, 0, pack_from(ga))
    for p in FIRST:
        reduce_start(p)
    for p in LATER:
        reduce_step(p, 0)
    dh1 = nt(dqkv_s[...], wa[:, 0:1536])
    gvec[0:1, 0:512] = jnp.sum(dh1 * xhat[...], axis=0, keepdims=True)
    gvec[1:2, 0:512] = jnp.sum(dh1, axis=0, keepdims=True)
    gvec[4:5, 0:1024] = jnp.sum(dqkv_s[:, 0:1024].astype(F32), axis=0, keepdims=True)
    gvec[5:6, 0:512] = jnp.sum(dqkv_s[:, 1024:1536].astype(F32), axis=0, keepdims=True)
    spread_out = jnp.zeros((128, 128), F32)
    left = 0
    for i, (n, off) in enumerate(SECTIONS_OUT):
        cols = slice(left, left + 128 * n)
        left += 128 * n
        value = gvec[i : i + 1, 0 : 128 * n]
        high = value.astype(BF16)
        low = (value - high.astype(F32)).astype(BF16)
        pick, own = pick_out[:, cols], own_out[:, cols]
        spread_out = spread_out + nt(own * high, pick) + nt(own * low, pick)
    gmat[...] = spread_out
    grads[SMALL][...] = jnp.zeros_like(grads[SMALL])

    def small_grads(row, carry):
        for t in range(4):
            where, c = place_of(row, t)
            grads[SMALL][c, slot_of(SMALL, where), 0:1, :] = gmat[pl.ds(row * 4 + t, 1), :]
        return carry

    lax.fori_loop(0, 32, small_grads, 0)
    reduce_start(SMALL)
    for p in FIRST:
        reduce_step(p, 2)
    reduce_step(SMALL, 2)
    d_norm = dh1 * vecs[0:1, 0:512] + dh2_s[...] * vecs[2:3, 0:512]
    normed = xhat[...]
    d_x = d_norm - jnp.mean(d_norm, axis=1, keepdims=True)
    d_x = d_x - normed * jnp.mean(d_norm * normed, axis=1, keepdims=True)
    ingrad_ref[0] = dy.astype(F32) + d_x * inv_s[:, 0:1]
    result = hid[0].astype(F32) + nn(mixed, wa[:, 1536:2048]) + mlp_s[...] + vecs[5:6, 0:512]
    out_ref[0] = result.astype(BF16)
    for p in LATER:
        value = reduce_end(p)
        if p < 6:
            asm2[:, LEFT[p] : LEFT[p] + COLS[p]] = value
        else:
            gdown_ref[:, LEFT[p] : LEFT[p] + COLS[p]] = value
    for k in (1, 0):
        for p in FIRST + (SMALL,):
            reduce_step(p, k)
    for p in FIRST:
        asm2[:, LEFT[p] : LEFT[p] + COLS[p]] = reduce_end(p)
    gsmall_ref[...] = reduce_end(SMALL)
    squad2[...] = jnp.zeros_like(squad2)
    for t in range(4):
        squad2[t, 0:4, :] = asm2[4 * t : 4 * t + 4, :]
    quad = []
    for peer, delta in quad_peers:
        quad.append(
            send(
                squad2.at[quad_index(delta)], rquad2.at[q], q2s.at[delta - 1], q2r.at[delta - 1],
                peer,
            )
        )
    started += quad
    rquad2[q] = squad2[q]
    for copy in quad:
        copy.wait_recv()
    for t in range(3):
        gqkv_ref[:, 512 * t : 512 * (t + 1)] = rquad2[t, 0:4, 0:512]
    gproj_ref[...] = rquad2[3, 0:4, 0:512]
    for t in range(4):
        gup_ref[:, 512 * t : 512 * (t + 1)] = rquad2[t, 0:4, 512:1024]
    for copy in started:
        copy.wait_send()


def run_block(*args):
    dma = pltpu.SemaphoreType.DMA
    scratch = [VMEM((2, 64) + tile, dtype) for tile, dtype in TILES] * 2
    scratch += [VMEM((128,) + tile, dtype) for tile, dtype in TILES]
    scratch += [VMEM((4, 8, 1024), F32)] * 4 + [VMEM((16, 1024), F32)] * 2
    scratch += [VMEM((512, 2048), BF16), VMEM((512, 2048), BF16), VMEM((2048, 512), BF16)] * 2
    scratch += [VMEM((128, 128), F32)] * 2
    scratch += [VMEM((8, 2, 64, 256), BF16), VMEM((32, 64, 256), BF16), VMEM((32, 64, 256), BF16)]
    scratch += [VMEM((8, 2, 64, 256), BF16)] * 3
    scratch += [VMEM((2048, 64), BF16)] * 2 + [VMEM((2048, 128), BF16), VMEM((2048, 64), BF16)]
    scratch += [VMEM((32, 64, 64), F32)] * 4
    scratch += [VMEM((128, 512), F32)] + [VMEM((128, 128), F32)] * 3 + [VMEM((8, 2048), F32)] * 2
    scratch += [VMEM((128, 512), BF16)] * 2 + [VMEM((128, 2048), BF16)] * 2
    scratch += [VMEM((128, 512), F32)] * 2 + [VMEM((128, 1536), BF16)]
    scratch += [dma((3,))] * 4 + [dma((N, 9))] * 2 + [dma((N, 4))] * 2 + [dma((N, 10))] * 2
    scratch += [dma((7,)), dma((7,)), dma((8,)), dma((8,))] * 2
    scratch += [VMEM((128, 6144), BF16)] * 4 + [VMEM((64, 2048), BF16)] * 2
    shape = jax.ShapeDtypeStruct
    return pl.pallas_call(
        block_kernel,
        out_shape=(
            shape((1, 128, 512), BF16), shape((1, 128, 512), F32), shape((4, 1536), F32),
            shape((4, 512), F32), shape((4, 2048), F32), shape((16, 512), F32), shape((8, 128), F32),
        ),
        in_specs=[pl.BlockSpec(memory_space=pltpu.SMEM)] + [pl.BlockSpec(memory_space=VMEM)] * 9,
        out_specs=[pl.BlockSpec(memory_space=VMEM)] * 7,
        scratch_shapes=scratch,
        compiler_params=pltpu.CompilerParams(
            collective_id=0, has_side_effects=True, vmem_limit_bytes=LIMIT
        ),
    )(*args)


def finish_kernel(*refs):
    for src, dst in zip(refs[:6], refs[7:13]):
        dst[...] = src[...]
    row = refs[6][0:1, :]
    for (n, off), dst in zip(SECTIONS_OUT, refs[13:]):
        dst[...] = row[:, off : off + n]


def finish(*parts):
    shape = jax.ShapeDtypeStruct
    return pl.pallas_call(
        finish_kernel,
        out_shape=tuple(shape(part.shape, part.dtype) for part in parts[:6])
        + tuple(shape((1, n), F32) for n, _ in SECTIONS_OUT),
        in_specs=[pl.BlockSpec(memory_space=VMEM)] * 7,
        out_specs=[pl.BlockSpec(memory_space=VMEM)] * 14,
    )(*parts)


def per_device(
    hidden_in, positions, block_order, norm1_gain, norm1_bias, norm2_gain, norm2_bias,
    qkv_weight, qkv_bias, attn_out_weight, out_bias, up_weight, up_bias, down_weight, out_grad,
):
    small = jnp.concatenate(
        [norm1_gain, norm1_bias, norm2_gain, norm2_bias, qkv_bias, out_bias, up_bias]
    ).astype(F32)
    small = jnp.pad(small[None], ((0, 7), (0, 80)))
    held = block_order.reshape(8, 2, 2).transpose(1, 0, 2).reshape(32)
    ids = jnp.arange(32, dtype=jnp.int32)
    inverse = jnp.sum(jnp.where(held[:, None] == ids[None, :], ids[:, None], 0), axis=0)
    table = jnp.concatenate([held, inverse])
    freqs = 10000.0 ** (-np.arange(8, dtype=np.float32) * np.float32(2.0) / np.float32(16))
    lanes = np.concatenate([freqs, freqs, np.zeros(48)]).astype(np.float32)
    freq = jnp.asarray(np.concatenate([lanes, lanes])[None])
    parts = run_block(
        table, hidden_in, out_grad, positions, freq, small,
        qkv_weight, attn_out_weight, up_weight, down_weight,
    )
    done = finish(*parts)
    block_out, input_grad, g_qkv, g_proj, g_up, g_down = done[:6]
    n1g, n1b, n2g, n2b, qk, val, out, up = (item.reshape(-1) for item in done[6:])
    return (
        block_out, input_grad, n1g, n1b, n2g, n2b, g_qkv, qk, val, g_proj, out, g_up, up, g_down,
    )


def solution(mesh):
    both = ("dp", "ctx")
    rows, vec, mat = P("dp", "ctx", None), P(both), P(both, None)
    return jax.shard_map(
        per_device,
        mesh=mesh,
        in_specs=(
            rows, P("dp", "ctx"), P(), vec, vec, vec, vec, mat, vec, mat, vec, mat, vec, mat, rows,
        ),
        out_specs=(
            rows, rows, vec, vec, vec, vec, mat, vec, vec, mat, vec, mat, vec, mat,
        ),
        check_vma=False,
    )
```

```python
import jax
import jax.numpy as jnp
import numpy as np
from jax import lax
from jax.experimental import pallas as pl
from jax.experimental.pallas import tpu as pltpu
from jax.sharding import PartitionSpec as P

EPS = 1e-05
MESH = pl.DeviceIdType.MESH
F32 = jnp.float32
BF16 = jnp.bfloat16
VMEM = pltpu.VMEM
LIMIT = 60 * 1024 * 1024

ORDERS = ((0, 1, 2), (1, 2, 0), (2, 0, 1))
ORDER_OF = (0, 1, 2, 1, 0, 1, 1, 2)
COLS = (256, 128, 128, 128, 256, 256, 128, 384)
LEFT = (0, 256, 384, 0, 512, 768, 0, 128)
N = 8
FIRST, SMALL, LATER = (0, 1, 2), 3, (4, 5, 6, 7)
TILES = [((8, 128), F32) if p == SMALL else ((16, COLS[p]), BF16) for p in range(N)]
SECTIONS_IN = ((4, 0), (4, 4), (4, 8), (4, 12), (12, 16), (4, 28), (16, 32))
SECTIONS_OUT = ((4, 0), (4, 4), (4, 8), (4, 12), (8, 16), (4, 24), (4, 28), (16, 32))


def device_of(x, y, z, core):
    return (z * 2 + lax.rem(x, 2), y * 4 + lax.div(x, 2) * 2 + core)


def slot_of(p, at):
    return sum(at[axis] * 4**k for k, axis in enumerate(ORDERS[ORDER_OF[p]]))


def moved(at, axis, delta):
    at = list(at)
    at[axis] = lax.rem(at[axis] + delta, 4)
    return at


def send(src, dst, ssem, rsem, peer):
    copy = pltpu.make_async_remote_copy(
        src_ref=src, dst_ref=dst, send_sem=ssem, recv_sem=rsem, device_id=peer, device_id_type=MESH
    )
    copy.start()
    return copy


def nt(a, b):
    return lax.dot_general(a, b, (((1,), (1,)), ((), ())), preferred_element_type=F32)


def nn(a, b):
    return lax.dot_general(a, b, (((1,), (0,)), ((), ())), preferred_element_type=F32)


def tn(a, b):
    return lax.dot_general(a, b, (((0,), (0,)), ((), ())), preferred_element_type=F32)


def selectors(n, off):
    cols = lax.broadcasted_iota(jnp.int32, (1, 128 * n), 1)
    owner = ((cols.astype(F32) + 0.5) * (1.0 / n)).astype(jnp.int32)
    lane = cols - owner * n + off
    rows = lax.broadcasted_iota(jnp.int32, (128, 128 * n), 0)
    pick = jnp.where(rows == lane, 1.0, 0.0).astype(BF16)
    return pick, jnp.where(rows == owner, 1.0, 0.0).astype(BF16)


def swap_halves(u):
    lane = lax.broadcasted_iota(jnp.int32, u.shape, 1)
    lane = lane - 64 * (lane >= 64).astype(jnp.int32)
    return jnp.where(lane < 8, pltpu.roll(u, 120, 1), pltpu.roll(u, 8, 1))


def block_kernel(
    table, hid, dy_ref, pos, freq, small, w_qkv, w_proj, w_upper, w_lower,
    out_ref, ingrad_ref, gqkv_ref, gproj_ref, gup_ref, gdown_ref, gsmall_ref,
    *rest,
):
    rest = list(rest)

    def take(count):
        got = rest[:count]
        del rest[:count]
        return got

    bufs, grads, recv = take(N), take(N), take(N)
    squad, rquad, squad2, rquad2, asm, asm2 = take(6)
    wa, wu, wd, ga, gu, gd, smat, gmat = take(8)
    xs, ys, zs, crecv, ctotal, back = take(6)
    qb, kb, vb, db, att_b, dq_b, dk_b, dv_b = take(8)
    xhat, inv_s, cos_s, sin_s, vecs, gvec, h1_s, h2_s, g_s, dup_s, mlp_s, dh2_s, dqkv_s = take(13)
    qs, qr, q2s, q2r, ags, agr, fws, fwr, rss, rsr, sps, spr, sfs, sfr = take(14)
    cos_, cor_, cfs, cfr = take(4)
    pick_in, own_in, pick_out, own_out, kt_b, vt_b = take(6)

    dp, ctx = lax.axis_index("dp"), lax.axis_index("ctx")
    core = lax.rem(ctx, 2)
    at = [
        lax.rem(lax.div(ctx, 2), 2) * 2 + lax.rem(dp, 2), lax.div(ctx, 4), lax.div(dp, 2)
    ]
    sibling = device_of(*at, 1 - core)
    q = lax.rem(ctx, 4)
    axis_peers = [
        [device_of(*moved(at, axis, delta), core) for delta in (1, 2, 3)] for axis in range(3)
    ]
    far = moved(at, 0, 2)
    far_cross = device_of(*far, 1 - core)
    head_at = []
    for delta in range(8):
        place = moved(far if delta % 2 else at, 1, delta // 2)
        head_at.append((place[1] * 2 + lax.div(place[0], 2), device_of(*place, core)))
    me = head_at[0][0]
    quad_peers = [(sibling, 1), (head_at[1][1], 2), (far_cross, 3)]

    def quad_index(delta):
        core_t = 1 - core if delta % 2 else core
        hi = lax.div(at[0], 2)
        return (1 - hi if delta // 2 else hi) * 2 + core_t

    everyone = [sibling, far_cross] + sum(axis_peers, [])
    everyone += [head_at[delta][1] for delta in (3, 5, 7)]
    barrier = pltpu.get_barrier_semaphore()
    for peer in everyone:
        pl.semaphore_signal(barrier, inc=1, device_id=peer, device_id_type=MESH)

    slots = [slot_of(p, at) for p in range(N)]
    started = []

    squad[...] = jnp.zeros_like(squad)
    qkv_rows = w_qkv[...].astype(F32)
    up_rows = w_upper[...].astype(F32)
    for t in range(3):
        squad[t, 0:4, 0:512] = qkv_rows[:, 512 * t : 512 * (t + 1)]
    squad[3, 0:4, 0:512] = w_proj[...].astype(F32)
    for t in range(4):
        squad[t, 0:4, 512:1024] = up_rows[:, 512 * t : 512 * (t + 1)]
    for p in (6, 7):
        bufs[p][core, slots[p]] = w_lower[:, LEFT[p] : LEFT[p] + COLS[p]]
    bufs[SMALL][core, slots[SMALL]] = small[...]
    x = hid[0].astype(F32)
    center = x - jnp.mean(x, axis=1, keepdims=True)
    inv = lax.rsqrt(jnp.mean(center * center, axis=1, keepdims=True) + EPS)
    xhat[...] = center * inv
    inv_s[...] = jnp.broadcast_to(inv, (128, 128))
    places = jnp.transpose(jnp.broadcast_to(pos[...].astype(F32), (128, 128)))
    angle = places * freq[...]
    lane = lax.broadcasted_iota(jnp.int32, (128, 128), 1)
    lane = lane - 64 * (lane >= 64).astype(jnp.int32)
    sine = jnp.sin(angle)
    cos_s[...] = jnp.cos(angle)
    sin_s[...] = jnp.where(lane < 8, -sine, sine)
    pl.semaphore_wait(barrier, len(everyone))

    quad = []
    for peer, delta in quad_peers:
        quad.append(
            send(squad.at[quad_index(delta)], rquad.at[q], qs.at[delta - 1], qr.at[delta - 1], peer)
        )
    started += quad
    rquad[q] = squad[q]
    hops, fwd = {}, {}

    def block(p, k):
        size = 4**k
        return lax.div(slots[p], size) * size, size

    def gather_send(p, k):
        base, size = block(p, k)
        axis = ORDERS[ORDER_OF[p]][k]
        part = bufs[p].at[core, pl.ds(base, size)]
        for d in range(3):
            hops[p, k, d] = send(
                part, part, ags.at[p, 3 * k + d], agr.at[p, 3 * k + d], axis_peers[axis][d]
            )
            started.append(hops[p, k, d])
        if k == 2:
            fwd[p, 3] = send(part, part, fws.at[p, 3], fwr.at[p, 3], sibling)
            started.append(fwd[p, 3])

    def gather_wait(p, k):
        for d in range(3):
            hops[p, k, d].wait_recv()

    def gather_forward(p):
        axis = ORDERS[ORDER_OF[p]][2]
        for d in range(3):
            hops[p, 2, d].wait_recv()
            base = lax.rem(at[axis] + 3 - d, 4) * 16
            part = bufs[p].at[core, pl.ds(base, 16)]
            fwd[p, d] = send(part, part, fws.at[p, d], fwr.at[p, d], sibling)
            started.append(fwd[p, d])

    def gather_done(p):
        for d in range(4):
            fwd[p, d].wait_recv()

    for p in (SMALL, 6, 7):
        gather_send(p, 0)
    for copy in quad:
        copy.wait_recv()
    for t in range(4):
        asm[4 * t : 4 * t + 4, :] = rquad[t, 0:4, :]
    for p in (0, 1, 2, 4, 5):
        bufs[p][core, slots[p]] = asm[:, LEFT[p] : LEFT[p] + COLS[p]].astype(BF16)
        gather_send(p, 0)

    def build(sections, picks, owns):
        left = 0
        for n, off in sections:
            pick, own = selectors(n, off)
            picks[:, left : left + 128 * n] = pick
            owns[:, left : left + 128 * n] = own
            left += 128 * n

    build(SECTIONS_IN, pick_in, own_in)
    for p in (SMALL,) + FIRST + LATER:
        gather_wait(p, 0)
        gather_send(p, 1)
    build(SECTIONS_OUT, pick_out, own_out)
    for p in (SMALL,) + FIRST:
        gather_wait(p, 1)
        gather_send(p, 2)
    for p in (SMALL,) + FIRST:
        gather_forward(p)
    for p in LATER:
        gather_wait(p, 1)
        gather_send(p, 2)

    def place_of(row, t):
        x_lo = lax.rem(lax.div(row, 4), 2)
        return [(t // 2) * 2 + x_lo, lax.rem(row, 4), lax.div(row, 8)], t % 2

    def wide_loop(streams, left0, store):
        def body(row, carry):
            rows = pl.ds(pl.multiple_of(row * 16, 16), 16)
            for t in range(4):
                where, c = place_of(row, t)
                for p in streams:
                    left = 512 * t + LEFT[p] - left0
                    store(p, c, slot_of(p, where), rows, left)
            return carry

        lax.fori_loop(0, 32, body, 0)

    def tall_loop(store):
        def body(row, carry):
            for t in range(4):
                where, c = place_of(row, t)
                rows = pl.ds(pl.multiple_of(row * 64 + t * 16, 16), 16)
                for p in (6, 7):
                    store(p, c, slot_of(p, where), rows, LEFT[p])
            return carry

        lax.fori_loop(0, 32, body, 0)

    def unpack_to(dst):
        def store(p, c, slot, rows, left):
            dst[rows, left : left + COLS[p]] = bufs[p][c, slot]

        return store

    def pack_from(src):
        def store(p, c, slot, rows, left):
            grads[p][c, slot] = src[rows, left : left + COLS[p]]

        return store

    gather_done(SMALL)

    def small_rows(row, carry):
        for t in range(4):
            where, c = place_of(row, t)
            smat[pl.ds(row * 4 + t, 1), :] = bufs[SMALL][c, slot_of(SMALL, where), 0:1, :]
        return carry

    lax.fori_loop(0, 32, small_rows, 0)
    tiles = smat[...].astype(BF16)
    left = 0
    for i, (n, off) in enumerate(SECTIONS_IN):
        cols = slice(left, left + 128 * n)
        left += 128 * n
        vecs[i : i + 1, 0 : 128 * n] = jnp.sum(
            own_in[:, cols].astype(F32) * nn(tiles, pick_in[:, cols]), axis=0, keepdims=True
        )
    normed = xhat[...]
    h1_s[...] = (normed * vecs[0:1, 0:512] + vecs[1:2, 0:512]).astype(BF16)
    h2_s[...] = (normed * vecs[2:3, 0:512] + vecs[3:4, 0:512]).astype(BF16)
    for p in FIRST:
        gather_done(p)
    wide_loop(FIRST, 0, unpack_to(wa))

    dy = dy_ref[0]
    parts = [nn(h1_s[...], wa[:, 512 * i : 512 * (i + 1)]) for i in range(3)]
    parts = [parts[i] + vecs[4:5, 512 * i : 512 * (i + 1)] for i in range(3)]
    cos_t, sin_t = cos_s[...], sin_s[...]

    def turn(u, sign):
        return jnp.concatenate(
            [
                u[:, c : c + 128] * cos_t + swap_halves(u[:, c : c + 128]) * (sin_t * sign)
                for c in range(0, 512, 128)
            ],
            axis=1,
        )

    sent = [turn(parts[0], 1.0), turn(parts[1], 1.0), parts[2], nt(dy, wa[:, 1536:2048])]
    sent = [item.astype(BF16) for item in sent]
    for h in range(8):
        piece = jnp.concatenate([item[:, 64 * h : 64 * h + 64] for item in sent], axis=1)
        xs[h, 0] = piece[0:64]
        xs[h, 1] = piece[64:128]
    spread, spread_fwd = [], []

    def spot(c, m):
        return pl.ds(c * 16 + m * 2, 2)

    for delta in range(1, 8):
        m, peer = head_at[delta]
        spread.append(
            send(xs.at[m], ys.at[spot(core, me)], sps.at[delta - 1], spr.at[delta - 1], peer)
        )
    ys[spot(core, me)] = xs[me]
    mine = ys.at[spot(core, me)]
    spread_fwd.append(send(mine, mine, sfs.at[0], sfr.at[0], sibling))

    for p in LATER:
        gather_forward(p)
    for p in LATER:
        gather_done(p)
    wide_loop((4, 5), 512, unpack_to(wu))
    tall_loop(unpack_to(wd))

    def mlp(t):
        cols = slice(512 * t, 512 * (t + 1))
        up = nn(h2_s[...], wu[:, cols]) + vecs[6:7, cols]
        cdf = 0.5 * (1.0 + lax.erf(up * np.float32(0.5**0.5)))
        pdf = jnp.exp(-0.5 * up * up) * np.float32((2 * np.pi) ** -0.5)
        g = (up * cdf).astype(BF16)
        d_up = (nt(dy, wd[cols, :]) * (cdf + up * pdf)).astype(BF16)
        g_s[:, cols] = g
        dup_s[:, cols] = d_up
        gvec[7:8, cols] = jnp.sum(d_up.astype(F32), axis=0, keepdims=True)
        gu[:, cols] = tn(h2_s[...], d_up).astype(BF16)
        gd[cols, :] = tn(g, dy).astype(BF16)

    for t in range(4):
        mlp(t)
        if t == 1:
            for delta in range(1, 8):
                back_y = (4 - delta // 2) % 4
                m = head_at[back_y * 2 + delta % 2][0]
                spread[delta - 1].wait_recv()
                part = ys.at[spot(core, m)]
                spread_fwd.append(send(part, part, sfs.at[delta], sfr.at[delta], sibling))
    started += spread + spread_fwd

    adds = {}

    def reduce_start(p):
        adds[p, 3] = send(
            grads[p].at[1 - core], recv[p].at[pl.ds(0, 64)], rss.at[p, 9], rsr.at[p, 9], sibling
        )
        started.append(adds[p, 3])

    def offset(k):
        return 64 + {2: 0, 1: 48, 0: 60}[k]

    def reduce_step(p, k):
        if k == 2:
            adds[p, 3].wait_recv()
            total, others, base = 64, (0,), 0
        else:
            for d in range(3):
                adds[p, k + 1, d].wait_recv()
            base, total = block(p, k + 1)
            others = [offset(k + 1) + d * total for d in range(3)]
        unit = min(total, 8 if len(others) == 1 else 4)

        def body(i, carry):
            here = pl.ds(base + i * unit, unit)
            if len(others) == 1:
                grads[p][core, here] += recv[p][pl.ds(others[0] + i * unit, unit)]
                return carry
            value = grads[p][core, here].astype(F32)
            for other in others:
                value = value + recv[p][pl.ds(other + i * unit, unit)].astype(F32)
            grads[p][core, here] = value.astype(grads[p].dtype)
            return carry

        lax.fori_loop(0, total // unit, body, 0)
        axis = ORDERS[ORDER_OF[p]][k]
        size = 4**k
        own, _ = block(p, k)
        for d in range(3):
            there = lax.rem(at[axis] + d + 1, 4)
            part = grads[p].at[core, pl.ds(own + (there - at[axis]) * size, size)]
            adds[p, k, d] = send(
                part, recv[p].at[pl.ds(offset(k) + d * size, size)],
                rss.at[p, 3 * k + d], rsr.at[p, 3 * k + d], axis_peers[axis][d],
            )
            started.append(adds[p, k, d])

    def reduce_end(p):
        for d in range(3):
            adds[p, 0, d].wait_recv()
        value = grads[p][core, slots[p]].astype(F32)
        for d in range(3):
            value = value + recv[p][offset(0) + d].astype(F32)
        return value

    wide_loop((4, 5), 512, pack_from(gu))
    tall_loop(pack_from(gd))
    for p in LATER:
        reduce_start(p)

    for copy in spread_fwd:
        copy.wait_recv()
    ones = jnp.where(lax.broadcasted_iota(jnp.int32, (64, 64), 1) < 2, 1.0, 0.0).astype(BF16)
    for t in range(32):
        part = ys[table[32 + t]]
        rows = slice(64 * t, 64 * t + 64)
        qb[rows, :] = part[:, 0:64]
        kb[rows, :] = part[:, 64:128]
        vb[rows, :] = jnp.concatenate([part[:, 128:192], ones], axis=1)
        db[rows, :] = part[:, 192:256]
    kt_b[...] = jnp.transpose(kb[...].astype(F32)).astype(BF16)
    vt_b[...] = jnp.transpose(vb[:, 0:64].astype(F32)).astype(BF16)

    def tile(j):
        low, width = 512 * j, 512 * (j + 1)
        turn_off = 1 - core if j % 2 else core
        row = low + 256 * turn_off
        rows = pl.ds(pl.multiple_of(row, 256), 256)
        queries = qb[rows, :].astype(F32) * 0.125
        q_t = jnp.transpose(queries).astype(BF16)
        do_t = jnp.transpose(db[rows, :].astype(F32))
        at_k = low + lax.broadcasted_iota(jnp.int32, (512, 256), 0)
        at_q = row + lax.broadcasted_iota(jnp.int32, (512, 256), 1)
        near = jnp.where(at_q >= at_k, nn(kb[low:width, :], q_t), -1e30)
        top = jnp.max(near, axis=0, keepdims=True)
        if j:
            away = nn(kb[0:low, :], q_t)
            top = jnp.maximum(top, jnp.max(away, axis=0, keepdims=True))
        near = jnp.exp(near - top)
        total = jnp.sum(near, axis=0, keepdims=True)
        probs = near.astype(BF16)
        if j:
            away = jnp.exp(away - top)
            total = total + jnp.sum(away, axis=0, keepdims=True)
            probs = jnp.concatenate([away.astype(BF16), probs], axis=0)
        scale = 1.0 / total
        att_t = nn(vt_b[:, 0:width], probs) * scale
        do_t = (do_t * scale).astype(BF16).astype(F32)
        delta = jnp.sum(do_t * att_t, axis=0, keepdims=True)
        high = delta.astype(BF16).astype(F32)
        tail = lax.broadcasted_iota(jnp.int32, (8, 256), 0)
        tail = jnp.where(tail == 0, -high, jnp.where(tail == 1, high - delta, 0.0))
        right = jnp.concatenate([do_t, tail, jnp.zeros((56, 256), F32)], axis=0).astype(BF16)
        d_s = (probs.astype(F32) * nn(vb[0:width, :], right)).astype(BF16)
        blocks = pl.ds(8 * j + 4 * turn_off, 4)
        blank = pl.ds(8 * j + 4 * (1 - turn_off), 4)
        att_b[blocks] = jnp.transpose(att_t).reshape(4, 64, 64)
        dq_b[blocks] = jnp.transpose(nn(kt_b[:, 0:width], d_s) * 0.125).reshape(4, 64, 64)
        att_b[blank] = jnp.zeros((4, 64, 64), F32)
        dq_b[blank] = jnp.zeros((4, 64, 64), F32)
        d_k = nn(d_s, queries.astype(BF16)).reshape(8 * (j + 1), 64, 64)
        d_v = nn(probs, jnp.transpose(do_t).astype(BF16)).reshape(8 * (j + 1), 64, 64)
        if j == 3:
            dk_b[...] = d_k
            dv_b[...] = d_v
        else:
            dk_b[0 : 8 * (j + 1)] += d_k
            dv_b[0 : 8 * (j + 1)] += d_v

    tile(3)
    for p in LATER:
        reduce_step(p, 2)
    for j in (2, 1, 0):
        tile(j)
    for i in range(32):
        t = table[i]
        zs[i] = jnp.concatenate([att_b[t], dq_b[t], dk_b[t], dv_b[t]], axis=1).astype(BF16)

    order = (1, 2, 3, 4, 5, 6, 7, 0)
    halves, collect = {}, []
    for delta in order:
        m, _ = head_at[delta]
        halves[delta] = send(
            zs.at[spot(1 - core, m)], crecv.at[m], cfs.at[delta], cfr.at[delta], sibling
        )
    started += list(halves.values())
    mlp_s[...] = nn(g_s[...], wd[...])
    for delta in order:
        m, peer = head_at[delta]
        halves[delta].wait_recv()
        ctotal[m] = zs[spot(core, m)] + crecv[m]
        if delta:
            collect.append(
                send(ctotal.at[m], back.at[me], cos_.at[delta - 1], cor_.at[delta - 1], peer)
            )
        else:
            back[me] = ctotal[m]
    started += collect
    for p in LATER:
        reduce_step(p, 1)
    dh2_s[...] = nt(dup_s[...], wu[...])
    dh2 = dh2_s[...]
    gvec[2:3, 0:512] = jnp.sum(dh2 * xhat[...], axis=0, keepdims=True)
    gvec[3:4, 0:512] = jnp.sum(dh2, axis=0, keepdims=True)
    gvec[6:7, 0:512] = jnp.sum(dy.astype(F32), axis=0, keepdims=True)
    for copy in collect:
        copy.wait_recv()

    def whole(i):
        return jnp.concatenate(
            [
                jnp.concatenate(
                    [back[h, 0, :, 64 * i : 64 * i + 64], back[h, 1, :, 64 * i : 64 * i + 64]],
                    axis=0,
                )
                for h in range(8)
            ],
            axis=1,
        )

    dqkv_s[:, 0:512] = turn(whole(1).astype(F32), -1.0).astype(BF16)
    dqkv_s[:, 512:1024] = turn(whole(2).astype(F32), -1.0).astype(BF16)
    dqkv_s[:, 1024:1536] = whole(3)
    mixed = whole(0)
    ga[:, 1536:2048] = tn(mixed, dy).astype(BF16)
    for t in range(3):
        ga[:, 512 * t : 512 * (t + 1)] = tn(
            h1_s[...], dqkv_s[:, 512 * t : 512 * (t + 1)]
        ).astype(BF16)
    wide_loop(FIRST, 0, pack_from(ga))
    for p in FIRST:
        reduce_start(p)
    dh1 = nt(dqkv_s[...], wa[:, 0:1536])
    gvec[0:1, 0:512] = jnp.sum(dh1 * xhat[...], axis=0, keepdims=True)
    gvec[1:2, 0:512] = jnp.sum(dh1, axis=0, keepdims=True)
    gvec[4:5, 0:1024] = jnp.sum(dqkv_s[:, 0:1024].astype(F32), axis=0, keepdims=True)
    gvec[5:6, 0:512] = jnp.sum(dqkv_s[:, 1024:1536].astype(F32), axis=0, keepdims=True)
    for p in FIRST:
        reduce_step(p, 2)
    spread_out = jnp.zeros((128, 128), F32)
    left = 0
    for i, (n, off) in enumerate(SECTIONS_OUT):
        cols = slice(left, left + 128 * n)
        left += 128 * n
        value = gvec[i : i + 1, 0 : 128 * n]
        high = value.astype(BF16)
        low = (value - high.astype(F32)).astype(BF16)
        pick, own = pick_out[:, cols], own_out[:, cols]
        spread_out = spread_out + nt(own * high, pick) + nt(own * low, pick)
    gmat[...] = spread_out
    grads[SMALL][...] = jnp.zeros_like(grads[SMALL])

    def small_grads(row, carry):
        for t in range(4):
            where, c = place_of(row, t)
            grads[SMALL][c, slot_of(SMALL, where), 0:1, :] = gmat[pl.ds(row * 4 + t, 1), :]
        return carry

    lax.fori_loop(0, 32, small_grads, 0)
    reduce_start(SMALL)
    result = hid[0].astype(F32) + nn(mixed, wa[:, 1536:2048]) + mlp_s[...] + vecs[5:6, 0:512]
    out_ref[0] = result.astype(BF16)
    reduce_step(SMALL, 2)
    d_norm = dh1 * vecs[0:1, 0:512] + dh2_s[...] * vecs[2:3, 0:512]
    normed = xhat[...]
    d_x = d_norm - jnp.mean(d_norm, axis=1, keepdims=True)
    d_x = d_x - normed * jnp.mean(d_norm * normed, axis=1, keepdims=True)
    ingrad_ref[0] = dy.astype(F32) + d_x * inv_s[:, 0:1]
    for p in LATER:
        reduce_step(p, 0)
    for p in FIRST + (SMALL,):
        reduce_step(p, 1)
    for p in LATER:
        value = reduce_end(p)
        if p < 6:
            asm2[:, LEFT[p] : LEFT[p] + COLS[p]] = value
        else:
            gdown_ref[:, LEFT[p] : LEFT[p] + COLS[p]] = value
    for p in FIRST + (SMALL,):
        reduce_step(p, 0)
    for p in FIRST:
        asm2[:, LEFT[p] : LEFT[p] + COLS[p]] = reduce_end(p)
    gsmall_ref[...] = reduce_end(SMALL)
    squad2[...] = jnp.zeros_like(squad2)
    for t in range(4):
        squad2[t, 0:4, :] = asm2[4 * t : 4 * t + 4, :]
    quad = []
    for peer, delta in quad_peers:
        quad.append(
            send(
                squad2.at[quad_index(delta)], rquad2.at[q], q2s.at[delta - 1], q2r.at[delta - 1],
                peer,
            )
        )
    started += quad
    rquad2[q] = squad2[q]
    for copy in quad:
        copy.wait_recv()
    for t in range(3):
        gqkv_ref[:, 512 * t : 512 * (t + 1)] = rquad2[t, 0:4, 0:512]
    gproj_ref[...] = rquad2[3, 0:4, 0:512]
    for t in range(4):
        gup_ref[:, 512 * t : 512 * (t + 1)] = rquad2[t, 0:4, 512:1024]
    for copy in started:
        copy.wait_send()


def run_block(*args):
    dma = pltpu.SemaphoreType.DMA
    scratch = [VMEM((2, 64) + tile, dtype) for tile, dtype in TILES] * 2
    scratch += [VMEM((128,) + tile, dtype) for tile, dtype in TILES]
    scratch += [VMEM((4, 8, 1024), F32)] * 4 + [VMEM((16, 1024), F32)] * 2
    scratch += [VMEM((512, 2048), BF16), VMEM((512, 2048), BF16), VMEM((2048, 512), BF16)] * 2
    scratch += [VMEM((128, 128), F32)] * 2
    scratch += [VMEM((8, 2, 64, 256), BF16), VMEM((32, 64, 256), BF16), VMEM((32, 64, 256), BF16)]
    scratch += [VMEM((8, 2, 64, 256), BF16)] * 3
    scratch += [VMEM((2048, 64), BF16)] * 2 + [VMEM((2048, 128), BF16), VMEM((2048, 64), BF16)]
    scratch += [VMEM((32, 64, 64), F32)] * 4
    scratch += [VMEM((128, 512), F32)] + [VMEM((128, 128), F32)] * 3 + [VMEM((8, 2048), F32)] * 2
    scratch += [VMEM((128, 512), BF16)] * 2 + [VMEM((128, 2048), BF16)] * 2
    scratch += [VMEM((128, 512), F32)] * 2 + [VMEM((128, 1536), BF16)]
    scratch += [dma((3,))] * 4 + [dma((N, 9))] * 2 + [dma((N, 4))] * 2 + [dma((N, 10))] * 2
    scratch += [dma((7,)), dma((7,)), dma((8,)), dma((8,))] * 2
    scratch += [VMEM((128, 6144), BF16)] * 4 + [VMEM((64, 2048), BF16)] * 2
    shape = jax.ShapeDtypeStruct
    return pl.pallas_call(
        block_kernel,
        out_shape=(
            shape((1, 128, 512), BF16), shape((1, 128, 512), F32), shape((4, 1536), F32),
            shape((4, 512), F32), shape((4, 2048), F32), shape((16, 512), F32), shape((8, 128), F32),
        ),
        in_specs=[pl.BlockSpec(memory_space=pltpu.SMEM)] + [pl.BlockSpec(memory_space=VMEM)] * 9,
        out_specs=[pl.BlockSpec(memory_space=VMEM)] * 7,
        scratch_shapes=scratch,
        compiler_params=pltpu.CompilerParams(
            collective_id=0, has_side_effects=True, vmem_limit_bytes=LIMIT
        ),
    )(*args)


def finish_kernel(*refs):
    for src, dst in zip(refs[:6], refs[7:13]):
        dst[...] = src[...]
    row = refs[6][0:1, :]
    for (n, off), dst in zip(SECTIONS_OUT, refs[13:]):
        dst[...] = row[:, off : off + n]


def finish(*parts):
    shape = jax.ShapeDtypeStruct
    return pl.pallas_call(
        finish_kernel,
        out_shape=tuple(shape(part.shape, part.dtype) for part in parts[:6])
        + tuple(shape((1, n), F32) for n, _ in SECTIONS_OUT),
        in_specs=[pl.BlockSpec(memory_space=VMEM)] * 7,
        out_specs=[pl.BlockSpec(memory_space=VMEM)] * 14,
    )(*parts)


def per_device(
    hidden_in, positions, block_order, norm1_gain, norm1_bias, norm2_gain, norm2_bias,
    qkv_weight, qkv_bias, attn_out_weight, out_bias, up_weight, up_bias, down_weight, out_grad,
):
    small = jnp.concatenate(
        [norm1_gain, norm1_bias, norm2_gain, norm2_bias, qkv_bias, out_bias, up_bias]
    ).astype(F32)
    small = jnp.pad(small[None], ((0, 7), (0, 80)))
    held = block_order.reshape(8, 2, 2).transpose(1, 0, 2).reshape(32)
    ids = jnp.arange(32, dtype=jnp.int32)
    inverse = jnp.sum(jnp.where(held[:, None] == ids[None, :], ids[:, None], 0), axis=0)
    table = jnp.concatenate([held, inverse])
    freqs = 10000.0 ** (-np.arange(8, dtype=np.float32) * np.float32(2.0) / np.float32(16))
    lanes = np.concatenate([freqs, freqs, np.zeros(48)]).astype(np.float32)
    freq = jnp.asarray(np.concatenate([lanes, lanes])[None])
    parts = run_block(
        table, hidden_in, out_grad, positions, freq, small,
        qkv_weight, attn_out_weight, up_weight, down_weight,
    )
    done = finish(*parts)
    block_out, input_grad, g_qkv, g_proj, g_up, g_down = done[:6]
    n1g, n1b, n2g, n2b, qk, val, out, up = (item.reshape(-1) for item in done[6:])
    return (
        block_out, input_grad, n1g, n1b, n2g, n2b, g_qkv, qk, val, g_proj, out, g_up, up, g_down,
    )


def solution(mesh):
    both = ("dp", "ctx")
    rows, vec, mat = P("dp", "ctx", None), P(both), P(both, None)
    return jax.shard_map(
        per_device,
        mesh=mesh,
        in_specs=(
            rows, P("dp", "ctx"), P(), vec, vec, vec, vec, mat, vec, mat, vec, mat, vec, mat, rows,
        ),
        out_specs=(
            rows, rows, vec, vec, vec, vec, mat, vec, vec, mat, vec, mat, vec, mat,
        ),
        check_vma=False,
    )
```

```python
import jax
import jax.numpy as jnp
import numpy as np
from jax import lax
from jax.experimental import pallas as pl
from jax.experimental.pallas import tpu as pltpu
from jax.sharding import PartitionSpec as P

EPS = 1e-05
MESH = pl.DeviceIdType.MESH
F32 = jnp.float32
BF16 = jnp.bfloat16
VMEM = pltpu.VMEM
LIMIT = 60 * 1024 * 1024

ORDERS = ((0, 1, 2), (1, 2, 0), (2, 0, 1))
ORDER_OF = (0, 1, 2, 1, 0, 1, 2)
N = 7
FIRST, SMALL, LATER = (0, 1, 2), 3, (4, 5, 6)
TILES = [((16, c), BF16) for c in (256, 128, 128, 0, 384, 256, 384)]
TILES[SMALL] = ((8, 128), F32)
GATHERED = list(TILES)
GATHERED[1] = ((16, 256), BF16)
FIRST_PIECES = ((0, 0, 256, 0), (1, 0, 128, 256), (2, 0, 128, 384))
UP_PIECES = ((4, 0, 384, 0), (5, 0, 128, 384))
DOWN_PIECES = ((5, 128, 128, 0), (6, 0, 384, 128))
SECTIONS_IN = ((4, 0), (4, 4), (4, 8), (4, 12), (12, 16), (4, 28), (16, 32))
SECTIONS_OUT = ((4, 0), (4, 4), (4, 8), (4, 12), (8, 16), (4, 24), (4, 28), (16, 32))


def device_of(x, y, z, core):
    return (z * 2 + lax.rem(x, 2), y * 4 + lax.div(x, 2) * 2 + core)


def slot_of(p, at):
    return sum(at[axis] * 4**k for k, axis in enumerate(ORDERS[ORDER_OF[p]]))


def moved(at, axis, delta):
    at = list(at)
    at[axis] = lax.rem(at[axis] + delta, 4)
    return at


def send(src, dst, ssem, rsem, peer):
    copy = pltpu.make_async_remote_copy(
        src_ref=src, dst_ref=dst, send_sem=ssem, recv_sem=rsem, device_id=peer, device_id_type=MESH
    )
    copy.start()
    return copy


def nt(a, b):
    return lax.dot_general(a, b, (((1,), (1,)), ((), ())), preferred_element_type=F32)


def nn(a, b):
    return lax.dot_general(a, b, (((1,), (0,)), ((), ())), preferred_element_type=F32)


def tn(a, b):
    return lax.dot_general(a, b, (((0,), (0,)), ((), ())), preferred_element_type=F32)


def selectors(n, off):
    cols = lax.broadcasted_iota(jnp.int32, (1, 128 * n), 1)
    owner = ((cols.astype(F32) + 0.5) * (1.0 / n)).astype(jnp.int32)
    lane = cols - owner * n + off
    rows = lax.broadcasted_iota(jnp.int32, (128, 128 * n), 0)
    pick = jnp.where(rows == lane, 1.0, 0.0).astype(BF16)
    return pick, jnp.where(rows == owner, 1.0, 0.0).astype(BF16)


def swap_halves(u):
    lane = lax.broadcasted_iota(jnp.int32, u.shape, 1)
    lane = lane - 64 * (lane >= 64).astype(jnp.int32)
    return jnp.where(lane < 8, pltpu.roll(u, 120, 1), pltpu.roll(u, 8, 1))


def block_kernel(
    table, hid, dy_ref, pos, freq, small, w_qkv, w_proj, w_upper, w_lower,
    out_ref, ingrad_ref, gqkv_ref, gproj_ref, gup_ref, gdown_ref, gsmall_ref,
    *rest,
):
    rest = list(rest)

    def take(count):
        got = rest[:count]
        del rest[:count]
        return got

    bufs, grads, recv = take(N), take(N), take(N)
    squad, rquad, squad2, rquad2, asm, asm2 = take(6)
    wa, wu, wd, ga, gu, gd, smat, gmat = take(8)
    xs, ys, zs, crecv, ctotal, back = take(6)
    qb, kb, vb, db, att_b, dq_b, dk_b, dv_b = take(8)
    xhat, inv_s, cos_s, sin_s, vecs, gvec, h1_s, h2_s, g_s, dup_s, mlp_s, dh2_s, dqkv_s = take(13)
    qs, qr, q2s, q2r, ags, agr, fws, fwr, rss, rsr, sps, spr, sfs, sfr = take(14)
    cos_, cor_, cfs, cfr = take(4)
    pick_in, own_in, pick_out, own_out, kt_b, vt_b = take(6)

    dp, ctx = lax.axis_index("dp"), lax.axis_index("ctx")
    core = lax.rem(ctx, 2)
    at = [
        lax.rem(lax.div(ctx, 2), 2) * 2 + lax.rem(dp, 2), lax.div(ctx, 4), lax.div(dp, 2)
    ]
    sibling = device_of(*at, 1 - core)
    q = lax.rem(ctx, 4)
    axis_peers = [
        [device_of(*moved(at, axis, delta), core) for delta in (1, 2, 3)] for axis in range(3)
    ]
    far = moved(at, 0, 2)
    far_cross = device_of(*far, 1 - core)
    head_at = []
    for delta in range(8):
        place = moved(far if delta % 2 else at, 1, delta // 2)
        head_at.append((place[1] * 2 + lax.div(place[0], 2), device_of(*place, core)))
    me = head_at[0][0]
    quad_peers = [(sibling, 1), (head_at[1][1], 2), (far_cross, 3)]

    def quad_index(delta):
        core_t = 1 - core if delta % 2 else core
        hi = lax.div(at[0], 2)
        return (1 - hi if delta // 2 else hi) * 2 + core_t

    everyone = [sibling, far_cross] + sum(axis_peers, [])
    everyone += [head_at[delta][1] for delta in (3, 5, 7)]
    barrier = pltpu.get_barrier_semaphore()
    for peer in everyone:
        pl.semaphore_signal(barrier, inc=1, device_id=peer, device_id_type=MESH)

    slots = [slot_of(p, at) for p in range(N)]
    started = []

    def settle():
        while started:
            started.pop(0).wait_send()

    squad[...] = jnp.zeros_like(squad)
    qkv_rows = w_qkv[...].astype(F32)
    up_rows = w_upper[...].astype(F32)
    for t in range(3):
        squad[t, 0:4, 0:512] = qkv_rows[:, 512 * t : 512 * (t + 1)]
    squad[3, 0:4, 0:512] = w_proj[...].astype(F32)
    for t in range(4):
        squad[t, 0:4, 512:1024] = up_rows[:, 512 * t : 512 * (t + 1)]
    for p, left, cols, there in DOWN_PIECES:
        bufs[p][core, slots[p], :, left : left + cols] = w_lower[:, there : there + cols]
    bufs[1][core, slots[1], :, 128:256] = small[...]
    x = hid[0].astype(F32)
    center = x - jnp.mean(x, axis=1, keepdims=True)
    inv = lax.rsqrt(jnp.mean(center * center, axis=1, keepdims=True) + EPS)
    xhat[...] = center * inv
    inv_s[...] = jnp.broadcast_to(inv, (128, 128))
    places = jnp.transpose(jnp.broadcast_to(pos[...].astype(F32), (128, 128)))
    angle = places * freq[...]
    lane = lax.broadcasted_iota(jnp.int32, (128, 128), 1)
    lane = lane - 64 * (lane >= 64).astype(jnp.int32)
    sine = jnp.sin(angle)
    cos_s[...] = jnp.cos(angle)
    sin_s[...] = jnp.where(lane < 8, -sine, sine)
    pl.semaphore_wait(barrier, len(everyone))

    quad = []
    for peer, delta in quad_peers:
        quad.append(
            send(squad.at[quad_index(delta)], rquad.at[q], qs.at[delta - 1], qr.at[delta - 1], peer)
        )
    started += quad
    rquad[q] = squad[q]
    hops, fwd = {}, {}

    def block(p, k):
        size = 4**k
        return lax.div(slots[p], size) * size, size

    def gather_send(p, k):
        base, size = block(p, k)
        axis = ORDERS[ORDER_OF[p]][k]
        part = bufs[p].at[core, pl.ds(base, size)]
        for d in range(3):
            hops[p, k, d] = send(
                part, part, ags.at[p, 3 * k + d], agr.at[p, 3 * k + d], axis_peers[axis][d]
            )
            started.append(hops[p, k, d])

    def gather_wait(p, k):
        for d in range(3):
            hops[p, k, d].wait_recv()

    def gather_forward(p):
        gather_wait(p, 2)
        plane = bufs[p].at[core]
        fwd[p] = send(plane, plane, fws.at[p], fwr.at[p], sibling)
        started.append(fwd[p])

    def gather_done(p):
        fwd[p].wait_recv()

    gather_send(6, 0)
    for copy in quad:
        copy.wait_recv()
    for t in range(4):
        asm[4 * t : 4 * t + 4, :] = rquad[t, 0:4, :]
    for p, left, cols, there in FIRST_PIECES + UP_PIECES:
        there = there if p < 3 else there + 512
        bufs[p][core, slots[p], :, left : left + cols] = asm[:, there : there + cols].astype(BF16)
        gather_send(p, 0)

    def build(sections, picks, owns):
        left = 0
        for n, off in sections:
            pick, own = selectors(n, off)
            picks[:, left : left + 128 * n] = pick
            owns[:, left : left + 128 * n] = own
            left += 128 * n

    build(SECTIONS_IN, pick_in, own_in)
    for p in FIRST + LATER:
        gather_wait(p, 0)
        gather_send(p, 1)
    build(SECTIONS_OUT, pick_out, own_out)
    for p in FIRST:
        gather_wait(p, 1)
        gather_send(p, 2)
    for p in FIRST:
        gather_forward(p)
    for p in LATER:
        gather_wait(p, 1)
        gather_send(p, 2)

    def place_of(row, t):
        x_lo = lax.rem(lax.div(row, 4), 2)
        return [(t // 2) * 2 + x_lo, lax.rem(row, 4), lax.div(row, 8)], t % 2

    def wide_loop(pieces, store):
        def body(row, carry):
            rows = pl.ds(pl.multiple_of(row * 16, 16), 16)
            for t in range(4):
                where, c = place_of(row, t)
                for p, left, cols, there in pieces:
                    store(p, c, slot_of(p, where), rows, left, cols, 512 * t + there)
            return carry

        lax.fori_loop(0, 32, body, 0)

    def tall_loop(store):
        def body(row, carry):
            for t in range(4):
                where, c = place_of(row, t)
                rows = pl.ds(pl.multiple_of(row * 64 + t * 16, 16), 16)
                for p, left, cols, there in DOWN_PIECES:
                    store(p, c, slot_of(p, where), rows, left, cols, there)
            return carry

        lax.fori_loop(0, 32, body, 0)

    def unpack_to(dst):
        def store(p, c, slot, rows, left, cols, there):
            dst[rows, there : there + cols] = bufs[p][c, slot, :, left : left + cols]

        return store

    def pack_from(src):
        def store(p, c, slot, rows, left, cols, there):
            grads[p][c, slot, :, left : left + cols] = src[rows, there : there + cols]

        return store

    gather_done(1)

    def small_rows(row, carry):
        for t in range(4):
            where, c = place_of(row, t)
            smat[pl.ds(row * 4 + t, 1), :] = bufs[1][c, slot_of(1, where), :, 128:256].astype(F32)[0:1]
        return carry

    lax.fori_loop(0, 32, small_rows, 0)
    tiles = smat[...].astype(BF16)
    left = 0
    for i, (n, off) in enumerate(SECTIONS_IN):
        cols = slice(left, left + 128 * n)
        left += 128 * n
        vecs[i : i + 1, 0 : 128 * n] = jnp.sum(
            own_in[:, cols].astype(F32) * nn(tiles, pick_in[:, cols]), axis=0, keepdims=True
        )
    normed = xhat[...]
    h1_s[...] = (normed * vecs[0:1, 0:512] + vecs[1:2, 0:512]).astype(BF16)
    h2_s[...] = (normed * vecs[2:3, 0:512] + vecs[3:4, 0:512]).astype(BF16)
    for p in (0, 2):
        gather_done(p)
    wide_loop(FIRST_PIECES, unpack_to(wa))

    dy = dy_ref[0]
    parts = [nn(h1_s[...], wa[:, 512 * i : 512 * (i + 1)]) for i in range(3)]
    parts = [parts[i] + vecs[4:5, 512 * i : 512 * (i + 1)] for i in range(3)]
    cos_t, sin_t = cos_s[...], sin_s[...]

    def turn(u, sign):
        return jnp.concatenate(
            [
                u[:, c : c + 128] * cos_t + swap_halves(u[:, c : c + 128]) * (sin_t * sign)
                for c in range(0, 512, 128)
            ],
            axis=1,
        )

    sent = [turn(parts[0], 1.0), turn(parts[1], 1.0), parts[2], nt(dy, wa[:, 1536:2048])]
    sent = [item.astype(BF16) for item in sent]
    for h in range(8):
        piece = jnp.concatenate([item[:, 64 * h : 64 * h + 64] for item in sent], axis=1)
        xs[h, 0] = piece[0:64]
        xs[h, 1] = piece[64:128]
    spread, spread_fwd = [], []

    def spot(c, m):
        return pl.ds(c * 16 + m * 2, 2)

    for delta in range(1, 8):
        m, peer = head_at[delta]
        spread.append(
            send(xs.at[m], ys.at[spot(core, me)], sps.at[delta - 1], spr.at[delta - 1], peer)
        )
    ys[spot(core, me)] = xs[me]
    mine = ys.at[spot(core, me)]
    spread_fwd.append(send(mine, mine, sfs.at[0], sfr.at[0], sibling))

    for p in LATER:
        gather_forward(p)
    for p in LATER:
        gather_done(p)
    wide_loop(UP_PIECES, unpack_to(wu))
    tall_loop(unpack_to(wd))

    def mlp(t):
        cols = slice(512 * t, 512 * (t + 1))
        up = nn(h2_s[...], wu[:, cols]) + vecs[6:7, cols]
        cdf = 0.5 * (1.0 + lax.erf(up * np.float32(0.5**0.5)))
        pdf = jnp.exp(-0.5 * up * up) * np.float32((2 * np.pi) ** -0.5)
        g = (up * cdf).astype(BF16)
        d_up = (nt(dy, wd[cols, :]) * (cdf + up * pdf)).astype(BF16)
        g_s[:, cols] = g
        dup_s[:, cols] = d_up
        gvec[7:8, cols] = jnp.sum(d_up.astype(F32), axis=0, keepdims=True)
        gu[:, cols] = tn(h2_s[...], d_up).astype(BF16)
        gd[cols, :] = tn(g, dy).astype(BF16)

    for t in range(4):
        mlp(t)
        if t == 1:
            for delta in range(1, 8):
                back_y = (4 - delta // 2) % 4
                m = head_at[back_y * 2 + delta % 2][0]
                spread[delta - 1].wait_recv()
                part = ys.at[spot(core, m)]
                spread_fwd.append(send(part, part, sfs.at[delta], sfr.at[delta], sibling))
    started += spread + spread_fwd

    adds = {}

    def reduce_start(p):
        adds[p, 3] = send(
            grads[p].at[1 - core], recv[p].at[pl.ds(0, 64)], rss.at[p, 9], rsr.at[p, 9], sibling
        )
        started.append(adds[p, 3])

    def offset(k):
        return 64 + {2: 0, 1: 48, 0: 60}[k]

    def reduce_step(p, k):
        if k == 2:
            adds[p, 3].wait_recv()
            total, others, base = 64, (0,), 0
        else:
            for d in range(3):
                adds[p, k + 1, d].wait_recv()
            base, total = block(p, k + 1)
            others = [offset(k + 1) + d * total for d in range(3)]
        unit = min(total, 8 if len(others) == 1 else 4)

        def body(i, carry):
            here = pl.ds(base + i * unit, unit)
            if len(others) == 1:
                grads[p][core, here] += recv[p][pl.ds(others[0] + i * unit, unit)]
                return carry
            value = grads[p][core, here].astype(F32)
            for other in others:
                value = value + recv[p][pl.ds(other + i * unit, unit)].astype(F32)
            grads[p][core, here] = value.astype(grads[p].dtype)
            return carry

        lax.fori_loop(0, total // unit, body, 0)
        axis = ORDERS[ORDER_OF[p]][k]
        size = 4**k
        own, _ = block(p, k)
        for d in range(3):
            there = lax.rem(at[axis] + d + 1, 4)
            part = grads[p].at[core, pl.ds(own + (there - at[axis]) * size, size)]
            adds[p, k, d] = send(
                part, recv[p].at[pl.ds(offset(k) + d * size, size)],
                rss.at[p, 3 * k + d], rsr.at[p, 3 * k + d], axis_peers[axis][d],
            )
            started.append(adds[p, k, d])

    def reduce_end(p):
        for d in range(3):
            adds[p, 0, d].wait_recv()
        value = grads[p][core, slots[p]].astype(F32)
        for d in range(3):
            value = value + recv[p][offset(0) + d].astype(F32)
        return value

    wide_loop(UP_PIECES, pack_from(gu))
    tall_loop(pack_from(gd))
    for p in LATER:
        reduce_start(p)

    for copy in spread_fwd:
        copy.wait_recv()
    ones = jnp.where(lax.broadcasted_iota(jnp.int32, (64, 64), 1) < 2, 1.0, 0.0).astype(BF16)
    for t in range(32):
        part = ys[table[32 + t]]
        rows = slice(64 * t, 64 * t + 64)
        qb[rows, :] = part[:, 0:64]
        kb[rows, :] = part[:, 64:128]
        vb[rows, :] = jnp.concatenate([part[:, 128:192], ones], axis=1)
        db[rows, :] = part[:, 192:256]
    kt_b[...] = jnp.transpose(kb[...].astype(F32)).astype(BF16)
    vt_b[...] = jnp.transpose(vb[:, 0:64].astype(F32)).astype(BF16)

    def tile(j):
        low, width = 512 * j, 512 * (j + 1)
        turn_off = 1 - core if j % 2 else core
        row = low + 256 * turn_off
        rows = pl.ds(pl.multiple_of(row, 256), 256)
        queries = qb[rows, :].astype(F32) * 0.125
        q_t = jnp.transpose(queries).astype(BF16)
        do_t = jnp.transpose(db[rows, :].astype(F32))
        at_k = low + lax.broadcasted_iota(jnp.int32, (512, 256), 0)
        at_q = row + lax.broadcasted_iota(jnp.int32, (512, 256), 1)
        near = jnp.where(at_q >= at_k, nn(kb[low:width, :], q_t), -1e30)
        top = jnp.max(near, axis=0, keepdims=True)
        if j:
            away = nn(kb[0:low, :], q_t)
            top = jnp.maximum(top, jnp.max(away, axis=0, keepdims=True))
        near = jnp.exp(near - top)
        total = jnp.sum(near, axis=0, keepdims=True)
        probs = near.astype(BF16)
        if j:
            away = jnp.exp(away - top)
            total = total + jnp.sum(away, axis=0, keepdims=True)
            probs = jnp.concatenate([away.astype(BF16), probs], axis=0)
        scale = 1.0 / total
        att_t = nn(vt_b[:, 0:width], probs) * scale
        do_t = (do_t * scale).astype(BF16).astype(F32)
        delta = jnp.sum(do_t * att_t, axis=0, keepdims=True)
        high = delta.astype(BF16).astype(F32)
        tail = lax.broadcasted_iota(jnp.int32, (8, 256), 0)
        tail = jnp.where(tail == 0, -high, jnp.where(tail == 1, high - delta, 0.0))
        right = jnp.concatenate([do_t, tail, jnp.zeros((56, 256), F32)], axis=0).astype(BF16)
        d_s = (probs.astype(F32) * nn(vb[0:width, :], right)).astype(BF16)
        blocks = pl.ds(8 * j + 4 * turn_off, 4)
        blank = pl.ds(8 * j + 4 * (1 - turn_off), 4)
        att_b[blocks] = jnp.transpose(att_t).reshape(4, 64, 64)
        dq_b[blocks] = jnp.transpose(nn(kt_b[:, 0:width], d_s) * 0.125).reshape(4, 64, 64)
        att_b[blank] = jnp.zeros((4, 64, 64), F32)
        dq_b[blank] = jnp.zeros((4, 64, 64), F32)
        d_k = nn(d_s, queries.astype(BF16)).reshape(8 * (j + 1), 64, 64)
        d_v = nn(probs, jnp.transpose(do_t).astype(BF16)).reshape(8 * (j + 1), 64, 64)
        if j == 3:
            dk_b[...] = d_k
            dv_b[...] = d_v
        else:
            dk_b[0 : 8 * (j + 1)] += d_k
            dv_b[0 : 8 * (j + 1)] += d_v

    tile(3)
    for p in LATER:
        reduce_step(p, 2)
    for j in (2, 1, 0):
        tile(j)
    for i in range(32):
        t = table[i]
        zs[i] = jnp.concatenate([att_b[t], dq_b[t], dk_b[t], dv_b[t]], axis=1).astype(BF16)

    order = (1, 2, 3, 4, 5, 6, 7, 0)
    halves, collect = {}, []
    for delta in order:
        m, _ = head_at[delta]
        halves[delta] = send(
            zs.at[spot(1 - core, m)], crecv.at[m], cfs.at[delta], cfr.at[delta], sibling
        )
    started += list(halves.values())
    mlp_s[...] = nn(g_s[...], wd[...])
    for delta in order:
        m, peer = head_at[delta]
        halves[delta].wait_recv()
        ctotal[m] = zs[spot(core, m)] + crecv[m]
        if delta:
            collect.append(
                send(ctotal.at[m], back.at[me], cos_.at[delta - 1], cor_.at[delta - 1], peer)
            )
        else:
            back[me] = ctotal[m]
    started += collect
    for p in LATER:
        reduce_step(p, 1)
    dh2_s[...] = nt(dup_s[...], wu[...])
    dh2 = dh2_s[...]
    gvec[2:3, 0:512] = jnp.sum(dh2 * xhat[...], axis=0, keepdims=True)
    gvec[3:4, 0:512] = jnp.sum(dh2, axis=0, keepdims=True)
    gvec[6:7, 0:512] = jnp.sum(dy.astype(F32), axis=0, keepdims=True)
    settle()
    for copy in collect:
        copy.wait_recv()

    def whole(i):
        return jnp.concatenate(
            [
                jnp.concatenate(
                    [back[h, 0, :, 64 * i : 64 * i + 64], back[h, 1, :, 64 * i : 64 * i + 64]],
                    axis=0,
                )
                for h in range(8)
            ],
            axis=1,
        )

    dqkv_s[:, 0:512] = turn(whole(1).astype(F32), -1.0).astype(BF16)
    dqkv_s[:, 512:1024] = turn(whole(2).astype(F32), -1.0).astype(BF16)
    dqkv_s[:, 1024:1536] = whole(3)
    mixed = whole(0)
    ga[:, 1536:2048] = tn(mixed, dy).astype(BF16)
    for t in range(3):
        ga[:, 512 * t : 512 * (t + 1)] = tn(
            h1_s[...], dqkv_s[:, 512 * t : 512 * (t + 1)]
        ).astype(BF16)
    wide_loop(FIRST_PIECES, pack_from(ga))
    for p in FIRST:
        reduce_start(p)
    dh1 = nt(dqkv_s[...], wa[:, 0:1536])
    gvec[0:1, 0:512] = jnp.sum(dh1 * xhat[...], axis=0, keepdims=True)
    gvec[1:2, 0:512] = jnp.sum(dh1, axis=0, keepdims=True)
    gvec[4:5, 0:1024] = jnp.sum(dqkv_s[:, 0:1024].astype(F32), axis=0, keepdims=True)
    gvec[5:6, 0:512] = jnp.sum(dqkv_s[:, 1024:1536].astype(F32), axis=0, keepdims=True)
    for p in FIRST:
        reduce_step(p, 2)
    spread_out = jnp.zeros((128, 128), F32)
    left = 0
    for i, (n, off) in enumerate(SECTIONS_OUT):
        cols = slice(left, left + 128 * n)
        left += 128 * n
        value = gvec[i : i + 1, 0 : 128 * n]
        high = value.astype(BF16)
        low = (value - high.astype(F32)).astype(BF16)
        pick, own = pick_out[:, cols], own_out[:, cols]
        spread_out = spread_out + nt(own * high, pick) + nt(own * low, pick)
    gmat[...] = spread_out
    grads[SMALL][...] = jnp.zeros_like(grads[SMALL])

    def small_grads(row, carry):
        for t in range(4):
            where, c = place_of(row, t)
            grads[SMALL][c, slot_of(SMALL, where), 0:1, :] = gmat[pl.ds(row * 4 + t, 1), :]
        return carry

    lax.fori_loop(0, 32, small_grads, 0)
    reduce_start(SMALL)
    result = hid[0].astype(F32) + nn(mixed, wa[:, 1536:2048]) + mlp_s[...] + vecs[5:6, 0:512]
    out_ref[0] = result.astype(BF16)
    reduce_step(SMALL, 2)
    d_norm = dh1 * vecs[0:1, 0:512] + dh2_s[...] * vecs[2:3, 0:512]
    normed = xhat[...]
    d_x = d_norm - jnp.mean(d_norm, axis=1, keepdims=True)
    d_x = d_x - normed * jnp.mean(d_norm * normed, axis=1, keepdims=True)
    ingrad_ref[0] = dy.astype(F32) + d_x * inv_s[:, 0:1]
    for p in LATER:
        reduce_step(p, 0)
    for p in FIRST + (SMALL,):
        reduce_step(p, 1)
    for p in LATER:
        value = reduce_end(p)
        for p_of, left, cols, there in UP_PIECES:
            if p_of == p:
                asm2[:, 512 + there : 512 + there + cols] = value[:, left : left + cols]
        for p_of, left, cols, there in DOWN_PIECES:
            if p_of == p:
                gdown_ref[:, there : there + cols] = value[:, left : left + cols]
    for p in FIRST + (SMALL,):
        reduce_step(p, 0)
    for p, _, cols, there in FIRST_PIECES:
        asm2[:, there : there + cols] = reduce_end(p)
    gsmall_ref[...] = reduce_end(SMALL)
    squad2[...] = jnp.zeros_like(squad2)
    for t in range(4):
        squad2[t, 0:4, :] = asm2[4 * t : 4 * t + 4, :]
    quad = []
    for peer, delta in quad_peers:
        quad.append(
            send(
                squad2.at[quad_index(delta)], rquad2.at[q], q2s.at[delta - 1], q2r.at[delta - 1],
                peer,
            )
        )
    rquad2[q] = squad2[q]
    settle()
    for copy in quad:
        copy.wait_recv()
    for t in range(3):
        gqkv_ref[:, 512 * t : 512 * (t + 1)] = rquad2[t, 0:4, 0:512]
    gproj_ref[...] = rquad2[3, 0:4, 0:512]
    for t in range(4):
        gup_ref[:, 512 * t : 512 * (t + 1)] = rquad2[t, 0:4, 512:1024]
    for copy in quad:
        copy.wait_send()


def run_block(*args):
    dma = pltpu.SemaphoreType.DMA
    scratch = [VMEM((2, 64) + tile, dtype) for tile, dtype in GATHERED]
    scratch += [VMEM((2, 64) + tile, dtype) for tile, dtype in TILES]
    scratch += [VMEM((128,) + tile, dtype) for tile, dtype in TILES]
    scratch += [VMEM((4, 8, 1024), F32)] * 4 + [VMEM((16, 1024), F32)] * 2
    scratch += [VMEM((512, 2048), BF16), VMEM((512, 2048), BF16), VMEM((2048, 512), BF16)] * 2
    scratch += [VMEM((128, 128), F32)] * 2
    scratch += [VMEM((8, 2, 64, 256), BF16), VMEM((32, 64, 256), BF16), VMEM((32, 64, 256), BF16)]
    scratch += [VMEM((8, 2, 64, 256), BF16)] * 3
    scratch += [VMEM((2048, 64), BF16)] * 2 + [VMEM((2048, 128), BF16), VMEM((2048, 64), BF16)]
    scratch += [VMEM((32, 64, 64), F32)] * 4
    scratch += [VMEM((128, 512), F32)] + [VMEM((128, 128), F32)] * 3 + [VMEM((8, 2048), F32)] * 2
    scratch += [VMEM((128, 512), BF16)] * 2 + [VMEM((128, 2048), BF16)] * 2
    scratch += [VMEM((128, 512), F32)] * 2 + [VMEM((128, 1536), BF16)]
    scratch += [dma((3,))] * 4 + [dma((N, 9))] * 2 + [dma((N,))] * 2 + [dma((N, 10))] * 2
    scratch += [dma((7,)), dma((7,)), dma((8,)), dma((8,))] * 2
    scratch += [VMEM((128, 6144), BF16)] * 4 + [VMEM((64, 2048), BF16)] * 2
    shape = jax.ShapeDtypeStruct
    return pl.pallas_call(
        block_kernel,
        out_shape=(
            shape((1, 128, 512), BF16), shape((1, 128, 512), F32), shape((4, 1536), F32),
            shape((4, 512), F32), shape((4, 2048), F32), shape((16, 512), F32), shape((8, 128), F32),
        ),
        in_specs=[pl.BlockSpec(memory_space=pltpu.SMEM)] + [pl.BlockSpec(memory_space=VMEM)] * 9,
        out_specs=[pl.BlockSpec(memory_space=VMEM)] * 7,
        scratch_shapes=scratch,
        compiler_params=pltpu.CompilerParams(
            collective_id=0, has_side_effects=True, vmem_limit_bytes=LIMIT
        ),
    )(*args)


def finish_kernel(*refs):
    for src, dst in zip(refs[:6], refs[7:13]):
        dst[...] = src[...]
    row = refs[6][0:1, :]
    for (n, off), dst in zip(SECTIONS_OUT, refs[13:]):
        dst[...] = row[:, off : off + n]


def finish(*parts):
    shape = jax.ShapeDtypeStruct
    return pl.pallas_call(
        finish_kernel,
        out_shape=tuple(shape(part.shape, part.dtype) for part in parts[:6])
        + tuple(shape((1, n), F32) for n, _ in SECTIONS_OUT),
        in_specs=[pl.BlockSpec(memory_space=VMEM)] * 7,
        out_specs=[pl.BlockSpec(memory_space=VMEM)] * 14,
    )(*parts)


def per_device(
    hidden_in, positions, block_order, norm1_gain, norm1_bias, norm2_gain, norm2_bias,
    qkv_weight, qkv_bias, attn_out_weight, out_bias, up_weight, up_bias, down_weight, out_grad,
):
    small = jnp.concatenate(
        [norm1_gain, norm1_bias, norm2_gain, norm2_bias, qkv_bias, out_bias, up_bias]
    )
    small = jnp.pad(small[None], ((0, 15), (0, 80)))
    held = block_order.reshape(8, 2, 2).transpose(1, 0, 2).reshape(32)
    ids = jnp.arange(32, dtype=jnp.int32)
    inverse = jnp.sum(jnp.where(held[:, None] == ids[None, :], ids[:, None], 0), axis=0)
    table = jnp.concatenate([held, inverse])
    freqs = 10000.0 ** (-np.arange(8, dtype=np.float32) * np.float32(2.0) / np.float32(16))
    lanes = np.concatenate([freqs, freqs, np.zeros(48)]).astype(np.float32)
    freq = jnp.asarray(np.concatenate([lanes, lanes])[None])
    parts = run_block(
        table, hidden_in, out_grad, positions, freq, small,
        qkv_weight, attn_out_weight, up_weight, down_weight,
    )
    done = finish(*parts)
    block_out, input_grad, g_qkv, g_proj, g_up, g_down = done[:6]
    n1g, n1b, n2g, n2b, qk, val, out, up = (item.reshape(-1) for item in done[6:])
    return (
        block_out, input_grad, n1g, n1b, n2g, n2b, g_qkv, qk, val, g_proj, out, g_up, up, g_down,
    )


def solution(mesh):
    both = ("dp", "ctx")
    rows, vec, mat = P("dp", "ctx", None), P(both), P(both, None)
    return jax.shard_map(
        per_device,
        mesh=mesh,
        in_specs=(
            rows, P("dp", "ctx"), P(), vec, vec, vec, vec, mat, vec, mat, vec, mat, vec, mat, rows,
        ),
        out_specs=(
            rows, rows, vec, vec, vec, vec, mat, vec, vec, mat, vec, mat, vec, mat,
        ),
        check_vma=False,
    )
```

```python
import jax
import jax.numpy as jnp
import numpy as np
from jax import lax
from jax.experimental import pallas as pl
from jax.experimental.pallas import tpu as pltpu
from jax.sharding import PartitionSpec as P

EPS = 1e-05
MESH = pl.DeviceIdType.MESH
F32 = jnp.float32
BF16 = jnp.bfloat16
VMEM = pltpu.VMEM
LIMIT = 60 * 1024 * 1024

ORDERS = ((0, 1, 2), (1, 2, 0), (2, 0, 1))
ORDER_OF = (0, 1, 2, 1, 0, 1, 2)
N = 7
FIRST, SMALL, LATER = (0, 1, 2), 3, (4, 5, 6)
TILES = [((16, c), BF16) for c in (256, 128, 128, 0, 384, 256, 384)]
TILES[SMALL] = ((8, 128), F32)
GATHERED = list(TILES)
GATHERED[1] = ((16, 256), BF16)
FIRST_PIECES = ((0, 0, 256, 0), (1, 0, 128, 256), (2, 0, 128, 384))
UP_PIECES = ((4, 0, 384, 0), (5, 0, 128, 384))
DOWN_PIECES = ((5, 128, 128, 0), (6, 0, 384, 128))
SECTIONS_IN = ((4, 0), (4, 4), (4, 8), (4, 12), (12, 16), (4, 28), (16, 32))
SECTIONS_OUT = ((4, 0), (4, 4), (4, 8), (4, 12), (8, 16), (4, 24), (4, 28), (16, 32))


def device_of(x, y, z, core):
    return (z * 2 + lax.rem(x, 2), y * 4 + lax.div(x, 2) * 2 + core)


def slot_of(p, at):
    return sum(at[axis] * 4**k for k, axis in enumerate(ORDERS[ORDER_OF[p]]))


def moved(at, axis, delta):
    at = list(at)
    at[axis] = lax.rem(at[axis] + delta, 4)
    return at


def send(src, dst, ssem, rsem, peer):
    copy = pltpu.make_async_remote_copy(
        src_ref=src, dst_ref=dst, send_sem=ssem, recv_sem=rsem, device_id=peer, device_id_type=MESH
    )
    copy.start()
    return copy


def nt(a, b):
    return lax.dot_general(a, b, (((1,), (1,)), ((), ())), preferred_element_type=F32)


def nn(a, b):
    return lax.dot_general(a, b, (((1,), (0,)), ((), ())), preferred_element_type=F32)


def tn(a, b):
    return lax.dot_general(a, b, (((0,), (0,)), ((), ())), preferred_element_type=F32)


def selectors(n, off):
    cols = lax.broadcasted_iota(jnp.int32, (1, 128 * n), 1)
    owner = ((cols.astype(F32) + 0.5) * (1.0 / n)).astype(jnp.int32)
    lane = cols - owner * n + off
    rows = lax.broadcasted_iota(jnp.int32, (128, 128 * n), 0)
    pick = jnp.where(rows == lane, 1.0, 0.0).astype(BF16)
    return pick, jnp.where(rows == owner, 1.0, 0.0).astype(BF16)


def swap_halves(u):
    lane = lax.broadcasted_iota(jnp.int32, u.shape, 1)
    lane = lane - 64 * (lane >= 64).astype(jnp.int32)
    return jnp.where(lane < 8, pltpu.roll(u, 120, 1), pltpu.roll(u, 8, 1))


def block_kernel(
    table, hid, dy_ref, pos, freq, small, w_qkv, w_proj, w_upper, w_lower,
    out_ref, ingrad_ref, gqkv_ref, gproj_ref, gup_ref, gdown_ref, gsmall_ref,
    *rest,
):
    rest = list(rest)

    def take(count):
        got = rest[:count]
        del rest[:count]
        return got

    bufs, grads, recv = take(N), take(N), take(N)
    squad, rquad, squad2, rquad2, asm, asm2 = take(6)
    wa, wu, wd, ga, gu, gd, smat, gmat = take(8)
    xs, ys, zs, crecv, ctotal, back = take(6)
    qb, kb, vb, db, att_b, dq_b, dk_b, dv_b = take(8)
    xhat, inv_s, cos_s, sin_s, vecs, gvec, h1_s, h2_s, g_s, dup_s, mlp_s, dh2_s, dqkv_s = take(13)
    qs, qr, q2s, q2r, ags, agr, fws, fwr, rss, rsr, sps, spr, sfs, sfr = take(14)
    cos_, cor_, cfs, cfr = take(4)
    pick_in, own_in, pick_out, own_out, kt_b, vt_b = take(6)

    dp, ctx = lax.axis_index("dp"), lax.axis_index("ctx")
    core = lax.rem(ctx, 2)
    at = [
        lax.rem(lax.div(ctx, 2), 2) * 2 + lax.rem(dp, 2), lax.div(ctx, 4), lax.div(dp, 2)
    ]
    sibling = device_of(*at, 1 - core)
    q = lax.rem(ctx, 4)
    axis_peers = [
        [device_of(*moved(at, axis, delta), core) for delta in (1, 2, 3)] for axis in range(3)
    ]
    far = moved(at, 0, 2)
    far_cross = device_of(*far, 1 - core)
    head_at = []
    for delta in range(8):
        place = moved(far if delta % 2 else at, 1, delta // 2)
        head_at.append((place[1] * 2 + lax.div(place[0], 2), device_of(*place, core)))
    me = head_at[0][0]
    quad_peers = [(sibling, 1), (head_at[1][1], 2), (far_cross, 3)]

    def quad_index(delta):
        core_t = 1 - core if delta % 2 else core
        hi = lax.div(at[0], 2)
        return (1 - hi if delta // 2 else hi) * 2 + core_t

    everyone = [sibling, far_cross] + sum(axis_peers, [])
    everyone += [head_at[delta][1] for delta in (3, 5, 7)]
    barrier = pltpu.get_barrier_semaphore()
    for peer in everyone:
        pl.semaphore_signal(barrier, inc=1, device_id=peer, device_id_type=MESH)

    slots = [slot_of(p, at) for p in range(N)]
    started = []

    def settle():
        while started:
            started.pop(0).wait_send()

    squad[...] = jnp.zeros_like(squad)
    qkv_rows = w_qkv[...].astype(F32)
    up_rows = w_upper[...].astype(F32)
    for t in range(3):
        squad[t, 0:4, 0:512] = qkv_rows[:, 512 * t : 512 * (t + 1)]
    squad[3, 0:4, 0:512] = w_proj[...].astype(F32)
    for t in range(4):
        squad[t, 0:4, 512:1024] = up_rows[:, 512 * t : 512 * (t + 1)]
    for p, left, cols, there in DOWN_PIECES:
        bufs[p][core, slots[p], :, left : left + cols] = w_lower[:, there : there + cols]
    bufs[1][core, slots[1], :, 128:256] = small[...]
    x = hid[0].astype(F32)
    center = x - jnp.mean(x, axis=1, keepdims=True)
    inv = lax.rsqrt(jnp.mean(center * center, axis=1, keepdims=True) + EPS)
    xhat[...] = center * inv
    inv_s[...] = jnp.broadcast_to(inv, (128, 128))
    places = jnp.transpose(jnp.broadcast_to(pos[...].astype(F32), (128, 128)))
    angle = places * freq[...]
    lane = lax.broadcasted_iota(jnp.int32, (128, 128), 1)
    lane = lane - 64 * (lane >= 64).astype(jnp.int32)
    sine = jnp.sin(angle)
    cos_s[...] = jnp.cos(angle)
    sin_s[...] = jnp.where(lane < 8, -sine, sine)
    pl.semaphore_wait(barrier, len(everyone))

    quad = []
    for peer, delta in quad_peers:
        quad.append(
            send(squad.at[quad_index(delta)], rquad.at[q], qs.at[delta - 1], qr.at[delta - 1], peer)
        )
    started += quad
    rquad[q] = squad[q]
    hops, fwd = {}, {}

    def block(p, k):
        size = 4**k
        return lax.div(slots[p], size) * size, size

    def gather_send(p, k):
        base, size = block(p, k)
        axis = ORDERS[ORDER_OF[p]][k]
        part = bufs[p].at[core, pl.ds(base, size)]
        for d in range(3):
            hops[p, k, d] = send(
                part, part, ags.at[p, 3 * k + d], agr.at[p, 3 * k + d], axis_peers[axis][d]
            )
            started.append(hops[p, k, d])

    def gather_wait(p, k):
        for d in range(3):
            hops[p, k, d].wait_recv()

    def gather_forward(p):
        gather_wait(p, 2)
        plane = bufs[p].at[core]
        fwd[p] = send(plane, plane, fws.at[p], fwr.at[p], sibling)
        started.append(fwd[p])

    def gather_done(p):
        fwd[p].wait_recv()

    gather_send(6, 0)
    for copy in quad:
        copy.wait_recv()
    for t in range(4):
        asm[4 * t : 4 * t + 4, :] = rquad[t, 0:4, :]
    for p, left, cols, there in FIRST_PIECES + UP_PIECES:
        there = there if p < 3 else there + 512
        bufs[p][core, slots[p], :, left : left + cols] = asm[:, there : there + cols].astype(BF16)
        gather_send(p, 0)

    def build(sections, picks, owns):
        left = 0
        for n, off in sections:
            pick, own = selectors(n, off)
            picks[:, left : left + 128 * n] = pick
            owns[:, left : left + 128 * n] = own
            left += 128 * n

    build(SECTIONS_IN, pick_in, own_in)
    for p in FIRST + LATER:
        gather_wait(p, 0)
        gather_send(p, 1)
    build(SECTIONS_OUT, pick_out, own_out)
    for p in FIRST:
        gather_wait(p, 1)
        gather_send(p, 2)
    for p in FIRST:
        gather_forward(p)
    for p in LATER:
        gather_wait(p, 1)
        gather_send(p, 2)

    def each_device(step):
        def body(z, carry):
            for low in range(8):
                for t in range(4):
                    step(z, low, t, [(t // 2) * 2 + low // 4, low % 4, z], t % 2)
            return carry

        lax.fori_loop(0, 4, body, 0)

    def wide_loop(pieces, store):
        def step(z, low, t, where, c):
            rows = pl.ds(pl.multiple_of(z * 128 + low * 16, 16), 16)
            for p, left, cols, there in pieces:
                store(p, c, slot_of(p, where), rows, left, cols, 512 * t + there)

        each_device(step)

    def tall_loop(store):
        def step(z, low, t, where, c):
            rows = pl.ds(pl.multiple_of(z * 512 + low * 64 + t * 16, 16), 16)
            for p, left, cols, there in DOWN_PIECES:
                store(p, c, slot_of(p, where), rows, left, cols, there)

        each_device(step)

    def unpack_to(dst):
        def store(p, c, slot, rows, left, cols, there):
            dst[rows, there : there + cols] = bufs[p][c, slot, :, left : left + cols]

        return store

    def pack_from(src):
        def store(p, c, slot, rows, left, cols, there):
            grads[p][c, slot, :, left : left + cols] = src[rows, there : there + cols]

        return store

    gather_done(1)

    def small_rows(z, low, t, where, c):
        tile = bufs[1][c, slot_of(1, where), :, 128:256].astype(F32)
        smat[pl.ds(z * 32 + (low * 4 + t), 1), :] = tile[0:1]

    each_device(small_rows)
    tiles = smat[...].astype(BF16)
    left = 0
    for i, (n, off) in enumerate(SECTIONS_IN):
        cols = slice(left, left + 128 * n)
        left += 128 * n
        vecs[i : i + 1, 0 : 128 * n] = jnp.sum(
            own_in[:, cols].astype(F32) * nn(tiles, pick_in[:, cols]), axis=0, keepdims=True
        )
    normed = xhat[...]
    h1_s[...] = (normed * vecs[0:1, 0:512] + vecs[1:2, 0:512]).astype(BF16)
    h2_s[...] = (normed * vecs[2:3, 0:512] + vecs[3:4, 0:512]).astype(BF16)
    for p in (0, 2):
        gather_done(p)
    wide_loop(FIRST_PIECES, unpack_to(wa))

    dy = dy_ref[0]
    parts = [nn(h1_s[...], wa[:, 512 * i : 512 * (i + 1)]) for i in range(3)]
    parts = [parts[i] + vecs[4:5, 512 * i : 512 * (i + 1)] for i in range(3)]
    cos_t, sin_t = cos_s[...], sin_s[...]

    def turn(u, sign):
        return jnp.concatenate(
            [
                u[:, c : c + 128] * cos_t + swap_halves(u[:, c : c + 128]) * (sin_t * sign)
                for c in range(0, 512, 128)
            ],
            axis=1,
        )

    sent = [turn(parts[0], 1.0), turn(parts[1], 1.0), parts[2], nt(dy, wa[:, 1536:2048])]
    sent = [item.astype(BF16) for item in sent]
    for h in range(8):
        piece = jnp.concatenate([item[:, 64 * h : 64 * h + 64] for item in sent], axis=1)
        xs[h, 0] = piece[0:64]
        xs[h, 1] = piece[64:128]
    spread, spread_fwd = [], []

    def spot(c, m):
        return pl.ds(c * 16 + m * 2, 2)

    for delta in range(1, 8):
        m, peer = head_at[delta]
        spread.append(
            send(xs.at[m], ys.at[spot(core, me)], sps.at[delta - 1], spr.at[delta - 1], peer)
        )
    ys[spot(core, me)] = xs[me]
    mine = ys.at[spot(core, me)]
    spread_fwd.append(send(mine, mine, sfs.at[0], sfr.at[0], sibling))

    for p in LATER:
        gather_forward(p)
    for p in LATER:
        gather_done(p)
    wide_loop(UP_PIECES, unpack_to(wu))
    tall_loop(unpack_to(wd))

    def mlp(t):
        cols = slice(512 * t, 512 * (t + 1))
        up = nn(h2_s[...], wu[:, cols]) + vecs[6:7, cols]
        cdf = 0.5 * (1.0 + lax.erf(up * np.float32(0.5**0.5)))
        pdf = jnp.exp(-0.5 * up * up) * np.float32((2 * np.pi) ** -0.5)
        g = (up * cdf).astype(BF16)
        d_up = (nt(dy, wd[cols, :]) * (cdf + up * pdf)).astype(BF16)
        g_s[:, cols] = g
        dup_s[:, cols] = d_up
        gvec[7:8, cols] = jnp.sum(d_up.astype(F32), axis=0, keepdims=True)
        gu[:, cols] = tn(h2_s[...], d_up).astype(BF16)
        gd[cols, :] = tn(g, dy).astype(BF16)

    for t in range(4):
        mlp(t)
        if t == 1:
            for delta in range(1, 8):
                back_y = (4 - delta // 2) % 4
                m = head_at[back_y * 2 + delta % 2][0]
                spread[delta - 1].wait_recv()
                part = ys.at[spot(core, m)]
                spread_fwd.append(send(part, part, sfs.at[delta], sfr.at[delta], sibling))
    started += spread + spread_fwd

    adds = {}

    def reduce_start(p):
        adds[p, 3] = send(
            grads[p].at[1 - core], recv[p].at[pl.ds(0, 64)], rss.at[p, 9], rsr.at[p, 9], sibling
        )
        started.append(adds[p, 3])

    def offset(k):
        return 64 + {2: 0, 1: 48, 0: 60}[k]

    def reduce_step(p, k):
        if k == 2:
            adds[p, 3].wait_recv()
            total, others, base = 64, (0,), 0
        else:
            for d in range(3):
                adds[p, k + 1, d].wait_recv()
            base, total = block(p, k + 1)
            others = [offset(k + 1) + d * total for d in range(3)]
        unit = min(total, 8 if len(others) == 1 else 4)

        def body(i, carry):
            here = pl.ds(base + i * unit, unit)
            if len(others) == 1:
                grads[p][core, here] += recv[p][pl.ds(others[0] + i * unit, unit)]
                return carry
            value = grads[p][core, here].astype(F32)
            for other in others:
                value = value + recv[p][pl.ds(other + i * unit, unit)].astype(F32)
            grads[p][core, here] = value.astype(grads[p].dtype)
            return carry

        lax.fori_loop(0, total // unit, body, 0)
        axis = ORDERS[ORDER_OF[p]][k]
        size = 4**k
        own, _ = block(p, k)
        for d in range(3):
            there = lax.rem(at[axis] + d + 1, 4)
            part = grads[p].at[core, pl.ds(own + (there - at[axis]) * size, size)]
            adds[p, k, d] = send(
                part, recv[p].at[pl.ds(offset(k) + d * size, size)],
                rss.at[p, 3 * k + d], rsr.at[p, 3 * k + d], axis_peers[axis][d],
            )
            started.append(adds[p, k, d])

    def reduce_end(p):
        for d in range(3):
            adds[p, 0, d].wait_recv()
        value = grads[p][core, slots[p]].astype(F32)
        for d in range(3):
            value = value + recv[p][offset(0) + d].astype(F32)
        return value

    wide_loop(UP_PIECES, pack_from(gu))
    tall_loop(pack_from(gd))
    for p in LATER:
        reduce_start(p)

    for copy in spread_fwd:
        copy.wait_recv()
    ones = jnp.where(lax.broadcasted_iota(jnp.int32, (64, 64), 1) < 2, 1.0, 0.0).astype(BF16)
    for t in range(32):
        part = ys[table[32 + t]]
        rows = slice(64 * t, 64 * t + 64)
        qb[rows, :] = part[:, 0:64]
        kb[rows, :] = part[:, 64:128]
        vb[rows, :] = jnp.concatenate([part[:, 128:192], ones], axis=1)
        db[rows, :] = part[:, 192:256]
    kt_b[...] = jnp.transpose(kb[...].astype(F32)).astype(BF16)
    vt_b[...] = jnp.transpose(vb[:, 0:64].astype(F32)).astype(BF16)

    def tile(j):
        low, width = 512 * j, 512 * (j + 1)
        turn_off = 1 - core if j % 2 else core
        row = low + 256 * turn_off
        rows = pl.ds(pl.multiple_of(row, 256), 256)
        queries = qb[rows, :].astype(F32) * 0.125
        q_t = jnp.transpose(queries).astype(BF16)
        do_t = jnp.transpose(db[rows, :].astype(F32))
        at_k = low + lax.broadcasted_iota(jnp.int32, (512, 256), 0)
        at_q = row + lax.broadcasted_iota(jnp.int32, (512, 256), 1)
        near = jnp.where(at_q >= at_k, nn(kb[low:width, :], q_t), -1e30)
        top = jnp.max(near, axis=0, keepdims=True)
        if j:
            away = nn(kb[0:low, :], q_t)
            top = jnp.maximum(top, jnp.max(away, axis=0, keepdims=True))
        near = jnp.exp(near - top)
        total = jnp.sum(near, axis=0, keepdims=True)
        probs = near.astype(BF16)
        if j:
            away = jnp.exp(away - top)
            total = total + jnp.sum(away, axis=0, keepdims=True)
            probs = jnp.concatenate([away.astype(BF16), probs], axis=0)
        scale = 1.0 / total
        att_t = nn(vt_b[:, 0:width], probs) * scale
        do_t = (do_t * scale).astype(BF16).astype(F32)
        delta = jnp.sum(do_t * att_t, axis=0, keepdims=True)
        high = delta.astype(BF16).astype(F32)
        tail = lax.broadcasted_iota(jnp.int32, (8, 256), 0)
        tail = jnp.where(tail == 0, -high, jnp.where(tail == 1, high - delta, 0.0))
        right = jnp.concatenate([do_t, tail, jnp.zeros((56, 256), F32)], axis=0).astype(BF16)
        d_s = (probs.astype(F32) * nn(vb[0:width, :], right)).astype(BF16)
        blocks = pl.ds(8 * j + 4 * turn_off, 4)
        blank = pl.ds(8 * j + 4 * (1 - turn_off), 4)
        att_b[blocks] = jnp.transpose(att_t).reshape(4, 64, 64)
        dq_b[blocks] = jnp.transpose(nn(kt_b[:, 0:width], d_s) * 0.125).reshape(4, 64, 64)
        att_b[blank] = jnp.zeros((4, 64, 64), F32)
        dq_b[blank] = jnp.zeros((4, 64, 64), F32)
        d_k = nn(d_s, queries.astype(BF16)).reshape(8 * (j + 1), 64, 64)
        d_v = nn(probs, jnp.transpose(do_t).astype(BF16)).reshape(8 * (j + 1), 64, 64)
        if j == 3:
            dk_b[...] = d_k
            dv_b[...] = d_v
        else:
            dk_b[0 : 8 * (j + 1)] += d_k
            dv_b[0 : 8 * (j + 1)] += d_v

    tile(3)
    for p in LATER:
        reduce_step(p, 2)
    for j in (2, 1, 0):
        tile(j)
    for i in range(32):
        t = table[i]
        zs[i] = jnp.concatenate([att_b[t], dq_b[t], dk_b[t], dv_b[t]], axis=1).astype(BF16)

    order = (1, 2, 3, 4, 5, 6, 7, 0)
    halves, collect = {}, []
    for delta in order:
        m, _ = head_at[delta]
        halves[delta] = send(
            zs.at[spot(1 - core, m)], crecv.at[m], cfs.at[delta], cfr.at[delta], sibling
        )
    started += list(halves.values())
    mlp_s[...] = nn(g_s[...], wd[...])
    for delta in order:
        m, peer = head_at[delta]
        halves[delta].wait_recv()
        ctotal[m] = zs[spot(core, m)] + crecv[m]
        if delta:
            collect.append(
                send(ctotal.at[m], back.at[me], cos_.at[delta - 1], cor_.at[delta - 1], peer)
            )
        else:
            back[me] = ctotal[m]
    started += collect
    for p in LATER:
        reduce_step(p, 1)
    dh2_s[...] = nt(dup_s[...], wu[...])
    dh2 = dh2_s[...]
    gvec[2:3, 0:512] = jnp.sum(dh2 * xhat[...], axis=0, keepdims=True)
    gvec[3:4, 0:512] = jnp.sum(dh2, axis=0, keepdims=True)
    gvec[6:7, 0:512] = jnp.sum(dy.astype(F32), axis=0, keepdims=True)
    settle()
    for copy in collect:
        copy.wait_recv()

    def whole(i):
        return jnp.concatenate(
            [
                jnp.concatenate(
                    [back[h, 0, :, 64 * i : 64 * i + 64], back[h, 1, :, 64 * i : 64 * i + 64]],
                    axis=0,
                )
                for h in range(8)
            ],
            axis=1,
        )

    dqkv_s[:, 0:512] = turn(whole(1).astype(F32), -1.0).astype(BF16)
    dqkv_s[:, 512:1024] = turn(whole(2).astype(F32), -1.0).astype(BF16)
    dqkv_s[:, 1024:1536] = whole(3)
    mixed = whole(0)
    ga[:, 1536:2048] = tn(mixed, dy).astype(BF16)
    for t in range(3):
        ga[:, 512 * t : 512 * (t + 1)] = tn(
            h1_s[...], dqkv_s[:, 512 * t : 512 * (t + 1)]
        ).astype(BF16)
    wide_loop(FIRST_PIECES, pack_from(ga))
    for p in FIRST:
        reduce_start(p)
    dh1 = nt(dqkv_s[...], wa[:, 0:1536])
    gvec[0:1, 0:512] = jnp.sum(dh1 * xhat[...], axis=0, keepdims=True)
    gvec[1:2, 0:512] = jnp.sum(dh1, axis=0, keepdims=True)
    gvec[4:5, 0:1024] = jnp.sum(dqkv_s[:, 0:1024].astype(F32), axis=0, keepdims=True)
    gvec[5:6, 0:512] = jnp.sum(dqkv_s[:, 1024:1536].astype(F32), axis=0, keepdims=True)
    for p in FIRST:
        reduce_step(p, 2)
    spread_out = jnp.zeros((128, 128), F32)
    left = 0
    for i, (n, off) in enumerate(SECTIONS_OUT):
        cols = slice(left, left + 128 * n)
        left += 128 * n
        value = gvec[i : i + 1, 0 : 128 * n]
        high = value.astype(BF16)
        low = (value - high.astype(F32)).astype(BF16)
        pick, own = pick_out[:, cols], own_out[:, cols]
        spread_out = spread_out + nt(own * high, pick) + nt(own * low, pick)
    gmat[...] = spread_out
    grads[SMALL][...] = jnp.zeros_like(grads[SMALL])

    def small_grads(z, low, t, where, c):
        row = gmat[pl.ds(z * 32 + (low * 4 + t), 1), :]
        grads[SMALL][c, slot_of(SMALL, where), 0:1, :] = row

    each_device(small_grads)
    reduce_start(SMALL)
    result = hid[0].astype(F32) + nn(mixed, wa[:, 1536:2048]) + mlp_s[...] + vecs[5:6, 0:512]
    out_ref[0] = result.astype(BF16)
    reduce_step(SMALL, 2)
    d_norm = dh1 * vecs[0:1, 0:512] + dh2_s[...] * vecs[2:3, 0:512]
    normed = xhat[...]
    d_x = d_norm - jnp.mean(d_norm, axis=1, keepdims=True)
    d_x = d_x - normed * jnp.mean(d_norm * normed, axis=1, keepdims=True)
    ingrad_ref[0] = dy.astype(F32) + d_x * inv_s[:, 0:1]
    for p in LATER:
        reduce_step(p, 0)
    for p in FIRST + (SMALL,):
        reduce_step(p, 1)
    for p in LATER:
        value = reduce_end(p)
        for p_of, left, cols, there in UP_PIECES:
            if p_of == p:
                asm2[:, 512 + there : 512 + there + cols] = value[:, left : left + cols]
        for p_of, left, cols, there in DOWN_PIECES:
            if p_of == p:
                gdown_ref[:, there : there + cols] = value[:, left : left + cols]
    for p in FIRST + (SMALL,):
        reduce_step(p, 0)
    for p, _, cols, there in FIRST_PIECES:
        asm2[:, there : there + cols] = reduce_end(p)
    gsmall_ref[...] = reduce_end(SMALL)
    squad2[...] = jnp.zeros_like(squad2)
    for t in range(4):
        squad2[t, 0:4, :] = asm2[4 * t : 4 * t + 4, :]
    quad = []
    for peer, delta in quad_peers:
        quad.append(
            send(
                squad2.at[quad_index(delta)], rquad2.at[q], q2s.at[delta - 1], q2r.at[delta - 1],
                peer,
            )
        )
    rquad2[q] = squad2[q]
    settle()
    for copy in quad:
        copy.wait_recv()
    for t in range(3):
        gqkv_ref[:, 512 * t : 512 * (t + 1)] = rquad2[t, 0:4, 0:512]
    gproj_ref[...] = rquad2[3, 0:4, 0:512]
    for t in range(4):
        gup_ref[:, 512 * t : 512 * (t + 1)] = rquad2[t, 0:4, 512:1024]
    for copy in quad:
        copy.wait_send()


def run_block(*args):
    dma = pltpu.SemaphoreType.DMA
    scratch = [VMEM((2, 64) + tile, dtype) for tile, dtype in GATHERED]
    scratch += [VMEM((2, 64) + tile, dtype) for tile, dtype in TILES]
    scratch += [VMEM((128,) + tile, dtype) for tile, dtype in TILES]
    scratch += [VMEM((4, 8, 1024), F32)] * 4 + [VMEM((16, 1024), F32)] * 2
    scratch += [VMEM((512, 2048), BF16), VMEM((512, 2048), BF16), VMEM((2048, 512), BF16)] * 2
    scratch += [VMEM((128, 128), F32)] * 2
    scratch += [VMEM((8, 2, 64, 256), BF16), VMEM((32, 64, 256), BF16), VMEM((32, 64, 256), BF16)]
    scratch += [VMEM((8, 2, 64, 256), BF16)] * 3
    scratch += [VMEM((2048, 64), BF16)] * 2 + [VMEM((2048, 128), BF16), VMEM((2048, 64), BF16)]
    scratch += [VMEM((32, 64, 64), F32)] * 4
    scratch += [VMEM((128, 512), F32)] + [VMEM((128, 128), F32)] * 3 + [VMEM((8, 2048), F32)] * 2
    scratch += [VMEM((128, 512), BF16)] * 2 + [VMEM((128, 2048), BF16)] * 2
    scratch += [VMEM((128, 512), F32)] * 2 + [VMEM((128, 1536), BF16)]
    scratch += [dma((3,))] * 4 + [dma((N, 9))] * 2 + [dma((N,))] * 2 + [dma((N, 10))] * 2
    scratch += [dma((7,)), dma((7,)), dma((8,)), dma((8,))] * 2
    scratch += [VMEM((128, 6144), BF16)] * 4 + [VMEM((64, 2048), BF16)] * 2
    shape = jax.ShapeDtypeStruct
    return pl.pallas_call(
        block_kernel,
        out_shape=(
            shape((1, 128, 512), BF16), shape((1, 128, 512), F32), shape((4, 1536), F32),
            shape((4, 512), F32), shape((4, 2048), F32), shape((16, 512), F32), shape((8, 128), F32),
        ),
        in_specs=[pl.BlockSpec(memory_space=pltpu.SMEM)] + [pl.BlockSpec(memory_space=VMEM)] * 9,
        out_specs=[pl.BlockSpec(memory_space=VMEM)] * 7,
        scratch_shapes=scratch,
        compiler_params=pltpu.CompilerParams(
            collective_id=0, has_side_effects=True, vmem_limit_bytes=LIMIT
        ),
    )(*args)


def finish_kernel(*refs):
    for src, dst in zip(refs[:6], refs[7:13]):
        dst[...] = src[...]
    row = refs[6][0:1, :]
    for (n, off), dst in zip(SECTIONS_OUT, refs[13:]):
        dst[...] = row[:, off : off + n]


def finish(*parts):
    shape = jax.ShapeDtypeStruct
    return pl.pallas_call(
        finish_kernel,
        out_shape=tuple(shape(part.shape, part.dtype) for part in parts[:6])
        + tuple(shape((1, n), F32) for n, _ in SECTIONS_OUT),
        in_specs=[pl.BlockSpec(memory_space=VMEM)] * 7,
        out_specs=[pl.BlockSpec(memory_space=VMEM)] * 14,
    )(*parts)


def per_device(
    hidden_in, positions, block_order, norm1_gain, norm1_bias, norm2_gain, norm2_bias,
    qkv_weight, qkv_bias, attn_out_weight, out_bias, up_weight, up_bias, down_weight, out_grad,
):
    small = jnp.concatenate(
        [norm1_gain, norm1_bias, norm2_gain, norm2_bias, qkv_bias, out_bias, up_bias]
    )
    small = jnp.pad(small[None], ((0, 15), (0, 80)))
    held = block_order.reshape(8, 2, 2).transpose(1, 0, 2).reshape(32)
    ids = jnp.arange(32, dtype=jnp.int32)
    inverse = jnp.sum(jnp.where(held[:, None] == ids[None, :], ids[:, None], 0), axis=0)
    table = jnp.concatenate([held, inverse])
    freqs = 10000.0 ** (-np.arange(8, dtype=np.float32) * np.float32(2.0) / np.float32(16))
    lanes = np.concatenate([freqs, freqs, np.zeros(48)]).astype(np.float32)
    freq = jnp.asarray(np.concatenate([lanes, lanes])[None])
    parts = run_block(
        table, hidden_in, out_grad, positions, freq, small,
        qkv_weight, attn_out_weight, up_weight, down_weight,
    )
    done = finish(*parts)
    block_out, input_grad, g_qkv, g_proj, g_up, g_down = done[:6]
    n1g, n1b, n2g, n2b, qk, val, out, up = (item.reshape(-1) for item in done[6:])
    return (
        block_out, input_grad, n1g, n1b, n2g, n2b, g_qkv, qk, val, g_proj, out, g_up, up, g_down,
    )


def solution(mesh):
    both = ("dp", "ctx")
    rows, vec, mat = P("dp", "ctx", None), P(both), P(both, None)
    return jax.shard_map(
        per_device,
        mesh=mesh,
        in_specs=(
            rows, P("dp", "ctx"), P(), vec, vec, vec, vec, mat, vec, mat, vec, mat, vec, mat, rows,
        ),
        out_specs=(
            rows, rows, vec, vec, vec, vec, mat, vec, vec, mat, vec, mat, vec, mat,
        ),
        check_vma=False,
    )
```

```python
import jax
import jax.numpy as jnp
import numpy as np
from jax import lax
from jax.experimental import pallas as pl
from jax.experimental.pallas import tpu as pltpu
from jax.sharding import PartitionSpec as P

EPS = 1e-05
MESH = pl.DeviceIdType.MESH
F32 = jnp.float32
BF16 = jnp.bfloat16
VMEM = pltpu.VMEM
LIMIT = 60 * 1024 * 1024

ORDERS = ((0, 1, 2), (1, 2, 0), (2, 0, 1))
ORDER_OF = (0, 1, 2, 1, 0, 1, 2)
N = 7
FIRST, SMALL, LATER = (0, 1, 2), 3, (4, 5, 6)
TILES = [((16, c), BF16) for c in (256, 128, 128, 0, 384, 256, 384)]
TILES[SMALL] = ((8, 128), F32)
GATHERED = list(TILES)
GATHERED[1] = ((16, 256), BF16)
FIRST_PIECES = ((0, 0, 256, 0), (1, 0, 128, 256), (2, 0, 128, 384))
UP_PIECES = ((4, 0, 384, 0), (5, 0, 128, 384))
DOWN_PIECES = ((5, 128, 128, 0), (6, 0, 384, 128))
SECTIONS_IN = ((4, 0), (4, 4), (4, 8), (4, 12), (12, 16), (4, 28), (16, 32))
SECTIONS_OUT = ((4, 0), (4, 4), (4, 8), (4, 12), (8, 16), (4, 24), (4, 28), (16, 32))


def device_of(x, y, z, core):
    return (z * 2 + lax.rem(x, 2), y * 4 + lax.div(x, 2) * 2 + core)


def slot_of(p, at):
    return sum(at[axis] * 4**k for k, axis in enumerate(ORDERS[ORDER_OF[p]]))


def moved(at, axis, delta):
    at = list(at)
    at[axis] = lax.rem(at[axis] + delta, 4)
    return at


def send(src, dst, ssem, rsem, peer):
    copy = pltpu.make_async_remote_copy(
        src_ref=src, dst_ref=dst, send_sem=ssem, recv_sem=rsem, device_id=peer, device_id_type=MESH
    )
    copy.start()
    return copy


def nt(a, b):
    return lax.dot_general(a, b, (((1,), (1,)), ((), ())), preferred_element_type=F32)


def nn(a, b):
    return lax.dot_general(a, b, (((1,), (0,)), ((), ())), preferred_element_type=F32)


def tn(a, b):
    return lax.dot_general(a, b, (((0,), (0,)), ((), ())), preferred_element_type=F32)


def selectors(n, off):
    cols = lax.broadcasted_iota(jnp.int32, (1, 128 * n), 1)
    owner = ((cols.astype(F32) + 0.5) * (1.0 / n)).astype(jnp.int32)
    lane = cols - owner * n + off
    rows = lax.broadcasted_iota(jnp.int32, (128, 128 * n), 0)
    pick = jnp.where(rows == lane, 1.0, 0.0).astype(BF16)
    return pick, jnp.where(rows == owner, 1.0, 0.0).astype(BF16)


def swap_halves(u):
    lane = lax.broadcasted_iota(jnp.int32, u.shape, 1)
    lane = lane - 64 * (lane >= 64).astype(jnp.int32)
    return jnp.where(lane < 8, pltpu.roll(u, 120, 1), pltpu.roll(u, 8, 1))


def block_kernel(
    table, hid, dy_ref, pos, freq, small, w_qkv, w_proj, w_upper, w_lower,
    out_ref, ingrad_ref, gqkv_ref, gproj_ref, gup_ref, gdown_ref, gsmall_ref,
    *rest,
):
    rest = list(rest)

    def take(count):
        got = rest[:count]
        del rest[:count]
        return got

    bufs, grads, recv = take(N), take(N), take(N)
    squad, rquad, squad2, rquad2, asm, asm2 = take(6)
    wa, wu, wd, ga, gu, gd, smat, gmat = take(8)
    xs, ys, zs, crecv, ctotal, back = take(6)
    qb, kb, vb, db, att_b, dq_b, dk_b, dv_b = take(8)
    xhat, inv_s, cos_s, sin_s, vecs, gvec, h1_s, h2_s, g_s, dup_s, mlp_s, dh2_s, dqkv_s = take(13)
    qs, qr, q2s, q2r, ags, agr, fws, fwr, rss, rsr, sps, spr, sfs, sfr = take(14)
    cos_, cor_, cfs, cfr = take(4)
    pick_in, own_in, pick_out, own_out, kt_b, vt_b = take(6)

    dp, ctx = lax.axis_index("dp"), lax.axis_index("ctx")
    core = lax.rem(ctx, 2)
    at = [
        lax.rem(lax.div(ctx, 2), 2) * 2 + lax.rem(dp, 2), lax.div(ctx, 4), lax.div(dp, 2)
    ]
    sibling = device_of(*at, 1 - core)
    q = lax.rem(ctx, 4)
    axis_peers = [
        [device_of(*moved(at, axis, delta), core) for delta in (1, 2, 3)] for axis in range(3)
    ]
    far = moved(at, 0, 2)
    far_cross = device_of(*far, 1 - core)
    head_at = []
    for delta in range(8):
        place = moved(far if delta % 2 else at, 1, delta // 2)
        head_at.append((place[1] * 2 + lax.div(place[0], 2), device_of(*place, core)))
    me = head_at[0][0]
    quad_peers = [(sibling, 1), (head_at[1][1], 2), (far_cross, 3)]

    def quad_index(delta):
        core_t = 1 - core if delta % 2 else core
        hi = lax.div(at[0], 2)
        return (1 - hi if delta // 2 else hi) * 2 + core_t

    everyone = [sibling, far_cross] + sum(axis_peers, [])
    everyone += [head_at[delta][1] for delta in (3, 5, 7)]
    barrier = pltpu.get_barrier_semaphore()
    for peer in everyone:
        pl.semaphore_signal(barrier, inc=1, device_id=peer, device_id_type=MESH)

    slots = [slot_of(p, at) for p in range(N)]
    started = []

    def settle():
        while started:
            started.pop(0).wait_send()

    squad[...] = jnp.zeros_like(squad)
    qkv_rows = w_qkv[...].astype(F32)
    up_rows = w_upper[...].astype(F32)
    for t in range(3):
        squad[t, 0:4, 0:512] = qkv_rows[:, 512 * t : 512 * (t + 1)]
    squad[3, 0:4, 0:512] = w_proj[...].astype(F32)
    for t in range(4):
        squad[t, 0:4, 512:1024] = up_rows[:, 512 * t : 512 * (t + 1)]
    for p, left, cols, there in DOWN_PIECES:
        bufs[p][core, slots[p], :, left : left + cols] = w_lower[:, there : there + cols]
    bufs[1][core, slots[1], :, 128:256] = small[...]
    x = hid[0].astype(F32)
    center = x - jnp.mean(x, axis=1, keepdims=True)
    inv = lax.rsqrt(jnp.mean(center * center, axis=1, keepdims=True) + EPS)
    xhat[...] = center * inv
    inv_s[...] = jnp.broadcast_to(inv, (128, 128))
    places = jnp.transpose(jnp.broadcast_to(pos[...].astype(F32), (128, 128)))
    angle = places * freq[...]
    lane = lax.broadcasted_iota(jnp.int32, (128, 128), 1)
    lane = lane - 64 * (lane >= 64).astype(jnp.int32)
    sine = jnp.sin(angle)
    cos_s[...] = jnp.cos(angle)
    sin_s[...] = jnp.where(lane < 8, -sine, sine)
    pl.semaphore_wait(barrier, len(everyone))

    quad = []
    for peer, delta in quad_peers:
        quad.append(
            send(squad.at[quad_index(delta)], rquad.at[q], qs.at[delta - 1], qr.at[delta - 1], peer)
        )
    started += quad
    rquad[q] = squad[q]
    hops, fwd = {}, {}

    def block(p, k):
        size = 4**k
        return lax.div(slots[p], size) * size, size

    def gather_send(p, k):
        base, size = block(p, k)
        axis = ORDERS[ORDER_OF[p]][k]
        part = bufs[p].at[core, pl.ds(base, size)]
        for d in range(3):
            hops[p, k, d] = send(
                part, part, ags.at[p, 3 * k + d], agr.at[p, 3 * k + d], axis_peers[axis][d]
            )
            started.append(hops[p, k, d])

    def gather_wait(p, k):
        for d in range(3):
            hops[p, k, d].wait_recv()

    def gather_forward(p):
        gather_wait(p, 2)
        plane = bufs[p].at[core]
        fwd[p] = send(plane, plane, fws.at[p], fwr.at[p], sibling)
        started.append(fwd[p])

    def gather_done(p):
        fwd[p].wait_recv()

    gather_send(6, 0)
    for copy in quad:
        copy.wait_recv()
    for t in range(4):
        asm[4 * t : 4 * t + 4, :] = rquad[t, 0:4, :]
    for p, left, cols, there in FIRST_PIECES + UP_PIECES:
        there = there if p < 3 else there + 512
        bufs[p][core, slots[p], :, left : left + cols] = asm[:, there : there + cols].astype(BF16)
        gather_send(p, 0)

    def build(sections, picks, owns):
        left = 0
        for n, off in sections:
            pick, own = selectors(n, off)
            picks[:, left : left + 128 * n] = pick
            owns[:, left : left + 128 * n] = own
            left += 128 * n

    build(SECTIONS_IN, pick_in, own_in)
    for p in FIRST + LATER:
        gather_wait(p, 0)
        gather_send(p, 1)
    build(SECTIONS_OUT, pick_out, own_out)
    for p in FIRST:
        gather_wait(p, 1)
        gather_send(p, 2)
    for p in FIRST:
        gather_forward(p)
    for p in LATER:
        gather_wait(p, 1)
        gather_send(p, 2)

    def each_device(step):
        def body(z, carry):
            for low in range(8):
                for t in range(4):
                    step(z, low, t, [(t // 2) * 2 + low // 4, low % 4, z], t % 2)
            return carry

        lax.fori_loop(0, 4, body, 0)

    def wide_loop(pieces, store):
        def step(z, low, t, where, c):
            rows = pl.ds(pl.multiple_of(z * 128 + low * 16, 16), 16)
            for p, left, cols, there in pieces:
                store(p, c, slot_of(p, where), rows, left, cols, 512 * t + there)

        each_device(step)

    def tall_loop(store):
        def step(z, low, t, where, c):
            rows = pl.ds(pl.multiple_of(z * 512 + low * 64 + t * 16, 16), 16)
            for p, left, cols, there in DOWN_PIECES:
                store(p, c, slot_of(p, where), rows, left, cols, there)

        each_device(step)

    def unpack_to(dst):
        def store(p, c, slot, rows, left, cols, there):
            dst[rows, there : there + cols] = bufs[p][c, slot, :, left : left + cols]

        return store

    def pack_from(src):
        def store(p, c, slot, rows, left, cols, there):
            grads[p][c, slot, :, left : left + cols] = src[rows, there : there + cols]

        return store

    gather_done(1)

    def small_rows(z, low, t, where, c):
        tile = bufs[1][c, slot_of(1, where), :, 128:256].astype(F32)
        smat[pl.ds(z * 32 + (low * 4 + t), 1), :] = tile[0:1]

    each_device(small_rows)
    tiles = smat[...].astype(BF16)

    def vectors(wanted):
        for i in wanted:
            n = SECTIONS_IN[i][0]
            left = 128 * sum(m for m, _ in SECTIONS_IN[:i])
            cols = slice(left, left + 128 * n)
            vecs[i : i + 1, 0 : 128 * n] = jnp.sum(
                own_in[:, cols].astype(F32) * nn(tiles, pick_in[:, cols]), axis=0, keepdims=True
            )

    vectors((0, 1, 4))
    normed = xhat[...]
    h1_s[...] = (normed * vecs[0:1, 0:512] + vecs[1:2, 0:512]).astype(BF16)
    for p in (0, 2):
        gather_done(p)
    wide_loop(FIRST_PIECES, unpack_to(wa))

    dy = dy_ref[0]
    parts = [nn(h1_s[...], wa[:, 512 * i : 512 * (i + 1)]) for i in range(3)]
    parts = [parts[i] + vecs[4:5, 512 * i : 512 * (i + 1)] for i in range(3)]
    cos_t, sin_t = cos_s[...], sin_s[...]

    def turn(u, sign):
        return jnp.concatenate(
            [
                u[:, c : c + 128] * cos_t + swap_halves(u[:, c : c + 128]) * (sin_t * sign)
                for c in range(0, 512, 128)
            ],
            axis=1,
        )

    sent = [turn(parts[0], 1.0), turn(parts[1], 1.0), parts[2], nt(dy, wa[:, 1536:2048])]
    sent = [item.astype(BF16) for item in sent]
    for h in range(8):
        piece = jnp.concatenate([item[:, 64 * h : 64 * h + 64] for item in sent], axis=1)
        xs[h, 0] = piece[0:64]
        xs[h, 1] = piece[64:128]
    spread, spread_fwd = [], []

    def spot(c, m):
        return pl.ds(c * 16 + m * 2, 2)

    for delta in range(1, 8):
        m, peer = head_at[delta]
        spread.append(
            send(xs.at[m], ys.at[spot(core, me)], sps.at[delta - 1], spr.at[delta - 1], peer)
        )
    ys[spot(core, me)] = xs[me]
    mine = ys.at[spot(core, me)]
    spread_fwd.append(send(mine, mine, sfs.at[0], sfr.at[0], sibling))

    for p in LATER:
        gather_forward(p)
    vectors((2, 3, 5, 6))
    h2_s[...] = (xhat[...] * vecs[2:3, 0:512] + vecs[3:4, 0:512]).astype(BF16)
    for p in LATER:
        gather_done(p)
    wide_loop(UP_PIECES, unpack_to(wu))
    tall_loop(unpack_to(wd))

    def mlp(t):
        cols = slice(512 * t, 512 * (t + 1))
        up = nn(h2_s[...], wu[:, cols]) + vecs[6:7, cols]
        cdf = 0.5 * (1.0 + lax.erf(up * np.float32(0.5**0.5)))
        pdf = jnp.exp(-0.5 * up * up) * np.float32((2 * np.pi) ** -0.5)
        g = (up * cdf).astype(BF16)
        d_up = (nt(dy, wd[cols, :]) * (cdf + up * pdf)).astype(BF16)
        g_s[:, cols] = g
        dup_s[:, cols] = d_up
        gvec[7:8, cols] = jnp.sum(d_up.astype(F32), axis=0, keepdims=True)
        gu[:, cols] = tn(h2_s[...], d_up).astype(BF16)
        gd[cols, :] = tn(g, dy).astype(BF16)

    for t in range(4):
        mlp(t)
        if t == 1:
            for delta in range(1, 8):
                back_y = (4 - delta // 2) % 4
                m = head_at[back_y * 2 + delta % 2][0]
                spread[delta - 1].wait_recv()
                part = ys.at[spot(core, m)]
                spread_fwd.append(send(part, part, sfs.at[delta], sfr.at[delta], sibling))
    started += spread + spread_fwd

    adds = {}

    def reduce_start(p):
        adds[p, 3] = send(
            grads[p].at[1 - core], recv[p].at[pl.ds(0, 64)], rss.at[p, 9], rsr.at[p, 9], sibling
        )
        started.append(adds[p, 3])

    def offset(k):
        return 64 + {2: 0, 1: 48, 0: 60}[k]

    def reduce_step(p, k):
        if k == 2:
            adds[p, 3].wait_recv()
            total, others, base = 64, (0,), 0
        else:
            for d in range(3):
                adds[p, k + 1, d].wait_recv()
            base, total = block(p, k + 1)
            others = [offset(k + 1) + d * total for d in range(3)]
        unit = min(total, 8 if len(others) == 1 else 4)

        def body(i, carry):
            here = pl.ds(base + i * unit, unit)
            if len(others) == 1:
                grads[p][core, here] += recv[p][pl.ds(others[0] + i * unit, unit)]
                return carry
            value = grads[p][core, here].astype(F32)
            for other in others:
                value = value + recv[p][pl.ds(other + i * unit, unit)].astype(F32)
            grads[p][core, here] = value.astype(grads[p].dtype)
            return carry

        lax.fori_loop(0, total // unit, body, 0)
        axis = ORDERS[ORDER_OF[p]][k]
        size = 4**k
        own, _ = block(p, k)
        for d in range(3):
            there = lax.rem(at[axis] + d + 1, 4)
            part = grads[p].at[core, pl.ds(own + (there - at[axis]) * size, size)]
            adds[p, k, d] = send(
                part, recv[p].at[pl.ds(offset(k) + d * size, size)],
                rss.at[p, 3 * k + d], rsr.at[p, 3 * k + d], axis_peers[axis][d],
            )
            started.append(adds[p, k, d])

    def reduce_end(p):
        for d in range(3):
            adds[p, 0, d].wait_recv()
        value = grads[p][core, slots[p]].astype(F32)
        for d in range(3):
            value = value + recv[p][offset(0) + d].astype(F32)
        return value

    wide_loop(UP_PIECES, pack_from(gu))
    tall_loop(pack_from(gd))
    for p in LATER:
        reduce_start(p)

    for copy in spread_fwd:
        copy.wait_recv()
    ones = jnp.where(lax.broadcasted_iota(jnp.int32, (64, 64), 1) < 2, 1.0, 0.0).astype(BF16)
    for t in range(32):
        part = ys[table[32 + t]]
        rows = slice(64 * t, 64 * t + 64)
        qb[rows, :] = part[:, 0:64]
        kb[rows, :] = part[:, 64:128]
        vb[rows, :] = jnp.concatenate([part[:, 128:192], ones], axis=1)
        db[rows, :] = part[:, 192:256]
    kt_b[...] = jnp.transpose(kb[...].astype(F32)).astype(BF16)
    vt_b[...] = jnp.transpose(vb[:, 0:64].astype(F32)).astype(BF16)

    def tile(j):
        low, width = 512 * j, 512 * (j + 1)
        turn_off = 1 - core if j % 2 else core
        row = low + 256 * turn_off
        rows = pl.ds(pl.multiple_of(row, 256), 256)
        queries = qb[rows, :].astype(F32) * 0.125
        q_t = jnp.transpose(queries).astype(BF16)
        do_t = jnp.transpose(db[rows, :].astype(F32))
        at_k = low + lax.broadcasted_iota(jnp.int32, (512, 256), 0)
        at_q = row + lax.broadcasted_iota(jnp.int32, (512, 256), 1)
        near = jnp.where(at_q >= at_k, nn(kb[low:width, :], q_t), -1e30)
        top = jnp.max(near, axis=0, keepdims=True)
        if j:
            away = nn(kb[0:low, :], q_t)
            top = jnp.maximum(top, jnp.max(away, axis=0, keepdims=True))
        near = jnp.exp(near - top)
        total = jnp.sum(near, axis=0, keepdims=True)
        probs = near.astype(BF16)
        if j:
            away = jnp.exp(away - top)
            total = total + jnp.sum(away, axis=0, keepdims=True)
            probs = jnp.concatenate([away.astype(BF16), probs], axis=0)
        scale = 1.0 / total
        att_t = nn(vt_b[:, 0:width], probs) * scale
        do_t = (do_t * scale).astype(BF16).astype(F32)
        delta = jnp.sum(do_t * att_t, axis=0, keepdims=True)
        high = delta.astype(BF16).astype(F32)
        tail = lax.broadcasted_iota(jnp.int32, (8, 256), 0)
        tail = jnp.where(tail == 0, -high, jnp.where(tail == 1, high - delta, 0.0))
        right = jnp.concatenate([do_t, tail, jnp.zeros((56, 256), F32)], axis=0).astype(BF16)
        d_s = (probs.astype(F32) * nn(vb[0:width, :], right)).astype(BF16)
        blocks = pl.ds(8 * j + 4 * turn_off, 4)
        blank = pl.ds(8 * j + 4 * (1 - turn_off), 4)
        att_b[blocks] = jnp.transpose(att_t).reshape(4, 64, 64)
        dq_b[blocks] = jnp.transpose(nn(kt_b[:, 0:width], d_s) * 0.125).reshape(4, 64, 64)
        att_b[blank] = jnp.zeros((4, 64, 64), F32)
        dq_b[blank] = jnp.zeros((4, 64, 64), F32)
        d_k = nn(d_s, queries.astype(BF16)).reshape(8 * (j + 1), 64, 64)
        d_v = nn(probs, jnp.transpose(do_t).astype(BF16)).reshape(8 * (j + 1), 64, 64)
        if j == 3:
            dk_b[...] = d_k
            dv_b[...] = d_v
        else:
            dk_b[0 : 8 * (j + 1)] += d_k
            dv_b[0 : 8 * (j + 1)] += d_v

    tile(3)
    for p in LATER:
        reduce_step(p, 2)
    for j in (2, 1, 0):
        tile(j)
    for i in range(32):
        t = table[i]
        zs[i] = jnp.concatenate([att_b[t], dq_b[t], dk_b[t], dv_b[t]], axis=1).astype(BF16)

    order = (1, 2, 3, 4, 5, 6, 7, 0)
    halves, collect = {}, []
    for delta in order:
        m, _ = head_at[delta]
        halves[delta] = send(
            zs.at[spot(1 - core, m)], crecv.at[m], cfs.at[delta], cfr.at[delta], sibling
        )
    started += list(halves.values())
    mlp_s[...] = nn(g_s[...], wd[...])
    for delta in order:
        m, peer = head_at[delta]
        halves[delta].wait_recv()
        ctotal[m] = zs[spot(core, m)] + crecv[m]
        if delta:
            collect.append(
                send(ctotal.at[m], back.at[me], cos_.at[delta - 1], cor_.at[delta - 1], peer)
            )
        else:
            back[me] = ctotal[m]
    settle()
    started += collect
    for p in LATER:
        reduce_step(p, 1)
    dh2_s[...] = nt(dup_s[...], wu[...])
    dh2 = dh2_s[...]
    gvec[2:3, 0:512] = jnp.sum(dh2 * xhat[...], axis=0, keepdims=True)
    gvec[3:4, 0:512] = jnp.sum(dh2, axis=0, keepdims=True)
    gvec[6:7, 0:512] = jnp.sum(dy.astype(F32), axis=0, keepdims=True)
    grads[SMALL][...] = jnp.zeros_like(grads[SMALL])

    def laid_out(wanted):
        result = jnp.zeros((128, 128), F32)
        for i in wanted:
            n = SECTIONS_OUT[i][0]
            left = 128 * sum(m for m, _ in SECTIONS_OUT[:i])
            cols = slice(left, left + 128 * n)
            value = gvec[i : i + 1, 0 : 128 * n]
            high = value.astype(BF16)
            low = (value - high.astype(F32)).astype(BF16)
            pick, own = pick_out[:, cols], own_out[:, cols]
            result = result + nt(own * high, pick) + nt(own * low, pick)
        return result

    gmat[...] = laid_out((2, 3, 6, 7))
    for copy in collect:
        copy.wait_recv()

    def whole(i):
        return jnp.concatenate(
            [
                jnp.concatenate(
                    [back[h, 0, :, 64 * i : 64 * i + 64], back[h, 1, :, 64 * i : 64 * i + 64]],
                    axis=0,
                )
                for h in range(8)
            ],
            axis=1,
        )

    dqkv_s[:, 0:512] = turn(whole(1).astype(F32), -1.0).astype(BF16)
    dqkv_s[:, 512:1024] = turn(whole(2).astype(F32), -1.0).astype(BF16)
    dqkv_s[:, 1024:1536] = whole(3)
    mixed = whole(0)
    ga[:, 1536:2048] = tn(mixed, dy).astype(BF16)
    for t in range(3):
        ga[:, 512 * t : 512 * (t + 1)] = tn(
            h1_s[...], dqkv_s[:, 512 * t : 512 * (t + 1)]
        ).astype(BF16)
    wide_loop(FIRST_PIECES, pack_from(ga))
    for p in FIRST:
        reduce_start(p)
    dh1 = nt(dqkv_s[...], wa[:, 0:1536])
    gvec[0:1, 0:512] = jnp.sum(dh1 * xhat[...], axis=0, keepdims=True)
    gvec[1:2, 0:512] = jnp.sum(dh1, axis=0, keepdims=True)
    gvec[4:5, 0:1024] = jnp.sum(dqkv_s[:, 0:1024].astype(F32), axis=0, keepdims=True)
    gvec[5:6, 0:512] = jnp.sum(dqkv_s[:, 1024:1536].astype(F32), axis=0, keepdims=True)
    for p in FIRST:
        reduce_step(p, 2)
    gmat[...] += laid_out((0, 1, 4, 5))

    def small_grads(z, low, t, where, c):
        row = gmat[pl.ds(z * 32 + (low * 4 + t), 1), :]
        grads[SMALL][c, slot_of(SMALL, where), 0:1, :] = row

    each_device(small_grads)
    reduce_start(SMALL)
    result = hid[0].astype(F32) + nn(mixed, wa[:, 1536:2048]) + mlp_s[...] + vecs[5:6, 0:512]
    out_ref[0] = result.astype(BF16)
    reduce_step(SMALL, 2)
    d_norm = dh1 * vecs[0:1, 0:512] + dh2_s[...] * vecs[2:3, 0:512]
    normed = xhat[...]
    d_x = d_norm - jnp.mean(d_norm, axis=1, keepdims=True)
    d_x = d_x - normed * jnp.mean(d_norm * normed, axis=1, keepdims=True)
    ingrad_ref[0] = dy.astype(F32) + d_x * inv_s[:, 0:1]
    for p in LATER:
        reduce_step(p, 0)
    for p in FIRST + (SMALL,):
        reduce_step(p, 1)
    for p in LATER:
        value = reduce_end(p)
        for p_of, left, cols, there in UP_PIECES:
            if p_of == p:
                asm2[:, 512 + there : 512 + there + cols] = value[:, left : left + cols]
        for p_of, left, cols, there in DOWN_PIECES:
            if p_of == p:
                gdown_ref[:, there : there + cols] = value[:, left : left + cols]
    for p in FIRST + (SMALL,):
        reduce_step(p, 0)
    for p, _, cols, there in FIRST_PIECES:
        asm2[:, there : there + cols] = reduce_end(p)
    gsmall_ref[...] = reduce_end(SMALL)
    squad2[...] = jnp.zeros_like(squad2)
    for t in range(4):
        squad2[t, 0:4, :] = asm2[4 * t : 4 * t + 4, :]
    quad = []
    for peer, delta in quad_peers:
        quad.append(
            send(
                squad2.at[quad_index(delta)], rquad2.at[q], q2s.at[delta - 1], q2r.at[delta - 1],
                peer,
            )
        )
    rquad2[q] = squad2[q]
    settle()
    for copy in quad:
        copy.wait_recv()
    for t in range(3):
        gqkv_ref[:, 512 * t : 512 * (t + 1)] = rquad2[t, 0:4, 0:512]
    gproj_ref[...] = rquad2[3, 0:4, 0:512]
    for t in range(4):
        gup_ref[:, 512 * t : 512 * (t + 1)] = rquad2[t, 0:4, 512:1024]
    for copy in quad:
        copy.wait_send()


def run_block(*args):
    dma = pltpu.SemaphoreType.DMA
    scratch = [VMEM((2, 64) + tile, dtype) for tile, dtype in GATHERED]
    scratch += [VMEM((2, 64) + tile, dtype) for tile, dtype in TILES]
    scratch += [VMEM((128,) + tile, dtype) for tile, dtype in TILES]
    scratch += [VMEM((4, 8, 1024), F32)] * 4 + [VMEM((16, 1024), F32)] * 2
    scratch += [VMEM((512, 2048), BF16), VMEM((512, 2048), BF16), VMEM((2048, 512), BF16)] * 2
    scratch += [VMEM((128, 128), F32)] * 2
    scratch += [VMEM((8, 2, 64, 256), BF16), VMEM((32, 64, 256), BF16), VMEM((32, 64, 256), BF16)]
    scratch += [VMEM((8, 2, 64, 256), BF16)] * 3
    scratch += [VMEM((2048, 64), BF16)] * 2 + [VMEM((2048, 128), BF16), VMEM((2048, 64), BF16)]
    scratch += [VMEM((32, 64, 64), F32)] * 4
    scratch += [VMEM((128, 512), F32)] + [VMEM((128, 128), F32)] * 3 + [VMEM((8, 2048), F32)] * 2
    scratch += [VMEM((128, 512), BF16)] * 2 + [VMEM((128, 2048), BF16)] * 2
    scratch += [VMEM((128, 512), F32)] * 2 + [VMEM((128, 1536), BF16)]
    scratch += [dma((3,))] * 4 + [dma((N, 9))] * 2 + [dma((N,))] * 2 + [dma((N, 10))] * 2
    scratch += [dma((7,)), dma((7,)), dma((8,)), dma((8,))] * 2
    scratch += [VMEM((128, 6144), BF16)] * 4 + [VMEM((64, 2048), BF16)] * 2
    shape = jax.ShapeDtypeStruct
    return pl.pallas_call(
        block_kernel,
        out_shape=(
            shape((1, 128, 512), BF16), shape((1, 128, 512), F32), shape((4, 1536), F32),
            shape((4, 512), F32), shape((4, 2048), F32), shape((16, 512), F32), shape((8, 128), F32),
        ),
        in_specs=[pl.BlockSpec(memory_space=pltpu.SMEM)] + [pl.BlockSpec(memory_space=VMEM)] * 9,
        out_specs=[pl.BlockSpec(memory_space=VMEM)] * 7,
        scratch_shapes=scratch,
        compiler_params=pltpu.CompilerParams(
            collective_id=0, has_side_effects=True, vmem_limit_bytes=LIMIT
        ),
    )(*args)


def finish_kernel(*refs):
    for src, dst in zip(refs[:6], refs[7:13]):
        dst[...] = src[...]
    row = refs[6][0:1, :]
    for (n, off), dst in zip(SECTIONS_OUT, refs[13:]):
        dst[...] = row[:, off : off + n]


def finish(*parts):
    shape = jax.ShapeDtypeStruct
    return pl.pallas_call(
        finish_kernel,
        out_shape=tuple(shape(part.shape, part.dtype) for part in parts[:6])
        + tuple(shape((1, n), F32) for n, _ in SECTIONS_OUT),
        in_specs=[pl.BlockSpec(memory_space=VMEM)] * 7,
        out_specs=[pl.BlockSpec(memory_space=VMEM)] * 14,
    )(*parts)


def per_device(
    hidden_in, positions, block_order, norm1_gain, norm1_bias, norm2_gain, norm2_bias,
    qkv_weight, qkv_bias, attn_out_weight, out_bias, up_weight, up_bias, down_weight, out_grad,
):
    small = jnp.concatenate(
        [norm1_gain, norm1_bias, norm2_gain, norm2_bias, qkv_bias, out_bias, up_bias]
    )
    small = jnp.pad(small[None], ((0, 15), (0, 80)))
    held = block_order.reshape(8, 2, 2).transpose(1, 0, 2).reshape(32)
    ids = jnp.arange(32, dtype=jnp.int32)
    inverse = jnp.sum(jnp.where(held[:, None] == ids[None, :], ids[:, None], 0), axis=0)
    table = jnp.concatenate([held, inverse])
    freqs = 10000.0 ** (-np.arange(8, dtype=np.float32) * np.float32(2.0) / np.float32(16))
    lanes = np.concatenate([freqs, freqs, np.zeros(48)]).astype(np.float32)
    freq = jnp.asarray(np.concatenate([lanes, lanes])[None])
    parts = run_block(
        table, hidden_in, out_grad, positions, freq, small,
        qkv_weight, attn_out_weight, up_weight, down_weight,
    )
    done = finish(*parts)
    block_out, input_grad, g_qkv, g_proj, g_up, g_down = done[:6]
    n1g, n1b, n2g, n2b, qk, val, out, up = (item.reshape(-1) for item in done[6:])
    return (
        block_out, input_grad, n1g, n1b, n2g, n2b, g_qkv, qk, val, g_proj, out, g_up, up, g_down,
    )


def solution(mesh):
    both = ("dp", "ctx")
    rows, vec, mat = P("dp", "ctx", None), P(both), P(both, None)
    return jax.shard_map(
        per_device,
        mesh=mesh,
        in_specs=(
            rows, P("dp", "ctx"), P(), vec, vec, vec, vec, mat, vec, mat, vec, mat, vec, mat, rows,
        ),
        out_specs=(
            rows, rows, vec, vec, vec, vec, mat, vec, vec, mat, vec, mat, vec, mat,
        ),
        check_vma=False,
    )
```
